128 devices in a mesh: col: 16 (over x, z), blk: 8 (over y, core).
Axes of the slice: x: 4, y: 4, z: 4, core: 2. Of those that a mesh axis runs over, the one named last changes fastest.
Arguments:
- col_tiles: bfloat16 [2048, 4, 128, 128], P(('col', 'blk')), may hold values from -0.19921875 to 0.19921875
- scales: float32 [2048, 128], P(('col', 'blk')), may hold values from 0.01 to 100
- positions: int32 [2048, 4], P(('col', 'blk')), may hold values from 0 to 7, as said below
- targets: int32 [2048, 1], P(('col', 'blk')), may hold values from 0 to 7; in each aligned block of 16 rows (0 to 15, 16 to 31, ...) at most 4 rows name the same one
- parents: int32 [16, 8], P('col', 'blk'), may hold values from 0 to 15
Outputs:
- leaf_factor: float32 [128, 512, 512], P(('col', 'blk'))
- leaf_panel: float32 [128, 512, 512], P(('col', 'blk'))
- parent_factor: float32 [128, 512, 512], P(('col', 'blk'))
The draws below stay inside these ranges and needn't reach their ends.
Inputs may be any that keep to these rules, and one draw needn't show every extreme that they name: `positions`: each column tile names 2 distinct tile rows below 4 and then 2 distinct ones at or above it. `targets`: among the rows of one device no value appears more than 4 times.
All inputs are finite; a program needn't handle non-finite values.
Results may differ from the reference program's by a relative error of at most 0.0047.
Values may be sent and summed in bfloat16 or wider, within the bound.
No kernel may reach another device: no remote copies, remote signals or barrier semaphores. Data moves between devices by JAX's collectives and lax.ppermute only.
A program may use at most 128 MiB of HBM per device.

```python
import math
import jax
import jax.numpy as jnp
import numpy as np
from jax import lax

TILE = 128
SUPER = 512
NZT = 4
CT_DEV = 16
CAP = 4
LEAVES = 128
COLT = 2048
N_COL = 16
N_BLK = 8


def draw_positions(key, part):
    key = jax.random.fold_in(key, 11)
    half_rows = SUPER // TILE
    first_key, second_key = jax.random.split(key)
    offsets = jnp.arange(half_rows, dtype=jnp.int32)[None, :]
    first_score = jax.random.randint(first_key, (COLT, half_rows), 0, 1 << 20, dtype=jnp.int32) * half_rows + offsets
    second_score = jax.random.randint(second_key, (COLT, half_rows), 0, 1 << 20, dtype=jnp.int32) * half_rows + offsets
    first_rows = jnp.argsort(first_score, axis=1, stable=True)[:, :2].astype(jnp.int32)
    second_rows = jnp.argsort(second_score, axis=1, stable=True)[:, :2].astype(jnp.int32) + half_rows
    return jnp.concatenate([first_rows, second_rows], axis=1).astype(jnp.int32)


def place_ends(drawn, key, least, largest):
    shape = drawn.shape
    spot = [jax.random.randint(jax.random.fold_in(key, axis), (), 0, shape[axis]) for axis in range(len(shape))]
    drawn = drawn.at[tuple(spot)].set(least)
    longest = shape.index(max(shape))
    spot[longest] = (spot[longest] + 1) % shape[longest]
    return drawn.at[tuple(spot)].set(largest)


def steps_of(rng, extent, shards, smallest, top_value):
    def one(dim, shards_of):
        steps = jax.random.uniform(jax.random.fold_in(jax.random.fold_in(rng, 6), dim), (shards_of,), jnp.float32, smallest / len(shards), top_value / len(shards))
        return jnp.repeat(jnp.exp(steps), extent[dim] // shards_of).reshape((-1,) + (1,) * (len(extent) - dim - 1))

    factor_of = one(*shards[0])
    for cut in shards[1:]:
        factor_of = factor_of * one(*cut)
    return factor_of


def deal_out(rng, own, number, rows, amount, top, bound, skew):
    order = jax.random.permutation(rng, amount)
    heavy_load, usual = shares(amount, rows * top, bound, skew, True), shares(amount, rows * top, bound, skew, False)
    places = jnp.arange(amount)

    def named(tallies, offset_by):
        used = int((tallies > 0).sum())
        fixed = max(1, used // 4)
        moved = fixed + (places - fixed + offset_by * (used - fixed)) % max(1, amount - fixed)
        return jnp.zeros((amount,), jnp.int32).at[order[jnp.where(places < fixed, places, moved)]].set(jnp.asarray(tallies, jnp.int32))

    tallies = jnp.where(number % 4 == 0, named(heavy_load, number // 4), named(usual, number - number // 4 - 1))
    mixed = jax.random.permutation(jax.random.fold_in(own, 3), amount)
    donor, receiver = mixed[0:amount // 2 * 2:2], mixed[1:amount // 2 * 2:2]
    margin = jnp.minimum(tallies[donor] - 1, bound - tallies[receiver]) // 2
    margin = jnp.where((donor == order[0]) | (receiver == order[0]) | (tallies[receiver] == 0), 0, jnp.maximum(margin, 0))
    moved = jax.random.randint(jax.random.fold_in(own, 4), (amount // 2,), 0, 1 << 20) % (margin + 1)
    tallies = tallies.at[donor].add(-moved).at[receiver].add(moved)
    members = jnp.searchsorted(jnp.cumsum(tallies), jnp.arange(rows * top), side="right").astype(jnp.int32)
    table = members.reshape(top, rows).T
    table = table[jax.random.permutation(jax.random.fold_in(own, 1), rows)]
    offset_by = jax.random.randint(jax.random.fold_in(own, 2), (rows, 1), 0, top)
    return jnp.take_along_axis(table, (jnp.arange(top)[None, :] + offset_by) % top, axis=1)


def shares(number_of, total, limit, skew, full):
    weights = [(1 << 20) // math.isqrt(standing ** skew) + 1 for standing in range(1, number_of + 1)]
    largest = limit if full else min(limit, max(-(-total // number_of), total * weights[0] // sum(weights)))
    least = 1 if total - largest >= number_of - 1 else 0
    counts, rest = [largest] + [least] * (number_of - 1), total - largest - least * (number_of - 1)
    while rest > 0:
        free = [i for i in range(1, number_of) if counts[i] < largest] or [i for i in range(1, number_of) if counts[i] < limit]
        whole, left = sum([weights[i] for i in free]), rest
        for i in free:
            addition = min(limit - counts[i], max(1, left * weights[i] // whole), rest)
            counts[i] = counts[i] + addition
            rest = rest - addition
    return np.array(counts)


def normal_values(stream_key, extent, spread, reach, shards=(), kind=jnp.bfloat16):
    gain = steps_of(stream_key, extent, shards, -0.22, 0.18) if shards else 1.0
    drawn = jax.random.normal(stream_key, extent, jnp.float32) * spread * gain
    return jnp.minimum(jnp.maximum(drawn, -reach), reach).astype(kind)


def setup_inputs(seed: int = 0) -> dict:
    splits = jax.random.split(jax.random.key(seed), 6)
    col_tiles = normal_values(splits[0], (COLT, NZT, TILE, TILE), 0.03125, 0.19921875, ((0, 128),))
    scales = jnp.clip(jnp.exp(math.log(100.0) - 9.2103404 * jax.random.uniform(splits[1], (COLT, TILE), jnp.float32) ** steps_of(splits[1], (COLT, TILE), ((0, 128),), -0.2, 0.2)), 0.01, 100.0)
    positions = draw_positions(jax.random.fold_in(splits[5], 71), 0)
    targets_keys = jax.random.split(jax.random.fold_in(splits[3], 1), COLT // CT_DEV)
    targets_turns = jax.random.permutation(jax.random.fold_in(splits[3], 3), COLT // CT_DEV)
    targets = jax.vmap(lambda own, number: deal_out(jax.random.fold_in(splits[3], 2), own, number, CT_DEV, N_BLK, 1, CAP, 2))(targets_keys, targets_turns).reshape((COLT, 1))
    parents = place_ends(jax.random.randint(splits[4], (N_COL, N_BLK), 0, N_COL), jax.random.fold_in(splits[4], 1), 0, N_COL - 1).astype(jnp.int32)
    return dict(col_tiles=col_tiles, scales=scales, positions=positions, targets=targets, parents=parents)


RIDGE = 1.0

def factor_front(front_block):
    identity_mat = jnp.eye(SUPER, dtype=jnp.float32)
    factor = jnp.linalg.cholesky(front_block[:SUPER, :SUPER] + RIDGE * identity_mat)
    leaf_panel = lax.linalg.triangular_solve(factor, front_block[SUPER:, :SUPER], left_side=False, lower=True, transpose_a=True)
    product = jnp.dot(leaf_panel.astype(jnp.float32), leaf_panel.T.astype(jnp.float32), precision=lax.Precision.HIGHEST, preferred_element_type=jnp.float32)
    return (factor, leaf_panel, front_block[SUPER:, SUPER:] - product)

def reference(col_tiles, scales, positions, targets, parents):
    scaled = (col_tiles.astype(jnp.float32) * jnp.sqrt(scales)[:, None, None, :]).astype(jnp.bfloat16)
    per_dev = targets[:, 0].reshape(LEAVES, CT_DEV)
    dest_marks = (per_dev[:, :, None] == jnp.arange(N_BLK, dtype=jnp.int32)[None, None, :]).astype(jnp.int32)
    rank_in_dest = lax.optimization_barrier(jnp.sum((jnp.cumsum(dest_marks, axis=1) - dest_marks) * dest_marks, axis=2))
    device = jnp.arange(LEAVES, dtype=jnp.int32)
    leaf_ids = (device // N_BLK)[:, None] * N_BLK + per_dev
    slot_index = (device % N_BLK)[:, None] * CAP + rank_in_dest
    tile_ids = jnp.arange(COLT, dtype=jnp.int32).reshape(LEAVES, CT_DEV)
    slot_table = jnp.full((LEAVES, N_BLK * CAP), -1, jnp.int32)
    slot_table = slot_table.at[leaf_ids.reshape(-1), slot_index.reshape(-1)].set(tile_ids.reshape(-1))
    spot_ids = jnp.arange(2 * (SUPER // TILE), dtype=jnp.int32)

    def one_leaf(table_row):
        is_used = table_row >= 0
        picked = jnp.maximum(table_row, 0)
        pieces = scaled[picked].astype(jnp.float32)
        placed = positions[picked]
        onehot = ((placed[:, :, None] == spot_ids[None, None, :]) & is_used[:, None, None]).astype(jnp.float32)
        spread_cols = jnp.einsum('kjr,kjac->rakc', onehot, pieces).astype(jnp.bfloat16)
        spread_cols = spread_cols.reshape(2 * SUPER, N_BLK * CAP * TILE)
        front_block = lax.dot_general(spread_cols.astype(jnp.float32), spread_cols.astype(jnp.float32), (((1,), (1,)), ((), ())), preferred_element_type=jnp.float32)
        return factor_front(front_block)
    leaf_factor, leaf_panel, updates = lax.map(one_leaf, slot_table)
    by_owner = updates.reshape(N_COL, N_BLK, SUPER, SUPER)
    identity_mat = jnp.eye(SUPER, dtype=jnp.float32)

    def one_parent(parent_index):
        col_index = parent_index // N_BLK
        blk_index = parent_index % N_BLK
        same_blk = lax.dynamic_index_in_dim(by_owner, blk_index, axis=1, keepdims=False)
        owners = lax.dynamic_index_in_dim(parents, blk_index, axis=1, keepdims=False)
        summed_block = lax.optimization_barrier(jnp.sum(jnp.where((owners == col_index)[:, None, None], same_blk, jnp.zeros((), jnp.float32)), axis=0))
        return jnp.linalg.cholesky(summed_block + RIDGE * identity_mat)
    parent_factor = lax.map(one_parent, jnp.arange(LEAVES, dtype=jnp.int32))
    return (leaf_factor, leaf_panel, parent_factor)
```

```python
import functools

import jax
import jax.numpy as jnp
from jax import lax
from jax.experimental import pallas as pl
from jax.experimental.pallas import tpu as pltpu
from jax.sharding import PartitionSpec as P

TILE = 128
SUPER = 512
RIDGE = 1.0
N_BLK = 8
CAP = 4
CT_DEV = 16
RING = 4
META = 5 * CT_DEV
GROUP = 8
LOWER = [(i, j) for j in range(4) for i in range(j, 4)]

F32 = jnp.float32
BF16 = jnp.bfloat16
NT = (((1,), (1,)), ((), ()))
NN = (((1,), (0,)), ((), ()))

VMEM = pl.BlockSpec(memory_space=pltpu.VMEM)
SMEM = pl.BlockSpec(memory_space=pltpu.SMEM)
PARAMS = pltpu.CompilerParams(vmem_limit_bytes=56 << 20)


def split(a):
    high = a.astype(BF16)
    return high, (a - high.astype(F32)).astype(BF16)


def dot3(a, b, dims=NT):
    def one(x, y):
        return lax.dot_general(x, y, dims, preferred_element_type=F32)

    return one(a[0], b[0]) + (one(a[0], b[1]) + one(a[1], b[0]))


def rows_of(pair, start, stop=None):
    return tuple(part[start:stop] for part in pair)


def place_kernel(target_ref, scale_ref, tile_ref, out_ref, count_ref):
    for group in range(N_BLK):
        count_ref[group] = 0

    def one(t, carry):
        owner = target_ref[t, 0]
        rank = count_ref[owner]
        count_ref[owner] = rank + 1
        root = jnp.sqrt(scale_ref[pl.ds(t, 1), :])
        for k in range(2):
            scaled = tile_ref[t, k].astype(F32) * root
            out_ref[owner, rank, k] = scaled.astype(BF16)
        return carry

    lax.fori_loop(0, CT_DEV, one, 0)


def place(col_tiles, scales, targets, half):
    return pl.pallas_call(
        place_kernel,
        grid=(1,),
        in_specs=[
            SMEM,
            pl.BlockSpec((CT_DEV, TILE), lambda i: (0, 0)),
            pl.BlockSpec((CT_DEV, 2, TILE, TILE), lambda i: (0, half, 0, 0)),
        ],
        out_specs=pl.BlockSpec((N_BLK, CAP, 2, TILE, TILE), lambda i: (0, 0, 0, 0, 0)),
        out_shape=jax.ShapeDtypeStruct((N_BLK, CAP, 2, TILE, TILE), BF16),
        scratch_shapes=[pltpu.SMEM((N_BLK,), jnp.int32)],
        compiler_params=PARAMS,
        name=f"place{half}",
    )(targets, scales, col_tiles)


def list_slots(meta_ref, slot_ref):
    me = lax.axis_index("blk")

    def device(b, total):
        def tile(t, carry):
            total, rank = carry
            mine = meta_ref[b * META + 4 * CT_DEV + t] == me

            @pl.when(mine)
            def _():
                slot_ref[5 * total] = b * CAP + rank
                for k in range(4):
                    slot_ref[5 * total + 1 + k] = meta_ref[b * META + 4 * t + k]

            step = mine.astype(jnp.int32)
            return total + step, rank + step

        return lax.fori_loop(0, CT_DEV, tile, (total, 0))[0]

    return lax.fori_loop(0, N_BLK, device, 0)


def spread(in_ref, slot_ref, s_ref, group, total, half):
    s_ref[...] = jnp.zeros(s_ref.shape, BF16)

    def one(i, carry):
        n = group * GROUP + i
        slot = slot_ref[5 * n]
        at = pl.multiple_of(i * TILE, TILE)
        for k in range(2):
            row = slot_ref[5 * n + 1 + 2 * half + k] - 4 * half
            row = pl.multiple_of(row * TILE, TILE)
            s_ref[pl.ds(row, TILE), pl.ds(at, TILE)] = in_ref[slot // CAP, slot % CAP, k]
        return carry

    lax.fori_loop(0, jnp.minimum(GROUP, total - group * GROUP), one, 0)


def add_gram(m_ref, s_ref):
    for j in range(2):
        o = 256 * j
        got = lax.dot_general(s_ref[o:, :], s_ref[o : o + 256, :], NT, preferred_element_type=F32)
        m_ref[2 * j, o:, :] += got[:, :TILE]
        m_ref[2 * j + 1, o:, :] += got[:, TILE:]


def lane(v, j):
    return jnp.broadcast_to(v[:, j : j + 1], (8, TILE))


def sub(v, i):
    return jnp.broadcast_to(v[i : i + 1, :], (8, TILE))


def eliminate64(aug):
    w = [aug[8 * q : 8 * q + 8] for q in range(8)]
    out = []
    sid = lax.broadcasted_iota(jnp.int32, (8, TILE), 0)
    for p in range(8):
        cols = [[lane(w[q], 8 * p + k) for k in range(8)] for q in range(p, 8)]
        rows = [sub(w[p], k) for k in range(8)]
        own = cols[0]
        for k in range(8):
            r = lax.rsqrt(sub(own[k], k))
            low = own[k] * r
            mult = [None] * 8
            for i in range(k + 1, 8):
                mult[i] = sub(low, i)
            for j in range(k + 1, 8):
                own[j] = own[j] - low * mult[j]
            rows[k] = rows[k] * r
            for i in range(k + 1, 8):
                rows[i] = rows[i] - mult[i] * rows[k]
            for q in range(p + 1, 8):
                col = cols[q - p]
                lq = col[k] * r
                for j in range(k + 1, 8):
                    col[j] = col[j] - lq * mult[j]
                w[q] = w[q] - lq * rows[k]
        block = rows[0]
        for k in range(1, 8):
            block = jnp.where(sid == k, rows[k], block)
        out.append(block)
    return jnp.concatenate(out, axis=0)


def factor(m_ref, l_ref, x_ref=None):
    col_id = lax.broadcasted_iota(jnp.int32, (64, TILE), 1)
    row_id = lax.broadcasted_iota(jnp.int32, (64, TILE), 0)
    eye = (col_id == row_id + 64).astype(F32)
    left = col_id < 64
    lower = row_id[:, :64] >= col_id[:, :64]
    zero = jnp.zeros((64, 64), F32)
    for kb in range(4):
        o = TILE * kb
        if kb:
            l_ref[:o, o : o + TILE] = jnp.zeros((o, TILE), F32)
        w1 = eliminate64(jnp.where(left, m_ref[kb, o : o + 64, :], eye))
        x1 = pltpu.roll(w1, 64, 1)[:, :64]
        x1s = split(x1)
        below = m_ref[kb, o + 64 : o + TILE, :]
        l21 = dot3(split(below[:, :64]), x1s)
        l21s = split(l21)
        rest = pltpu.roll(below, 64, 1)[:, :64] - dot3(l21s, l21s)
        w2 = eliminate64(jnp.where(left, jnp.concatenate([rest, rest], axis=1), eye))
        x2 = pltpu.roll(w2, 64, 1)[:, :64]
        x21 = -dot3(split(x2), split(dot3(l21s, x1s, NN)), NN)
        x = jnp.concatenate(
            [jnp.concatenate([x1, zero], axis=1), jnp.concatenate([x21, x2], axis=1)], axis=0
        )
        if x_ref is not None:
            x_ref[kb] = x
        l1 = jnp.where(lower, w1[:, :64].T, 0.0)
        l2 = jnp.where(lower, w2[:, :64].T, 0.0)
        l_ref[o : o + TILE, o : o + TILE] = jnp.concatenate(
            [jnp.concatenate([l1, zero], axis=1), jnp.concatenate([l21, l2], axis=1)], axis=0
        )
        if kb < 3:
            panel = dot3(split(m_ref[kb, o + TILE :, :]), split(x))
            l_ref[o + TILE :, o : o + TILE] = panel
            panels = split(panel)
            for j in range(kb + 1, 4):
                s = TILE * (j - kb - 1)
                m_ref[j, TILE * j :, :] -= dot3(rows_of(panels, s), rows_of(panels, s, s + TILE))


def add_ridge(m_ref):
    row = lax.broadcasted_iota(jnp.int32, (TILE, TILE), 0)
    col = lax.broadcasted_iota(jnp.int32, (TILE, TILE), 1)
    ridge = jnp.where(row == col, jnp.float32(RIDGE), 0.0)
    for j in range(4):
        m_ref[j, TILE * j : TILE * (j + 1), :] += ridge


def leaf_kernel(meta_ref, in_ref, l_ref, x_ref, m_ref, s_ref, slot_ref):
    total = list_slots(meta_ref, slot_ref)
    m_ref[...] = jnp.zeros(m_ref.shape, F32)

    def step(group, carry):
        spread(in_ref, slot_ref, s_ref, group, total, 0)
        add_gram(m_ref, s_ref)
        return carry

    lax.fori_loop(0, (total + GROUP - 1) // GROUP, step, 0)
    add_ridge(m_ref)
    factor(m_ref, l_ref, x_ref)


def leaf(meta, incoming):
    return pl.pallas_call(
        leaf_kernel,
        in_specs=[SMEM, VMEM],
        out_specs=[VMEM, VMEM],
        out_shape=[
            jax.ShapeDtypeStruct((SUPER, SUPER), F32),
            jax.ShapeDtypeStruct((4, TILE, TILE), F32),
        ],
        scratch_shapes=[
            pltpu.VMEM((4, SUPER, TILE), F32),
            pltpu.VMEM((SUPER, GROUP * TILE), BF16),
            pltpu.SMEM((5 * N_BLK * CAP,), jnp.int32),
        ],
        compiler_params=PARAMS,
        name="leaf",
    )(meta, incoming)


def panel_kernel(
    meta_ref, in1_ref, in2_ref, l_ref, x_ref, p_ref, u_ref, f_ref, m_ref, s1_ref, s2_ref, slot_ref
):
    total = list_slots(meta_ref, slot_ref)
    m_ref[...] = jnp.zeros(m_ref.shape, F32)
    f_ref[...] = jnp.zeros(f_ref.shape, F32)

    def step(group, carry):
        spread(in1_ref, slot_ref, s1_ref, group, total, 0)
        spread(in2_ref, slot_ref, s2_ref, group, total, 1)
        f_ref[...] += lax.dot_general(s2_ref[...], s1_ref[...], NT, preferred_element_type=F32)
        add_gram(m_ref, s2_ref)
        return carry

    lax.fori_loop(0, (total + GROUP - 1) // GROUP, step, 0)
    pairs = []
    for kb in range(4):
        o = TILE * kb
        rest = f_ref[:, o : o + TILE]
        for j in range(kb):
            rest = rest - dot3(pairs[j], split(l_ref[o : o + TILE, TILE * j : TILE * (j + 1)]))
        panel = dot3(split(rest), split(x_ref[kb]))
        p_ref[:, o : o + TILE] = panel
        pairs.append(split(panel))
    whole = tuple(jnp.concatenate([pair[i] for pair in pairs], axis=1) for i in range(2))
    n = 0
    for j in range(4):
        o = TILE * j
        update = m_ref[j, o:, :] - dot3(rows_of(whole, o), rows_of(whole, o, o + TILE))
        for i in range(4 - j):
            u_ref[n] = update[TILE * i : TILE * (i + 1)].astype(BF16)
            n += 1


def panel(meta, first, second, leaf_factor, inverses):
    return pl.pallas_call(
        panel_kernel,
        in_specs=[SMEM, VMEM, VMEM, VMEM, VMEM],
        out_specs=[VMEM, VMEM],
        out_shape=[
            jax.ShapeDtypeStruct((SUPER, SUPER), F32),
            jax.ShapeDtypeStruct((len(LOWER), TILE, TILE), BF16),
        ],
        scratch_shapes=[
            pltpu.VMEM((SUPER, SUPER), F32),
            pltpu.VMEM((4, SUPER, TILE), F32),
            pltpu.VMEM((SUPER, GROUP * TILE), BF16),
            pltpu.VMEM((SUPER, GROUP * TILE), BF16),
            pltpu.SMEM((5 * N_BLK * CAP,), jnp.int32),
        ],
        compiler_params=PARAMS,
        name="panel",
    )(meta, first, second, leaf_factor, inverses)


def sort_kernel(parent_ref, a0, a1, a2, a3, keep_ref, b1, b2, b3):
    c = lax.axis_index("col")
    x, z = c // RING, c % RING
    came = (a0, a1, a2, a3)
    owners = [parent_ref[lax.rem(x + RING - s, RING) * RING + z] for s in range(RING)]
    for step, out in enumerate((keep_ref, b1, b2, b3)):
        parent = x * RING + lax.rem(z + step, RING)
        takes = [owner == parent for owner in owners]
        for n in range(len(LOWER)):
            total = jnp.zeros((TILE, TILE), F32)
            for take, ref in zip(takes, came):
                total = total + jnp.where(take, ref[n].astype(F32), 0.0)
            out[n] = total.astype(out.dtype)


def sort(parents, came):
    shape = (len(LOWER), TILE, TILE)
    return pl.pallas_call(
        sort_kernel,
        in_specs=[SMEM] + [VMEM] * 4,
        out_specs=[VMEM] * 4,
        out_shape=[jax.ShapeDtypeStruct(shape, t) for t in (F32, BF16, BF16, BF16)],
        compiler_params=PARAMS,
        name="sort",
    )(parents, *came)


def parent_kernel(keep_ref, b1, b2, b3, l_ref, m_ref):
    for n, (i, j) in enumerate(LOWER):
        got = b1[n].astype(F32) + b2[n].astype(F32) + b3[n].astype(F32)
        m_ref[j, TILE * i : TILE * (i + 1), :] = keep_ref[n] + got
    add_ridge(m_ref)
    factor(m_ref, l_ref)


def parent(parts):
    return pl.pallas_call(
        parent_kernel,
        in_specs=[VMEM] * 4,
        out_specs=VMEM,
        out_shape=jax.ShapeDtypeStruct((SUPER, SUPER), F32),
        scratch_shapes=[pltpu.VMEM((4, SUPER, TILE), F32)],
        compiler_params=PARAMS,
        name="parent",
    )(*parts)


def shift(value, along_x, step):
    pairs = []
    for x in range(RING):
        for z in range(RING):
            to = ((x + step) % RING, z) if along_x else (x, (z + step) % RING)
            pairs.append((x * RING + z, to[0] * RING + to[1]))
    return lax.ppermute(value, "col", pairs)


def on_device(col_tiles, scales, positions, targets, parents):
    meta = jnp.concatenate([positions.reshape(-1), targets.reshape(-1)])
    meta = lax.all_gather(meta, "blk", tiled=True)
    owners = lax.all_gather(parents.reshape(-1), "col", tiled=True)

    def exchange(value):
        return lax.all_to_all(value, "blk", split_axis=0, concat_axis=0, tiled=True)

    out1 = place(col_tiles, scales, targets, 0)
    in1 = exchange(out1)
    out2 = place(col_tiles, scales, targets, 1)
    in1, out2 = lax.optimization_barrier((in1, out2))
    in2 = exchange(out2)
    leaf_factor, inverses = leaf(meta, in1)
    leaf_panel, update = panel(meta, in1, in2, leaf_factor, inverses)
    came = [update] + [shift(update, True, s) for s in (1, 2, 3)]
    keep, *sends = sort(owners, came)
    parts = [keep] + [shift(value, False, s + 1) for s, value in enumerate(sends)]
    parent_factor = parent(parts)
    return (leaf_factor[None], leaf_panel[None], parent_factor[None])


def solution(mesh):
    in_specs = (
        P(("col", "blk"), None, None, None),
        P(("col", "blk"), None),
        P(("col", "blk"), None),
        P(("col", "blk"), None),
        P("col", "blk"),
    )
    out_specs = (
        P(("col", "blk"), None, None),
        P(("col", "blk"), None, None),
        P(("col", "blk"), None, None),
    )
    return jax.shard_map(
        on_device, mesh=mesh, in_specs=in_specs, out_specs=out_specs, check_vma=False
    )
```

```python
import jax
import jax.numpy as jnp
from jax import lax
from jax.experimental import pallas as pl
from jax.experimental.pallas import tpu as pltpu
from jax.sharding import PartitionSpec as P

TILE = 128
SUPER = 512
RIDGE = 1.0
CAP = 4
CT_DEV = 16
RING = 4
PEERS = [(dy, dc) for dy in range(RING) for dc in range(2)]
TILES = CAP * 2 * TILE
BLOCK = TILES + 16
WIDTH = len(PEERS) * CAP * TILE
LOWER = [(i, j) for j in range(4) for i in range(j, 4)]
FIRST = LOWER[:4]
SECOND = LOWER[4:]

F32 = jnp.float32
BF16 = jnp.bfloat16
NT = (((1,), (1,)), ((), ()))
NN = (((1,), (0,)), ((), ()))

VMEM = pl.BlockSpec(memory_space=pltpu.VMEM)
SMEM = pl.BlockSpec(memory_space=pltpu.SMEM)
PARAMS = pltpu.CompilerParams(vmem_limit_bytes=56 << 20)


def shape_of(rows, dtype, columns=TILE):
    return jax.ShapeDtypeStruct((rows, columns), dtype)


def split(a):
    high = a.astype(BF16)
    return high, (a - high.astype(F32)).astype(BF16)


def dot3(a, b, dims=NT):
    def one(x, y):
        return lax.dot_general(x, y, dims, preferred_element_type=F32)
    return one(a[0], b[0]) + (one(a[0], b[1]) + one(a[1], b[0]))


def rows_of(pair, start, stop=None):
    return tuple(part[start:stop] for part in pair)


def on_top(pair):
    return tuple(jnp.concatenate([part, jnp.zeros_like(part)], axis=0) for part in pair)


def below(pair):
    return tuple(jnp.concatenate([jnp.zeros_like(part), part], axis=0) for part in pair)


def lane(v, j):
    return jnp.broadcast_to(v[:, j : j + 1], (8, TILE))


def sub(v, i):
    return jnp.broadcast_to(v[i : i + 1, :], (8, TILE))


def eliminate64(aug, base):
    w = [aug[8 * q : 8 * q + 8] for q in range(8)]
    out = []
    sid = lax.broadcasted_iota(jnp.int32, (8, TILE), 0)
    own = [lane(w[0], base + k) for k in range(8)]
    for p in range(8):
        at = base + 8 * p
        cols = [[lane(w[q], at + k) for k in range(8)] for q in range(p + 1, 8)]
        last = p == 7
        if not last:
            ahead = [lane(w[p + 1], at + 8 + k) for k in range(8)]
        rows = [sub(w[p], k) for k in range(8)]
        scale = None
        for k in range(8):
            if k % 2 == 0:
                a, b, c = sub(own[k], k), sub(own[k], k + 1), sub(own[k + 1], k + 1)
                r = lax.rsqrt(a)
                scale = lax.rsqrt(a * c - b * b) * (a * r)
            else:
                r = scale
            low = own[k] * r
            mult = [sub(low, i) if i > k else None for i in range(8)]
            for j in range(k + 1, 8):
                own[j] = own[j] - low * mult[j]
            rows[k] = rows[k] * r
            for i in range(k + 1, 8):
                rows[i] = rows[i] - mult[i] * rows[k]
            for q in range(p + 1, 8):
                col = cols[q - p - 1]
                lq = col[k] * r
                for j in range(k + 1, 8):
                    col[j] = col[j] - lq * mult[j]
                w[q] = w[q] - lq * rows[k]
                if q == p + 1:
                    for j in range(8):
                        ahead[j] = ahead[j] - lq * sub(lq, j)
        block = rows[0]
        for k in range(1, 8):
            block = jnp.where(sid == k, rows[k], block)
        out.append(block)
        if not last:
            own = ahead
    return jnp.concatenate(out, axis=0)


def factor(m_ref, l_ref, x_ref=None):
    col_id = lax.broadcasted_iota(jnp.int32, (64, TILE), 1)
    row_id = lax.broadcasted_iota(jnp.int32, (64, TILE), 0)
    eye = (col_id % 64 == row_id).astype(F32)
    left = col_id < 64
    lower = row_id >= col_id % 64
    zero = jnp.zeros((), F32)

    def keep_left(v):
        return jnp.where(lax.broadcasted_iota(jnp.int32, v.shape, 1) < 64, v, zero)

    def keep_right(v):
        return jnp.where(lax.broadcasted_iota(jnp.int32, v.shape, 1) < 64, zero, v)

    corner = pltpu.roll(m_ref[0, :64, :], 64, 1)
    for kb in range(4):
        o = TILE * kb
        if kb:
            l_ref[:o, o : o + TILE] = jnp.zeros((o, TILE), F32)
        corner_b = pltpu.roll(m_ref[kb, o + 64 : o + TILE, :], 64, 1)
        lhs = split(keep_left(m_ref[kb, o + 64 :, :]))
        w1 = eliminate64(jnp.where(left, eye, corner), 64)
        x1 = on_top(split(w1))
        l21 = dot3(rows_of(lhs, 0, 64), x1)
        l21s = split(l21)
        w2 = eliminate64(jnp.where(left, corner_b - dot3(l21s, on_top(l21s)), eye), 0)
        if kb < 3:
            pa = dot3(rows_of(lhs, 64), x1)
            pas = split(pa)
            rest = split(keep_right(m_ref[kb, o + TILE :, :] - dot3(pas, below(l21s))))
            x2 = below(split(w2))
            n = o + TILE
            pa_d = rows_of(pas, 0, 64)
            corner = pltpu.roll(m_ref[kb + 1, n : n + 64, :], 64, 1) - dot3(pa_d, below(pa_d))
            pb_d = dot3(rows_of(rest, 0, 64), x2)
            pb_ds = split(pb_d)
            corner = corner - dot3(pb_ds, below(pb_ds))
            pb = jnp.concatenate([pb_d, dot3(rows_of(rest, 64), x2)], axis=0)
            panel = pa + pb
            l_ref[n:, o:n] = panel
            panels = split(panel)
            for j in range(kb + 1, 4):
                s = TILE * (j - kb - 1)
                m_ref[j, TILE * j :, :] -= dot3(rows_of(panels, s), rows_of(panels, s, s + TILE))
        flip = jnp.concatenate([w1, w2], axis=0).T
        l_ref[o : o + 64, o : o + TILE] = jnp.where(left & lower, flip[64:], zero)
        l_ref[o + 64 : o + TILE, o : o + TILE] = jnp.where(left, l21, jnp.where(lower, flip[:64], zero))
        if x_ref is not None:
            x1f = jnp.where(left, w1, zero)
            x2f = jnp.where(left, zero, w2)
            t = dot3(l21s, on_top(split(x1f)), NN)
            x21 = -dot3(split(x2f), below(split(t)), NN)
            x = jnp.concatenate([x1f, jnp.where(left, x21, x2f)], axis=0)
            x_ref[o : o + TILE, o : o + TILE] = x
            if kb < 3:
                x_ref[o : o + TILE, o + TILE :] = jnp.zeros((TILE, SUPER - TILE - o), F32)
            if kb:
                before = dot3(split(l_ref[o : o + TILE, :o]), split(x_ref[:o, :o]), NN)
                x_ref[o : o + TILE, :o] = -dot3(split(x), split(before), NN)


def place_kernel(target_ref, spot_ref, scale_ref, tile_ref, *refs):
    outs, (block_ref, spots_ref, count_ref) = refs[:-3], refs[-3:]
    me = lax.axis_index("blk")
    for peer in range(len(PEERS)):
        count_ref[peer] = 0
    block_ref[...] = jnp.zeros(block_ref.shape, BF16)
    spots_ref[...] = jnp.zeros(spots_ref.shape, F32)

    def one(t, carry):
        owner = target_ref[t, 0]
        peer = lax.rem(owner // 2 - me // 2 + RING, RING) * 2 + lax.rem(owner + me, 2)
        rank = count_ref[peer]
        count_ref[peer] = rank + 1
        root = jnp.sqrt(scale_ref[pl.ds(t, 1), :])
        for k in range(2):
            scaled = tile_ref[t, k].astype(F32) * root
            block_ref[peer, 2 * rank + k] = scaled.astype(BF16)
        for k in range(4):
            spot = jnp.full((1, TILE), spot_ref[t, k].astype(F32))
            spots_ref[peer, pl.ds(4 * rank + k, 1), :] = spot
        return carry

    lax.fori_loop(0, CT_DEV, one, 0)
    at = 0
    for out in outs:
        for b in range(out.shape[0] // BLOCK):
            o = BLOCK * b
            for i in range(2 * CAP):
                out[o + TILE * i : o + TILE * (i + 1), :] = block_ref[ORDER[len(outs)][at], i]
            out[o + TILES : o + BLOCK, :] = spots_ref[ORDER[len(outs)][at]].astype(BF16)
            at += 1


ORDER = {8: list(range(8)), 5: [0, 2, 4, 6, 1, 3, 5, 7]}


def place(col_tiles, scales, positions, targets, half):
    blocks = [1] * 8 if half == 0 else [1, 1, 1, 1, 4]
    return pl.pallas_call(
        place_kernel,
        grid=(1,),
        in_specs=[
            SMEM,
            SMEM,
            pl.BlockSpec((CT_DEV, TILE), lambda i: (0, 0)),
            pl.BlockSpec((CT_DEV, 2, TILE, TILE), lambda i: (0, half, 0, 0)),
        ],
        out_specs=[pl.BlockSpec((n * BLOCK, TILE), lambda i: (0, 0)) for n in blocks],
        out_shape=[shape_of(n * BLOCK, BF16) for n in blocks],
        scratch_shapes=[
            pltpu.VMEM((len(PEERS), 2 * CAP, TILE, TILE), BF16),
            pltpu.VMEM((len(PEERS), 16, TILE), F32),
            pltpu.SMEM((len(PEERS),), jnp.int32),
        ],
        compiler_params=PARAMS,
        name=f"place{half}",
    )(targets, positions, scales, col_tiles)


def spread(blocks, s_ref, half):
    for n, (ref, o) in enumerate(blocks):
        spots = ref[o + TILES : o + BLOCK, :].astype(F32)
        for slot in range(CAP):
            at = TILE * (n * CAP + slot)
            tiles = []
            for k in range(2):
                s = o + TILE * (2 * slot + k)
                tiles.append(ref[s : s + TILE, :].reshape(8, 16, TILE))
            row = 4 * slot + 2 * half
            picks = [jnp.broadcast_to(spots[row + k : row + k + 1, :], (16, TILE)) for k in range(2)]
            for i in range(4):
                total = None
                for tile, pick in zip(tiles, picks):
                    flag = jnp.where(pick == 4.0 * half + i, 1.0, 0.0).astype(BF16)
                    part = tile * flag[None]
                    total = part if total is None else total + part
                s_ref[TILE * i : TILE * (i + 1), at : at + TILE] = total.reshape(TILE, TILE)


def gram(s_ref, j):
    o = 256 * j
    return lax.dot_general(s_ref[o:, :], s_ref[o : o + 256, :], NT, preferred_element_type=F32)


def add_ridge(m_ref):
    row = lax.broadcasted_iota(jnp.int32, (TILE, TILE), 0)
    col = lax.broadcasted_iota(jnp.int32, (TILE, TILE), 1)
    ridge = jnp.where(row == col, jnp.float32(RIDGE), 0.0)
    for j in range(4):
        m_ref[j, TILE * j : TILE * (j + 1), :] += ridge


def leaf_kernel(*refs):
    blocks, (l_ref, x_ref, m_ref, s_ref) = refs[:-4], refs[-4:]
    spread([(ref, 0) for ref in blocks], s_ref, 0)
    for j in range(2):
        got = gram(s_ref, j)
        m_ref[2 * j, 256 * j :, :] = got[:, :TILE]
        m_ref[2 * j + 1, 256 * j :, :] = got[:, TILE:]
    add_ridge(m_ref)
    factor(m_ref, l_ref, x_ref)


def leaf(blocks):
    return pl.pallas_call(
        leaf_kernel,
        in_specs=[VMEM] * len(blocks),
        out_specs=[VMEM, VMEM],
        out_shape=[shape_of(SUPER, F32, SUPER)] * 2,
        scratch_shapes=[
            pltpu.VMEM((4, SUPER, TILE), F32),
            pltpu.VMEM((SUPER, WIDTH), BF16),
        ],
        compiler_params=PARAMS,
        cost_estimate=pl.CostEstimate(flops=20 * 10**9, bytes_accessed=5 << 20, transcendentals=0),
        name="leaf",
    )(*blocks)


def panel_kernel(parent_ref, *refs):
    first, second = refs[:8], refs[8:13]
    x_ref, p_ref, a_ref, b_ref, s1_ref, s2_ref = refs[13:]
    spread([(ref, 0) for ref in first], s1_ref, 0)
    own, mate, *pairs = second
    later = [(own, 0), (mate, 0)] + [(ref, o) for ref in pairs for o in (0, BLOCK)]
    spread(later, s2_ref, 1)
    front = split(lax.dot_general(s2_ref[...], s1_ref[...], NT, preferred_element_type=F32))
    left = tuple(part[:, :256] for part in front)
    panels = [dot3(left, split(x_ref[:256, :256])), dot3(front, split(x_ref[256:, :]))]
    panel = jnp.concatenate(panels, axis=1)
    p_ref[...] = panel
    whole = split(panel)
    for j in range(2):
        o = 256 * j
        update = gram(s2_ref, j) - dot3(rows_of(whole, o), rows_of(whole, o, o + 256))
        for n, (row, col) in enumerate(LOWER):
            if col // 2 == j:
                out, at = (a_ref, n) if n < len(FIRST) else (b_ref, n - len(FIRST))
                r, c = TILE * row - o, TILE * col - o
                part = update[r : r + TILE, c : c + TILE]
                out[TILE * at : TILE * (at + 1), :] = part.astype(BF16)
    parent = jnp.full((16, TILE), parent_ref[0, 0].astype(F32)).astype(BF16)
    for out in (a_ref, b_ref):
        out[out.shape[0] - 16 :, :] = parent


def panel(parents, first, second, inverse):
    return pl.pallas_call(
        panel_kernel,
        in_specs=[SMEM] + [VMEM] * 14,
        out_specs=[VMEM] * 3,
        out_shape=[
            shape_of(SUPER, F32, SUPER),
            shape_of(TILE * len(FIRST) + 16, BF16),
            shape_of(TILE * len(SECOND) + 16, BF16),
        ],
        scratch_shapes=[pltpu.VMEM((SUPER, WIDTH), BF16)] * 2,
        compiler_params=PARAMS,
        name="panel",
    )(parents, *first, *second, inverse)


def sort_kernel(x_first, a0, a1, a2, a3, keep_ref, b1, b2, b3):
    c = lax.axis_index("col")
    x, z = c // RING, lax.rem(c, RING)
    rows = keep_ref.shape[0]
    came = (a0, a1, a2, a3)
    parents = [ref[rows:, :].astype(F32)[:8] for ref in came]
    for step, out in enumerate((keep_ref, b1, b2, b3)):
        if x_first:
            wanted = x * RING + lax.rem(z + step, RING)
        else:
            wanted = lax.rem(x + step, RING) * RING + z
        wanted = wanted.astype(F32)
        flags = [jnp.where(parent == wanted, 1.0, 0.0)[None] for parent in parents]
        for r in range(0, rows, TILE):
            total = None
            for flag, ref in zip(flags, came):
                part = ref[r : r + TILE, :].astype(F32).reshape(16, 8, TILE) * flag
                total = part if total is None else total + part
            out[r : r + TILE, :] = total.reshape(TILE, TILE).astype(out.dtype)


def sort(x_first, came):
    rows = came[0].shape[0] - 16

    def kernel(*refs):
        sort_kernel(x_first, *refs)

    return pl.pallas_call(
        kernel,
        in_specs=[VMEM] * 4,
        out_specs=[VMEM] * 4,
        out_shape=[shape_of(rows, t) for t in (F32, BF16, BF16, BF16)],
        compiler_params=PARAMS,
        name="sort_x" if x_first else "sort_z",
    )(*came)


def parent_kernel(*refs):
    first, second, (l_ref, m_ref) = refs[:4], refs[4:8], refs[8:]
    for n, (i, j) in enumerate(LOWER):
        parts, at = (first, n) if n < len(FIRST) else (second, n - len(FIRST))
        total = None
        for ref in parts:
            part = ref[TILE * at : TILE * (at + 1), :].astype(F32)
            total = part if total is None else total + part
        m_ref[j, TILE * i : TILE * (i + 1), :] = total
    add_ridge(m_ref)
    factor(m_ref, l_ref)


def parent(parts):
    return pl.pallas_call(
        parent_kernel,
        in_specs=[VMEM] * len(parts),
        out_specs=VMEM,
        out_shape=shape_of(SUPER, F32, SUPER),
        scratch_shapes=[pltpu.VMEM((4, SUPER, TILE), F32)],
        compiler_params=PARAMS,
        name="parent",
    )(*parts)


def shift(value, along_x, step):
    pairs = []
    for x in range(RING):
        for z in range(RING):
            to = ((x + step) % RING, z) if along_x else (x, (z + step) % RING)
            pairs.append((x * RING + z, to[0] * RING + to[1]))
    return lax.ppermute(value, "col", pairs)


def hand(value, dy, dc):
    pairs = [(y * 2 + c, (y + dy) % RING * 2 + (c ^ dc)) for y in range(RING) for c in range(2)]
    return lax.ppermute(value, "blk", pairs)


def on_device(col_tiles, scales, positions, targets, parents):
    out1 = place(col_tiles, scales, positions, targets, 0)
    in1 = list(out1)
    for dy, dc in ((1, 0), (3, 0), (2, 0), (1, 1), (3, 1), (2, 1), (0, 1)):
        in1[2 * dy + dc] = hand(out1[2 * dy + dc], dy, dc)
    *keep, give = place(col_tiles, scales, positions, targets, 1)
    got = hand(give, 0, 1)
    pairs = [
        jnp.concatenate([keep[dy], got[BLOCK * dy : BLOCK * (dy + 1)]]) for dy in range(1, RING)
    ]
    in1, pairs = lax.optimization_barrier((in1, pairs))
    in2 = [keep[0], got[:BLOCK]] + [hand(pairs[dy - 1], dy, 0) for dy in (1, 2, 3)]
    leaf_factor, inverse = leaf(in1)
    leaf_panel, first, second = panel(parents, in1, in2, inverse)
    parts = []
    for x_first, value in ((True, first), (False, second)):
        came = [value] + [shift(value, x_first, s) for s in (1, 2, 3)]
        own, *sends = sort(x_first, came)
        parts += [own] + [shift(send, not x_first, s + 1) for s, send in enumerate(sends)]
    parent_factor = parent(parts)
    return (leaf_factor[None], leaf_panel[None], parent_factor[None])


def solution(mesh):
    in_specs = (
        P(("col", "blk"), None, None, None),
        P(("col", "blk"), None),
        P(("col", "blk"), None),
        P(("col", "blk"), None),
        P("col", "blk"),
    )
    out_specs = (
        P(("col", "blk"), None, None),
        P(("col", "blk"), None, None),
        P(("col", "blk"), None, None),
    )
    return jax.shard_map(
        on_device, mesh=mesh, in_specs=in_specs, out_specs=out_specs, check_vma=False
    )
```

```python
import jax
import jax.numpy as jnp
from jax import lax
from jax.experimental import pallas as pl
from jax.experimental.pallas import tpu as pltpu
from jax.sharding import PartitionSpec as P

TILE = 128
SUPER = 512
RIDGE = 1.0
CAP = 4
CT_DEV = 16
RING = 4
PEERS = [(dy, dc) for dy in range(RING) for dc in range(2)]
TILES = CAP * 2 * TILE
BLOCK = TILES + 16
WIDTH = len(PEERS) * CAP * TILE
LOWER = [(i, j) for j in range(4) for i in range(j, 4)]
FIRST = LOWER[:4]
SECOND = LOWER[4:]

F32 = jnp.float32
BF16 = jnp.bfloat16
NT = (((1,), (1,)), ((), ()))
NN = (((1,), (0,)), ((), ()))

VMEM = pl.BlockSpec(memory_space=pltpu.VMEM)
SMEM = pl.BlockSpec(memory_space=pltpu.SMEM)
PARAMS = pltpu.CompilerParams(vmem_limit_bytes=56 << 20)


def shape_of(rows, dtype, columns=TILE):
    return jax.ShapeDtypeStruct((rows, columns), dtype)


def split(a):
    high = a.astype(BF16)
    return high, (a - high.astype(F32)).astype(BF16)


def dot3(a, b, dims=NT):
    def one(x, y):
        return lax.dot_general(x, y, dims, preferred_element_type=F32)
    return one(a[0], b[0]) + (one(a[0], b[1]) + one(a[1], b[0]))


def rows_of(pair, start, stop=None):
    return tuple(part[start:stop] for part in pair)


def on_top(pair):
    return tuple(jnp.concatenate([part, jnp.zeros_like(part)], axis=0) for part in pair)


def below(pair):
    return tuple(jnp.concatenate([jnp.zeros_like(part), part], axis=0) for part in pair)


def lane(v, j):
    return jnp.broadcast_to(v[:, j : j + 1], (8, TILE))


def sub(v, i):
    return jnp.broadcast_to(v[i : i + 1, :], (8, TILE))


def eliminate64(aug, base):
    w = [aug[8 * q : 8 * q + 8] for q in range(8)]
    out = []
    sid = lax.broadcasted_iota(jnp.int32, (8, TILE), 0)
    own = [lane(w[0], base + k) for k in range(8)]
    for p in range(8):
        at = base + 8 * p
        cols = [[lane(w[q], at + k) for k in range(8)] for q in range(p + 1, 8)]
        last = p == 7
        if not last:
            ahead = [lane(w[p + 1], at + 8 + k) for k in range(8)]
        rows = [sub(w[p], k) for k in range(8)]
        scale = None
        for k in range(8):
            if k % 2 == 0:
                a, b, c = sub(own[k], k), sub(own[k], k + 1), sub(own[k + 1], k + 1)
                r = lax.rsqrt(a)
                scale = lax.rsqrt(a * c - b * b) * (a * r)
            else:
                r = scale
            low = own[k] * r
            mult = [sub(low, i) if i > k else None for i in range(8)]
            for j in range(k + 1, 8):
                own[j] = own[j] - low * mult[j]
            rows[k] = rows[k] * r
            for i in range(k + 1, 8):
                rows[i] = rows[i] - mult[i] * rows[k]
            for q in range(p + 1, 8):
                col = cols[q - p - 1]
                lq = col[k] * r
                for j in range(k + 1, 8):
                    col[j] = col[j] - lq * mult[j]
                w[q] = w[q] - lq * rows[k]
                if q == p + 1:
                    for j in range(8):
                        ahead[j] = ahead[j] - lq * sub(lq, j)
        block = rows[0]
        for k in range(1, 8):
            block = jnp.where(sid == k, rows[k], block)
        out.append(block)
        if not last:
            own = ahead
    return jnp.concatenate(out, axis=0)


def trail(m_ref, kb, panels):
    for j in range(kb + 1, 4):
        s = TILE * (j - kb - 1)
        m_ref[j, TILE * j :, :] -= dot3(rows_of(panels, s), rows_of(panels, s, s + TILE))


def factor(m_ref, l_ref, x_ref=None, steps=range(4)):
    col_id = lax.broadcasted_iota(jnp.int32, (64, TILE), 1)
    row_id = lax.broadcasted_iota(jnp.int32, (64, TILE), 0)
    eye = (col_id % 64 == row_id).astype(F32)
    left = col_id < 64
    lower = row_id >= col_id % 64
    zero = jnp.zeros((), F32)

    def keep_left(v):
        return jnp.where(lax.broadcasted_iota(jnp.int32, v.shape, 1) < 64, v, zero)

    def keep_right(v):
        return jnp.where(lax.broadcasted_iota(jnp.int32, v.shape, 1) < 64, zero, v)

    o = TILE * steps[0]
    corner = pltpu.roll(m_ref[steps[0], o : o + 64, :], 64, 1)
    for kb in steps:
        o = TILE * kb
        if kb:
            l_ref[:o, o : o + TILE] = jnp.zeros((o, TILE), F32)
        corner_b = pltpu.roll(m_ref[kb, o + 64 : o + TILE, :], 64, 1)
        lhs = split(keep_left(m_ref[kb, o + 64 :, :]))
        w1 = eliminate64(jnp.where(left, eye, corner), 64)
        x1 = on_top(split(w1))
        l21 = dot3(rows_of(lhs, 0, 64), x1)
        l21s = split(l21)
        w2 = eliminate64(jnp.where(left, corner_b - dot3(l21s, on_top(l21s)), eye), 0)
        if kb < 3:
            pa = dot3(rows_of(lhs, 64), x1)
            pas = split(pa)
            rest = split(keep_right(m_ref[kb, o + TILE :, :] - dot3(pas, below(l21s))))
            x2 = below(split(w2))
            n = o + TILE
            last = kb == steps[-1]
            pb_d = dot3(rows_of(rest, 0, 64), x2)
            if not last:
                pa_d, pb_ds = rows_of(pas, 0, 64), split(pb_d)
                corner = pltpu.roll(m_ref[kb + 1, n : n + 64, :], 64, 1) - dot3(pa_d, below(pa_d))
                corner = corner - dot3(pb_ds, below(pb_ds))
            pb = jnp.concatenate([pb_d, dot3(rows_of(rest, 64), x2)], axis=0)
            panel = pa + pb
            l_ref[n:, o:n] = panel
            if not last:
                trail(m_ref, kb, split(panel))
        flip = jnp.concatenate([w1, w2], axis=0).T
        l_ref[o : o + 64, o : o + TILE] = jnp.where(left & lower, flip[64:], zero)
        l_ref[o + 64 : o + TILE, o : o + TILE] = jnp.where(left, l21, jnp.where(lower, flip[:64], zero))
        if x_ref is not None:
            x1f = jnp.where(left, w1, zero)
            x2f = jnp.where(left, zero, w2)
            t = dot3(l21s, on_top(split(x1f)), NN)
            x21 = -dot3(split(x2f), below(split(t)), NN)
            x = jnp.concatenate([x1f, jnp.where(left, x21, x2f)], axis=0)
            x_ref[o : o + TILE, o : o + TILE] = x
            if kb < 3:
                x_ref[o : o + TILE, o + TILE :] = jnp.zeros((TILE, SUPER - TILE - o), F32)
            if kb:
                before = dot3(split(l_ref[o : o + TILE, :o]), split(x_ref[:o, :o]), NN)
                x_ref[o : o + TILE, :o] = -dot3(split(x), split(before), NN)


def place_kernel(target_ref, spot_ref, scale_ref, tile_ref, after_ref, *refs):
    del after_ref
    outs, (block_ref, spots_ref, count_ref) = refs[:-3], refs[-3:]
    me = lax.axis_index("blk")
    for peer in range(len(PEERS)):
        count_ref[peer] = 0
    block_ref[...] = jnp.zeros(block_ref.shape, BF16)
    spots_ref[...] = jnp.zeros(spots_ref.shape, F32)

    for t in range(CT_DEV):
        owner = target_ref[t, 0]
        peer = lax.rem(owner // 2 - me // 2 + RING, RING) * 2 + lax.rem(owner + me, 2)
        rank = count_ref[peer]
        count_ref[peer] = rank + 1
        root = jnp.sqrt(scale_ref[t : t + 1, :])
        for k in range(2):
            scaled = tile_ref[t, k].astype(F32) * root
            block_ref[peer, 2 * rank + k] = scaled.astype(BF16)
        spots = spot_ref[t : t + 1, :].astype(F32)
        for k in range(4):
            spot = jnp.broadcast_to(spots[:, k : k + 1], (1, TILE))
            spots_ref[peer, pl.ds(4 * rank + k, 1), :] = spot
    at = 0
    for out in outs:
        for b in range(out.shape[0] // BLOCK):
            o = BLOCK * b
            for i in range(2 * CAP):
                out[o + TILE * i : o + TILE * (i + 1), :] = block_ref[ORDER[len(outs)][at], i]
            out[o + TILES : o + BLOCK, :] = spots_ref[ORDER[len(outs)][at]].astype(BF16)
            at += 1


ORDER = {8: list(range(8)), 5: [0, 2, 4, 6, 1, 3, 5, 7]}


def place(col_tiles, scales, positions, targets, half, after):
    blocks = [1] * 8 if half == 0 else [1, 1, 1, 1, 4]
    return pl.pallas_call(
        place_kernel,
        grid=(1,),
        in_specs=[
            SMEM,
            pl.BlockSpec((CT_DEV, 4), lambda i: (0, 0)),
            pl.BlockSpec((CT_DEV, TILE), lambda i: (0, 0)),
            pl.BlockSpec((CT_DEV, 2, TILE, TILE), lambda i: (0, half, 0, 0)),
            pl.BlockSpec(memory_space=pl.ANY),
        ],
        out_specs=[pl.BlockSpec((n * BLOCK, TILE), lambda i: (0, 0)) for n in blocks],
        out_shape=[shape_of(n * BLOCK, BF16) for n in blocks],
        scratch_shapes=[
            pltpu.VMEM((len(PEERS), 2 * CAP, TILE, TILE), BF16),
            pltpu.VMEM((len(PEERS), 16, TILE), F32),
            pltpu.SMEM((len(PEERS),), jnp.int32),
        ],
        compiler_params=PARAMS,
        cost_estimate=pl.CostEstimate(flops=4 * 10**9, bytes_accessed=6 << 20, transcendentals=0),
        name=f"place{half}",
    )(targets, positions, scales, col_tiles, after)


def spread(blocks, s_ref, half):
    for n, (ref, o) in enumerate(blocks):
        spots = ref[o + TILES : o + BLOCK, :].astype(F32)
        for slot in range(CAP):
            at = TILE * (n * CAP + slot)
            tiles = []
            for k in range(2):
                s = o + TILE * (2 * slot + k)
                tiles.append(ref[s : s + TILE, :].reshape(8, 16, TILE))
            row = 4 * slot + 2 * half
            picks = [jnp.broadcast_to(spots[row + k : row + k + 1, :], (16, TILE)) for k in range(2)]
            for i in range(4):
                total = None
                for tile, pick in zip(tiles, picks):
                    flag = jnp.where(pick == 4.0 * half + i, 1.0, 0.0).astype(BF16)
                    part = tile * flag[None]
                    total = part if total is None else total + part
                s_ref[TILE * i : TILE * (i + 1), at : at + TILE] = total.reshape(TILE, TILE)


def gram(s_ref, j):
    o = 256 * j
    return lax.dot_general(s_ref[o:, :], s_ref[o : o + 256, :], NT, preferred_element_type=F32)


def add_ridge(m_ref, columns=range(4)):
    row = lax.broadcasted_iota(jnp.int32, (TILE, TILE), 0)
    col = lax.broadcasted_iota(jnp.int32, (TILE, TILE), 1)
    ridge = jnp.where(row == col, jnp.float32(RIDGE), 0.0)
    for j in columns:
        m_ref[j, TILE * j : TILE * (j + 1), :] += ridge


def leaf_kernel(*refs):
    blocks, (l_ref, x_ref, m_ref, s_ref) = refs[:-4], refs[-4:]
    spread([(ref, 0) for ref in blocks], s_ref, 0)
    for j in range(2):
        got = gram(s_ref, j)
        m_ref[2 * j, 256 * j :, :] = got[:, :TILE]
        m_ref[2 * j + 1, 256 * j :, :] = got[:, TILE:]
    add_ridge(m_ref)
    factor(m_ref, l_ref, x_ref)


def leaf(blocks):
    return pl.pallas_call(
        leaf_kernel,
        in_specs=[VMEM] * len(blocks),
        out_specs=[VMEM, VMEM],
        out_shape=[shape_of(SUPER, F32, SUPER)] * 2,
        scratch_shapes=[
            pltpu.VMEM((4, SUPER, TILE), F32),
            pltpu.VMEM((SUPER, WIDTH), BF16),
        ],
        compiler_params=PARAMS,
        cost_estimate=pl.CostEstimate(flops=20 * 10**9, bytes_accessed=5 << 20, transcendentals=0),
        name="leaf",
    )(*blocks)


def panel_kernel(parent_ref, *refs):
    first, second = refs[:8], refs[8:13]
    x_ref, p_ref, a_ref, b_ref, s1_ref, s2_ref = refs[13:]
    spread([(ref, 0) for ref in first], s1_ref, 0)
    own, mate, *pairs = second
    later = [(own, 0), (mate, 0)] + [(ref, o) for ref in pairs for o in (0, BLOCK)]
    spread(later, s2_ref, 1)
    front = split(lax.dot_general(s2_ref[...], s1_ref[...], NT, preferred_element_type=F32))
    left = tuple(part[:, :256] for part in front)
    panels = [dot3(left, split(x_ref[:256, :256])), dot3(front, split(x_ref[256:, :]))]
    panel = jnp.concatenate(panels, axis=1)
    p_ref[...] = panel
    whole = split(panel)
    for j in range(2):
        o = 256 * j
        update = gram(s2_ref, j) - dot3(rows_of(whole, o), rows_of(whole, o, o + 256))
        for n, (row, col) in enumerate(LOWER):
            if col // 2 == j:
                out, at = (a_ref, n) if n < len(FIRST) else (b_ref, n - len(FIRST))
                r, c = TILE * row - o, TILE * col - o
                part = update[r : r + TILE, c : c + TILE]
                out[TILE * at : TILE * (at + 1), :] = part.astype(BF16)
    parent = jnp.full((16, TILE), parent_ref[0, 0].astype(F32)).astype(BF16)
    for out in (a_ref, b_ref):
        out[out.shape[0] - 16 :, :] = parent


def panel(parents, first, second, inverse):
    return pl.pallas_call(
        panel_kernel,
        in_specs=[SMEM] + [VMEM] * 14,
        out_specs=[VMEM] * 3,
        out_shape=[
            shape_of(SUPER, F32, SUPER),
            shape_of(TILE * len(FIRST) + 16, BF16),
            shape_of(TILE * len(SECOND) + 16, BF16),
        ],
        scratch_shapes=[pltpu.VMEM((SUPER, WIDTH), BF16)] * 2,
        compiler_params=PARAMS,
        name="panel",
    )(parents, *first, *second, inverse)


def sort_kernel(x_first, a0, a1, a2, a3, keep_ref, b1, b2, b3):
    c = lax.axis_index("col")
    x, z = c // RING, lax.rem(c, RING)
    rows = keep_ref.shape[0]
    came = (a0, a1, a2, a3)
    parents = [ref[rows:, :].astype(F32)[:8] for ref in came]
    for step, out in enumerate((keep_ref, b1, b2, b3)):
        if x_first:
            wanted = x * RING + lax.rem(z + step, RING)
        else:
            wanted = lax.rem(x + step, RING) * RING + z
        wanted = wanted.astype(F32)
        flags = [jnp.where(parent == wanted, 1.0, 0.0)[None] for parent in parents]
        for r in range(0, rows, TILE):
            total = None
            for flag, ref in zip(flags, came):
                part = ref[r : r + TILE, :].astype(F32).reshape(16, 8, TILE) * flag
                total = part if total is None else total + part
            out[r : r + TILE, :] = total.reshape(TILE, TILE).astype(out.dtype)


def sort(x_first, came):
    rows = came[0].shape[0] - 16

    def kernel(*refs):
        sort_kernel(x_first, *refs)

    return pl.pallas_call(
        kernel,
        in_specs=[VMEM] * 4,
        out_specs=[VMEM] * 4,
        out_shape=[shape_of(rows, t) for t in (F32, BF16, BF16, BF16)],
        compiler_params=PARAMS,
        name="sort_x" if x_first else "sort_z",
    )(*came)


def total_of(parts, at):
    total = None
    for ref in parts:
        part = ref[TILE * at : TILE * (at + 1), :].astype(F32)
        total = part if total is None else total + part
    return total


def start_kernel(*refs):
    parts, (l_ref, m_ref) = refs[:4], refs[4:]
    for i in range(4):
        m_ref[0, TILE * i : TILE * (i + 1), :] = total_of(parts, i)
    add_ridge(m_ref, (0,))
    factor(m_ref, l_ref, steps=(0,))


def start(parts):
    return pl.pallas_call(
        start_kernel,
        in_specs=[VMEM] * 4,
        out_specs=VMEM,
        out_shape=shape_of(SUPER, F32),
        scratch_shapes=[pltpu.VMEM((1, SUPER, TILE), F32)],
        compiler_params=PARAMS,
        cost_estimate=pl.CostEstimate(flops=5 * 10**9, bytes_accessed=1 << 20, transcendentals=0),
        name="start",
    )(*parts)


def rest_kernel(*refs):
    column_ref, parts, (l_ref, m_ref) = refs[0], refs[1:5], refs[5:]
    for n, (i, j) in enumerate(SECOND):
        m_ref[j, TILE * i : TILE * (i + 1), :] = total_of(parts, n)
    add_ridge(m_ref, (1, 2, 3))
    l_ref[:, :TILE] = column_ref[...]
    trail(m_ref, 0, split(column_ref[TILE:, :]))
    factor(m_ref, l_ref, steps=(1, 2, 3))


def rest(column, parts):
    return pl.pallas_call(
        rest_kernel,
        in_specs=[VMEM] * 5,
        out_specs=VMEM,
        out_shape=shape_of(SUPER, F32, SUPER),
        scratch_shapes=[pltpu.VMEM((4, SUPER, TILE), F32)],
        compiler_params=PARAMS,
        name="rest",
    )(column, *parts)


def shift(value, along_x, step):
    pairs = []
    for x in range(RING):
        for z in range(RING):
            to = ((x + step) % RING, z) if along_x else (x, (z + step) % RING)
            pairs.append((x * RING + z, to[0] * RING + to[1]))
    return lax.ppermute(value, "col", pairs)


def hand(value, dy, dc):
    pairs = [(y * 2 + c, (y + dy) % RING * 2 + (c ^ dc)) for y in range(RING) for c in range(2)]
    return lax.ppermute(value, "blk", pairs)


def gather(value, x_first):
    return [value] + [shift(value, x_first, s) for s in (1, 2, 3)]


def scatter(came, x_first):
    own, *sends = sort(x_first, came)
    return [own] + [shift(send, not x_first, s + 1) for s, send in enumerate(sends)]


def on_device(col_tiles, scales, positions, targets, parents):
    out1 = place(col_tiles, scales, positions, targets, 0, targets)
    in1 = list(out1)
    order = ((0, 1), (1, 0), (3, 0), (2, 0), (1, 1), (3, 1), (2, 1))
    for dy, dc in order:
        in1[2 * dy + dc] = hand(out1[2 * dy + dc], dy, dc)
    *keep, give = place(col_tiles, scales, positions, targets, 1, in1[2])
    got = hand(give, 0, 1)
    pairs = [
        jnp.concatenate([keep[dy], got[BLOCK * dy : BLOCK * (dy + 1)]]) for dy in range(1, RING)
    ]
    landed = [in1[2 * dy + dc] for dy, dc in order[:5]]
    landed, pairs = lax.optimization_barrier((landed, pairs))
    for (dy, dc), value in zip(order[:5], landed):
        in1[2 * dy + dc] = value
    in2 = [keep[0], got[:BLOCK]] + [hand(pairs[dy - 1], dy, 0) for dy in (1, 2, 3)]
    leaf_factor, inverse = leaf(in1)
    leaf_panel, first, second = panel(parents, in1, in2, inverse)
    came = gather(first, True)
    came2 = gather(second, False)
    column = start(scatter(came, True))
    parent_factor = rest(column, scatter(came2, False))
    return (leaf_factor[None], leaf_panel[None], parent_factor[None])


def solution(mesh):
    in_specs = (
        P(("col", "blk"), None, None, None),
        P(("col", "blk"), None),
        P(("col", "blk"), None),
        P(("col", "blk"), None),
        P("col", "blk"),
    )
    out_specs = (
        P(("col", "blk"), None, None),
        P(("col", "blk"), None, None),
        P(("col", "blk"), None, None),
    )
    return jax.shard_map(
        on_device, mesh=mesh, in_specs=in_specs, out_specs=out_specs, check_vma=False
    )
```

```python
import jax
import jax.numpy as jnp
from jax import lax
from jax.experimental import pallas as pl
from jax.experimental.pallas import tpu as pltpu
from jax.sharding import PartitionSpec as P

TILE = 128
SUPER = 512
RIDGE = 1.0
CAP = 4
CT_DEV = 16
RING = 4
PEERS = [(dy, dc) for dy in range(RING) for dc in range(2)]
TILES = CAP * 2 * TILE
BLOCK = TILES + 16
WIDTH = len(PEERS) * CAP * TILE
LOWER = [(i, j) for j in range(4) for i in range(j, 4)]
FIRST = LOWER[:5]
SECOND = LOWER[5:]

F32 = jnp.float32
BF16 = jnp.bfloat16
NT = (((1,), (1,)), ((), ()))
NN = (((1,), (0,)), ((), ()))

VMEM = pl.BlockSpec(memory_space=pltpu.VMEM)
SMEM = pl.BlockSpec(memory_space=pltpu.SMEM)
PARAMS = pltpu.CompilerParams(vmem_limit_bytes=56 << 20)


def shape_of(rows, dtype, columns=TILE):
    return jax.ShapeDtypeStruct((rows, columns), dtype)


def split(a):
    high = a.astype(BF16)
    return high, (a - high.astype(F32)).astype(BF16)


def dot3(a, b, dims=NT):
    x = jnp.concatenate([a[0], a[1], a[0]], axis=1)
    y = jnp.concatenate([b[0], b[0], b[1]], axis=1 if dims is NT else 0)
    return lax.dot_general(x, y, dims, preferred_element_type=F32)


def rows_of(pair, start, stop=None):
    return tuple(part[start:stop] for part in pair)


def on_top(pair):
    return tuple(jnp.concatenate([part, jnp.zeros_like(part)], axis=0) for part in pair)


def below(pair):
    return tuple(jnp.concatenate([jnp.zeros_like(part), part], axis=0) for part in pair)


def lane(v, j):
    return jnp.broadcast_to(v[:, j : j + 1], (8, TILE))


def sub(v, i):
    return jnp.broadcast_to(v[i : i + 1, :], (8, TILE))


def eliminate64(aug, base):
    w = [aug[8 * q : 8 * q + 8] for q in range(8)]
    out = []
    sid = lax.broadcasted_iota(jnp.int32, (8, TILE), 0)
    own = [lane(w[0], base + k) for k in range(8)]
    for p in range(8):
        at = base + 8 * p
        cols = [[lane(w[q], at + k) for k in range(8)] for q in range(p + 1, 8)]
        last = p == 7
        if not last:
            ahead = [lane(w[p + 1], at + 8 + k) for k in range(8)]
        rows = [sub(w[p], k) for k in range(8)]
        scale = None
        for k in range(8):
            if k % 2 == 0:
                a, b, c = sub(own[k], k), sub(own[k], k + 1), sub(own[k + 1], k + 1)
                r = lax.rsqrt(a)
                scale = lax.rsqrt(a * c - b * b) * (a * r)
            else:
                r = scale
            low = own[k] * r
            mult = [sub(low, i) if i > k else None for i in range(8)]
            for j in range(k + 1, 8):
                own[j] = own[j] - low * mult[j]
            rows[k] = rows[k] * r
            for i in range(k + 1, 8):
                rows[i] = rows[i] - mult[i] * rows[k]
            for q in range(p + 1, 8):
                col = cols[q - p - 1]
                lq = col[k] * r
                for j in range(k + 1, 8):
                    col[j] = col[j] - lq * mult[j]
                w[q] = w[q] - lq * rows[k]
                if q == p + 1:
                    for j in range(8):
                        ahead[j] = ahead[j] - lq * sub(lq, j)
        block = rows[0]
        for k in range(1, 8):
            block = jnp.where(sid == k, rows[k], block)
        out.append(block)
        if not last:
            own = ahead
    return jnp.concatenate(out, axis=0)


def trail(m_ref, kb, panels):
    for j in range(kb + 1, 4):
        s = TILE * (j - kb - 1)
        m_ref[j, TILE * j :, :] -= dot3(rows_of(panels, s), rows_of(panels, s, s + TILE))


def factor(m_ref, l_ref, x_ref=None):
    col_id = lax.broadcasted_iota(jnp.int32, (64, TILE), 1)
    row_id = lax.broadcasted_iota(jnp.int32, (64, TILE), 0)
    eye = (col_id % 64 == row_id).astype(F32)
    left = col_id < 64
    lower = row_id >= col_id % 64
    zero = jnp.zeros((), F32)

    def keep_left(v):
        return jnp.where(lax.broadcasted_iota(jnp.int32, v.shape, 1) < 64, v, zero)

    def keep_right(v):
        return jnp.where(lax.broadcasted_iota(jnp.int32, v.shape, 1) < 64, zero, v)

    corner = pltpu.roll(m_ref[0, :64, :], 64, 1)
    for kb in range(4):
        o = TILE * kb
        if kb:
            l_ref[:o, o : o + TILE] = jnp.zeros((o, TILE), F32)
        corner_b = pltpu.roll(m_ref[kb, o + 64 : o + TILE, :], 64, 1)
        lhs = split(keep_left(m_ref[kb, o + 64 :, :]))
        w1 = eliminate64(jnp.where(left, eye, corner), 64)
        x1 = on_top(split(w1))
        l21 = dot3(rows_of(lhs, 0, 64), x1)
        l21s = split(l21)
        w2 = eliminate64(jnp.where(left, corner_b - dot3(l21s, on_top(l21s)), eye), 0)
        if kb < 3:
            pa = dot3(rows_of(lhs, 64), x1)
            pas = split(pa)
            rest = split(keep_right(m_ref[kb, o + TILE :, :] - dot3(pas, below(l21s))))
            x2 = below(split(w2))
            n = o + TILE
            pa_d = rows_of(pas, 0, 64)
            corner = pltpu.roll(m_ref[kb + 1, n : n + 64, :], 64, 1) - dot3(pa_d, below(pa_d))
            pb_d = dot3(rows_of(rest, 0, 64), x2)
            pb_ds = split(pb_d)
            corner = corner - dot3(pb_ds, below(pb_ds))
            pb = jnp.concatenate([pb_d, dot3(rows_of(rest, 64), x2)], axis=0)
            panel = pa + pb
            l_ref[n:, o:n] = panel
            trail(m_ref, kb, split(panel))
        flip = jnp.concatenate([w1, w2], axis=0).T
        l_ref[o : o + 64, o : o + TILE] = jnp.where(left & lower, flip[64:], zero)
        l_ref[o + 64 : o + TILE, o : o + TILE] = jnp.where(left, l21, jnp.where(lower, flip[:64], zero))
        if x_ref is not None:
            x1f = jnp.where(left, w1, zero)
            x2f = jnp.where(left, zero, w2)
            t = dot3(l21s, on_top(split(x1f)), NN)
            x21 = -dot3(split(x2f), below(split(t)), NN)
            x = jnp.concatenate([x1f, jnp.where(left, x21, x2f)], axis=0)
            x_ref[o : o + TILE, o : o + TILE] = x
            if kb < 3:
                x_ref[o : o + TILE, o + TILE :] = jnp.zeros((TILE, SUPER - TILE - o), F32)
            if kb:
                before = dot3(split(l_ref[o : o + TILE, :o]), split(x_ref[:o, :o]), NN)
                x_ref[o : o + TILE, :o] = -dot3(split(x), split(before), NN)


def place_kernel(target_ref, spot_ref, scale_ref, tile_ref, *refs):
    outs, (block_ref, spots_ref, count_ref) = refs[:13], refs[13:]
    me = lax.axis_index("blk")
    for peer in range(len(PEERS)):
        count_ref[peer] = 0
    block_ref[...] = jnp.zeros(block_ref.shape, BF16)
    spots_ref[...] = jnp.zeros(spots_ref.shape, F32)
    for t in range(CT_DEV):
        owner = target_ref[0, t]
        peer = lax.rem(owner // 2 - me // 2 + RING, RING) * 2 + lax.rem(owner + me, 2)
        rank = count_ref[peer]
        count_ref[peer] = rank + 1
        root = jnp.sqrt(scale_ref[t : t + 1, :])
        for k in range(4):
            scaled = tile_ref[t, k].astype(F32) * root
            block_ref[k // 2, peer, 2 * rank + k % 2] = scaled.astype(BF16)
            spot = jnp.broadcast_to(spot_ref[k : k + 1, t : t + 1].astype(F32), (1, TILE))
            spots_ref[peer, pl.ds(4 * rank + k, 1), :] = spot
    pieces = [(out, 0, 0, peer) for peer, out in enumerate(outs[:8])]
    pieces += [(out, 0, 1, 2 * dy) for dy, out in enumerate(outs[8:12])]
    pieces += [(outs[12], BLOCK * dy, 1, 2 * dy + 1) for dy in range(RING)]
    for out, o, half, peer in pieces:
        out[o : o + TILES, :] = block_ref[half, peer].reshape(TILES, TILE)
        out[o + TILES : o + BLOCK, :] = spots_ref[peer].astype(BF16)


def place(col_tiles, scales, positions, targets):
    blocks = [1] * 12 + [4]
    return pl.pallas_call(
        place_kernel,
        grid=(1,),
        in_specs=[
            SMEM,
            pl.BlockSpec((4, CT_DEV), lambda i: (0, 0)),
            pl.BlockSpec((CT_DEV, TILE), lambda i: (0, 0)),
            pl.BlockSpec((CT_DEV, 4, TILE, TILE), lambda i: (0, 0, 0, 0)),
        ],
        out_specs=[pl.BlockSpec((n * BLOCK, TILE), lambda i: (0, 0)) for n in blocks],
        out_shape=[shape_of(n * BLOCK, BF16) for n in blocks],
        scratch_shapes=[
            pltpu.VMEM((2, len(PEERS), 2 * CAP, TILE, TILE), BF16),
            pltpu.VMEM((len(PEERS), 16, TILE), F32),
            pltpu.SMEM((len(PEERS),), jnp.int32),
        ],
        compiler_params=PARAMS,
        name="place",
    )(targets.T, positions.T, scales, col_tiles)


def spread(blocks, s_ref, half):
    for n, (ref, o) in enumerate(blocks):
        spots = ref[o + TILES : o + BLOCK, :].astype(F32)
        for slot in range(CAP):
            at = TILE * (n * CAP + slot)
            tiles = []
            for k in range(2):
                s = o + TILE * (2 * slot + k)
                tiles.append(ref[s : s + TILE, :].reshape(8, 16, TILE))
            row = 4 * slot + 2 * half
            picks = [jnp.broadcast_to(spots[row + k : row + k + 1, :], (16, TILE)) for k in range(2)]
            for i in range(4):
                total = None
                for tile, pick in zip(tiles, picks):
                    flag = jnp.where(pick == 4.0 * half + i, 1.0, 0.0).astype(BF16)
                    part = tile * flag[None]
                    total = part if total is None else total + part
                s_ref[TILE * i : TILE * (i + 1), at : at + TILE] = total.reshape(TILE, TILE)


def gram(s_ref, j):
    o = 256 * j
    return lax.dot_general(s_ref[o:, :], s_ref[o : o + 256, :], NT, preferred_element_type=F32)


def add_ridge(m_ref):
    row = lax.broadcasted_iota(jnp.int32, (TILE, TILE), 0)
    col = lax.broadcasted_iota(jnp.int32, (TILE, TILE), 1)
    ridge = jnp.where(row == col, jnp.float32(RIDGE), 0.0)
    for j in range(4):
        m_ref[j, TILE * j : TILE * (j + 1), :] += ridge


def leaf_kernel(*refs):
    blocks, (l_ref, x_ref, m_ref, s_ref) = refs[:-4], refs[-4:]
    spread([(ref, 0) for ref in blocks], s_ref, 0)
    for j in range(2):
        got = gram(s_ref, j)
        m_ref[2 * j, 256 * j :, :] = got[:, :TILE]
        m_ref[2 * j + 1, 256 * j :, :] = got[:, TILE:]
    add_ridge(m_ref)
    factor(m_ref, l_ref, x_ref)


def leaf(blocks):
    return pl.pallas_call(
        leaf_kernel,
        in_specs=[VMEM] * len(blocks),
        out_specs=[VMEM, VMEM],
        out_shape=[shape_of(SUPER, F32, SUPER)] * 2,
        scratch_shapes=[
            pltpu.VMEM((4, SUPER, TILE), F32),
            pltpu.VMEM((SUPER, WIDTH), BF16),
        ],
        compiler_params=PARAMS,
        cost_estimate=pl.CostEstimate(flops=20 * 10**9, bytes_accessed=5 << 20, transcendentals=0),
        name="leaf",
    )(*blocks)


def singles(refs):
    return [(ref, o) for ref in refs for o in range(0, ref.shape[0], BLOCK)]


def early_kernel(after_ref, *refs):
    del after_ref
    first, second = refs[:4], refs[4:7]
    f_ref, g_ref, s1_ref, s2_ref = refs[7:]
    spread(singles(first), s1_ref, 0)
    spread(singles(second), s2_ref, 1)
    f_ref[...] = lax.dot_general(s2_ref[...], s1_ref[...], NT, preferred_element_type=F32)
    for j in range(2):
        g_ref[256 * j :, 256 * j : 256 * (j + 1)] = gram(s2_ref, j)


def early(first, second, after):
    return pl.pallas_call(
        early_kernel,
        in_specs=[pl.BlockSpec(memory_space=pl.ANY)] + [VMEM] * 7,
        out_specs=[VMEM] * 2,
        out_shape=[shape_of(SUPER, F32, SUPER)] * 2,
        scratch_shapes=[pltpu.VMEM((SUPER, WIDTH // 2), BF16)] * 2,
        compiler_params=PARAMS,
        cost_estimate=pl.CostEstimate(flops=4 * 10**9, bytes_accessed=5 << 20, transcendentals=0),
        name="early",
    )(after, *first, *second)


def panel_kernel(parent_ref, *refs):
    first, second, fronts = refs[:4], refs[4:6], refs[6:8]
    x_ref, p_ref, a_ref, b_ref, s1_ref, s2_ref = refs[8:]
    spread(singles(first), s1_ref, 0)
    spread(singles(second), s2_ref, 1)
    late = lax.dot_general(s2_ref[...], s1_ref[...], NT, preferred_element_type=F32)
    front = split(fronts[0][...] + late)
    left = tuple(part[:, :256] for part in front)
    panels = [dot3(left, split(x_ref[:256, :256])), dot3(front, split(x_ref[256:, :]))]
    panel = jnp.concatenate(panels, axis=1)
    p_ref[...] = panel
    whole = split(panel)
    for j in range(2):
        o = 256 * j
        update = fronts[1][o:, o : o + 256] + gram(s2_ref, j)
        update = update - dot3(rows_of(whole, o), rows_of(whole, o, o + 256))
        for n, (row, col) in enumerate(LOWER):
            if col // 2 == j:
                out, at = (a_ref, n) if n < len(FIRST) else (b_ref, n - len(FIRST))
                r, c = TILE * row - o, TILE * col - o
                part = update[r : r + TILE, c : c + TILE]
                out[TILE * at : TILE * (at + 1), :] = part.astype(BF16)
    parent = jnp.full((16, TILE), parent_ref[0, 0].astype(F32)).astype(BF16)
    for out in (a_ref, b_ref):
        out[out.shape[0] - 16 :, :] = parent


def panel(parents, first, second, fronts, inverse):
    return pl.pallas_call(
        panel_kernel,
        in_specs=[SMEM] + [VMEM] * 9,
        out_specs=[VMEM] * 3,
        out_shape=[
            shape_of(SUPER, F32, SUPER),
            shape_of(TILE * len(FIRST) + 16, BF16),
            shape_of(TILE * len(SECOND) + 16, BF16),
        ],
        scratch_shapes=[pltpu.VMEM((SUPER, WIDTH // 2), BF16)] * 2,
        compiler_params=PARAMS,
        name="panel",
    )(parents, *first, *second, *fronts, inverse)


def sort_kernel(x_first, a0, a1, a2, a3, keep_ref, b1, b2, b3):
    c = lax.axis_index("col")
    x, z = c // RING, lax.rem(c, RING)
    rows = keep_ref.shape[0]
    came = (a0, a1, a2, a3)
    parents = [ref[rows:, :].astype(F32)[:8] for ref in came]
    flags = []
    for step in range(RING):
        if x_first:
            wanted = x * RING + lax.rem(z + step, RING)
        else:
            wanted = lax.rem(x + step, RING) * RING + z
        wanted = wanted.astype(F32)
        flags.append([jnp.where(parent == wanted, 1.0, 0.0)[None] for parent in parents])
    for r in range(0, rows, TILE):
        parts = [ref[r : r + TILE, :].astype(F32).reshape(16, 8, TILE) for ref in came]
        for flag, out in zip(flags, (keep_ref, b1, b2, b3)):
            total = parts[0] * flag[0]
            for s in range(1, RING):
                total = total + parts[s] * flag[s]
            out[r : r + TILE, :] = total.reshape(TILE, TILE).astype(out.dtype)


def whole_of(array):
    return pl.BlockSpec(array.shape, lambda i: (0, 0))


def sort(x_first, came):
    rows = came[0].shape[0] - 16

    def kernel(*refs):
        sort_kernel(x_first, *refs)

    return pl.pallas_call(
        kernel,
        grid=(1,),
        in_specs=[whole_of(part) for part in came],
        out_specs=[pl.BlockSpec((rows, TILE), lambda i: (0, 0))] * 4,
        out_shape=[shape_of(rows, t) for t in (F32, BF16, BF16, BF16)],
        compiler_params=PARAMS,
        name="sort_x" if x_first else "sort_z",
    )(*came)


def total_of(parts, at):
    total = None
    for ref in parts:
        part = ref[TILE * at : TILE * (at + 1), :].astype(F32)
        total = part if total is None else total + part
    return total


def parent_kernel(*refs):
    first, second, (l_ref, m_ref) = refs[:4], refs[4:8], refs[8:]
    for n, (i, j) in enumerate(LOWER):
        parts, at = (first, n) if n < len(FIRST) else (second, n - len(FIRST))
        m_ref[j, TILE * i : TILE * (i + 1), :] = total_of(parts, at)
    add_ridge(m_ref)
    factor(m_ref, l_ref)


def parent(parts):
    return pl.pallas_call(
        parent_kernel,
        grid=(1,),
        in_specs=[whole_of(part) for part in parts],
        out_specs=pl.BlockSpec((SUPER, SUPER), lambda i: (0, 0)),
        out_shape=shape_of(SUPER, F32, SUPER),
        scratch_shapes=[pltpu.VMEM((4, SUPER, TILE), F32)],
        compiler_params=PARAMS,
        name="parent",
    )(*parts)


def shift(value, along_x, step):
    pairs = []
    for x in range(RING):
        for z in range(RING):
            to = ((x + step) % RING, z) if along_x else (x, (z + step) % RING)
            pairs.append((x * RING + z, to[0] * RING + to[1]))
    return lax.ppermute(value, "col", pairs)


def hand(value, dy, dc):
    pairs = [(y * 2 + c, (y + dy) % RING * 2 + (c ^ dc)) for y in range(RING) for c in range(2)]
    return lax.ppermute(value, "blk", pairs)


def gather(value, x_first):
    return [value] + [shift(value, x_first, s) for s in (1, 2, 3)]


def scatter(came, x_first):
    own, *sends = sort(x_first, came)
    return [own] + [shift(send, not x_first, s + 1) for s, send in enumerate(sends)]


def on_device(col_tiles, scales, positions, targets, parents):
    *blocks, give = place(col_tiles, scales, positions, targets)
    in1, keep = blocks[:8], blocks[8:]
    order = ((1, 0), (3, 0), (2, 0), (1, 1), (3, 1), (2, 1), (0, 1))
    for dy, dc in order:
        in1[2 * dy + dc] = hand(in1[2 * dy + dc], dy, dc)
    got = hand(give, 0, 1)
    pairs = [
        jnp.concatenate([keep[dy], got[BLOCK * dy : BLOCK * (dy + 1)]]) for dy in range(1, RING)
    ]
    landed = [in1[2 * dy + dc] for dy, dc in order[:4]]
    landed, pairs = lax.optimization_barrier((landed, pairs))
    for (dy, dc), value in zip(order[:4], landed):
        in1[2 * dy + dc] = value
    in2 = [hand(pairs[dy - 1], dy, 0) for dy in (1, 2, 3)]
    leaf_factor, inverse = leaf(in1)
    fronts = early(in1[:4], [keep[0], got[:BLOCK], in2[0]], inverse)
    leaf_panel, first, second = panel(parents, in1[4:], in2[1:], fronts, inverse)
    came = gather(first, True)
    came2 = gather(second, False)
    parent_factor = parent(scatter(came, True) + scatter(came2, False))
    return (leaf_factor[None], leaf_panel[None], parent_factor[None])


def solution(mesh):
    in_specs = (
        P(("col", "blk"), None, None, None),
        P(("col", "blk"), None),
        P(("col", "blk"), None),
        P(("col", "blk"), None),
        P("col", "blk"),
    )
    out_specs = (
        P(("col", "blk"), None, None),
        P(("col", "blk"), None, None),
        P(("col", "blk"), None, None),
    )
    return jax.shard_map(
        on_device, mesh=mesh, in_specs=in_specs, out_specs=out_specs, check_vma=False
    )
```

```python
import jax
import jax.numpy as jnp
from jax import lax
from jax.experimental import pallas as pl
from jax.experimental.pallas import tpu as pltpu
from jax.sharding import PartitionSpec as P

TILE = 128
SUPER = 512
RIDGE = 1.0
CAP = 4
CT_DEV = 16
RING = 4
PEERS = [(dy, dc) for dy in range(RING) for dc in range(2)]
TILES = CAP * 2 * TILE
BLOCK = TILES + 16
WIDTH = len(PEERS) * CAP * TILE
LOWER = [(i, j) for j in range(4) for i in range(j, 4)]
FIRST = LOWER[:5]
SECOND = LOWER[5:]

F32 = jnp.float32
BF16 = jnp.bfloat16
NT = (((1,), (1,)), ((), ()))
NN = (((1,), (0,)), ((), ()))

VMEM = pl.BlockSpec(memory_space=pltpu.VMEM)
SMEM = pl.BlockSpec(memory_space=pltpu.SMEM)
PARAMS = pltpu.CompilerParams(vmem_limit_bytes=56 << 20)


def shape_of(rows, dtype, columns=TILE):
    return jax.ShapeDtypeStruct((rows, columns), dtype)


def split(a):
    high = a.astype(BF16)
    return high, (a - high.astype(F32)).astype(BF16)


def dot3(a, b, dims=NT):
    x = jnp.concatenate([a[0], a[1], a[0]], axis=1)
    y = jnp.concatenate([b[0], b[0], b[1]], axis=1 if dims is NT else 0)
    return lax.dot_general(x, y, dims, preferred_element_type=F32)


def rows_of(pair, start, stop=None):
    return tuple(part[start:stop] for part in pair)


def on_top(pair):
    return tuple(jnp.concatenate([part, jnp.zeros_like(part)], axis=0) for part in pair)


def below(pair):
    return tuple(jnp.concatenate([jnp.zeros_like(part), part], axis=0) for part in pair)


def lane(v, j):
    return jnp.broadcast_to(v[:, j : j + 1], (8, TILE))


def sub(v, i):
    return jnp.broadcast_to(v[i : i + 1, :], (8, TILE))


def eliminate64(aug, base):
    w = [aug[8 * q : 8 * q + 8] for q in range(8)]
    out = []
    sid = lax.broadcasted_iota(jnp.int32, (8, TILE), 0)
    own = [lane(w[0], base + k) for k in range(8)]
    for p in range(8):
        at = base + 8 * p
        cols = [[lane(w[q], at + k) for k in range(8)] for q in range(p + 1, 8)]
        last = p == 7
        if not last:
            ahead = [lane(w[p + 1], at + 8 + k) for k in range(8)]
        rows = [sub(w[p], k) for k in range(8)]
        scale = None
        for k in range(8):
            if k % 2 == 0:
                a, b, c = sub(own[k], k), sub(own[k], k + 1), sub(own[k + 1], k + 1)
                r = lax.rsqrt(a)
                scale = lax.rsqrt(a * c - b * b) * (a * r)
            else:
                r = scale
            low = own[k] * r
            mult = [sub(low, i) if i > k else None for i in range(8)]
            for j in range(k + 1, 8):
                own[j] = own[j] - low * mult[j]
            rows[k] = rows[k] * r
            for i in range(k + 1, 8):
                rows[i] = rows[i] - mult[i] * rows[k]
            for q in range(p + 1, 8):
                col = cols[q - p - 1]
                lq = col[k] * r
                for j in range(k + 1, 8):
                    col[j] = col[j] - lq * mult[j]
                w[q] = w[q] - lq * rows[k]
                if q == p + 1:
                    for j in range(8):
                        ahead[j] = ahead[j] - lq * sub(lq, j)
        block = rows[0]
        for k in range(1, 8):
            block = jnp.where(sid == k, rows[k], block)
        out.append(block)
        if not last:
            own = ahead
    return jnp.concatenate(out, axis=0)


def trail(m_ref, kb, panels):
    for j in range(kb + 1, 4):
        s = TILE * (j - kb - 1)
        m_ref[j, TILE * j :, :] -= dot3(rows_of(panels, s), rows_of(panels, s, s + TILE))


def factor(m_ref, l_ref, x_ref=None):
    col_id = lax.broadcasted_iota(jnp.int32, (64, TILE), 1)
    row_id = lax.broadcasted_iota(jnp.int32, (64, TILE), 0)
    eye = (col_id % 64 == row_id).astype(F32)
    left = col_id < 64
    lower = row_id >= col_id % 64
    zero = jnp.zeros((), F32)

    def keep_left(v):
        return jnp.where(lax.broadcasted_iota(jnp.int32, v.shape, 1) < 64, v, zero)

    def keep_right(v):
        return jnp.where(lax.broadcasted_iota(jnp.int32, v.shape, 1) < 64, zero, v)

    corner = pltpu.roll(m_ref[0, :64, :], 64, 1)
    for kb in range(4):
        o = TILE * kb
        if kb:
            l_ref[:o, o : o + TILE] = jnp.zeros((o, TILE), F32)
        corner_b = pltpu.roll(m_ref[kb, o + 64 : o + TILE, :], 64, 1)
        lhs = split(keep_left(m_ref[kb, o + 64 :, :]))
        w1 = eliminate64(jnp.where(left, eye, corner), 64)
        x1 = on_top(split(w1))
        l21 = dot3(rows_of(lhs, 0, 64), x1)
        l21s = split(l21)
        w2 = eliminate64(jnp.where(left, corner_b - dot3(l21s, on_top(l21s)), eye), 0)
        if kb < 3:
            pa = dot3(rows_of(lhs, 64), x1)
            pas = split(pa)
            rest = split(keep_right(m_ref[kb, o + TILE :, :] - dot3(pas, below(l21s))))
            x2 = below(split(w2))
            n = o + TILE
            pa_d = rows_of(pas, 0, 64)
            corner = pltpu.roll(m_ref[kb + 1, n : n + 64, :], 64, 1) - dot3(pa_d, below(pa_d))
            pb_d = dot3(rows_of(rest, 0, 64), x2)
            pb_ds = split(pb_d)
            corner = corner - dot3(pb_ds, below(pb_ds))
            pb = jnp.concatenate([pb_d, dot3(rows_of(rest, 64), x2)], axis=0)
            panel = pa + pb
            l_ref[n:, o:n] = panel
            trail(m_ref, kb, split(panel))
        flip = jnp.concatenate([w1, w2], axis=0).T
        l_ref[o : o + 64, o : o + TILE] = jnp.where(left & lower, flip[64:], zero)
        l_ref[o + 64 : o + TILE, o : o + TILE] = jnp.where(left, l21, jnp.where(lower, flip[:64], zero))
        if x_ref is not None:
            x1f = jnp.where(left, w1, zero)
            x2f = jnp.where(left, zero, w2)
            t = dot3(l21s, on_top(split(x1f)), NN)
            x21 = -dot3(split(x2f), below(split(t)), NN)
            x = jnp.concatenate([x1f, jnp.where(left, x21, x2f)], axis=0)
            x_ref[o : o + TILE, o : o + TILE] = x
            if kb < 3:
                x_ref[o : o + TILE, o + TILE :] = jnp.zeros((TILE, SUPER - TILE - o), F32)
            if kb:
                before = dot3(split(l_ref[o : o + TILE, :o]), split(x_ref[:o, :o]), NN)
                x_ref[o : o + TILE, :o] = -dot3(split(x), split(before), NN)


def place_kernel(target_ref, spot_ref, scale_ref, tile_ref, *refs):
    outs, (block_ref, spots_ref, count_ref) = refs[:13], refs[13:]
    me = lax.axis_index("blk")
    for peer in range(len(PEERS)):
        count_ref[peer] = 0
    block_ref[...] = jnp.zeros(block_ref.shape, BF16)
    spots_ref[...] = jnp.zeros(spots_ref.shape, F32)
    for t in range(CT_DEV):
        owner = target_ref[0, t]
        peer = lax.rem(owner // 2 - me // 2 + RING, RING) * 2 + lax.rem(owner + me, 2)
        rank = count_ref[peer]
        count_ref[peer] = rank + 1
        root = jnp.sqrt(scale_ref[t : t + 1, :])
        for k in range(4):
            scaled = tile_ref[t, k].astype(F32) * root
            block_ref[k // 2, peer, 2 * rank + k % 2] = scaled.astype(BF16)
            spot = jnp.broadcast_to(spot_ref[k : k + 1, t : t + 1].astype(F32), (1, TILE))
            spots_ref[peer, pl.ds(4 * rank + k, 1), :] = spot
    pieces = [(out, 0, 0, peer) for peer, out in enumerate(outs[:8])]
    pieces += [(out, 0, 1, 2 * dy) for dy, out in enumerate(outs[8:12])]
    pieces += [(outs[12], BLOCK * dy, 1, 2 * dy + 1) for dy in range(RING)]
    for out, o, half, peer in pieces:
        out[o : o + TILES, :] = block_ref[half, peer].reshape(TILES, TILE)
        out[o + TILES : o + BLOCK, :] = spots_ref[peer].astype(BF16)


def place(col_tiles, scales, positions, targets):
    blocks = [1] * 12 + [4]
    return pl.pallas_call(
        place_kernel,
        grid=(1,),
        in_specs=[
            SMEM,
            pl.BlockSpec((4, CT_DEV), lambda i: (0, 0)),
            pl.BlockSpec((CT_DEV, TILE), lambda i: (0, 0)),
            pl.BlockSpec((CT_DEV, 4, TILE, TILE), lambda i: (0, 0, 0, 0)),
        ],
        out_specs=[pl.BlockSpec((n * BLOCK, TILE), lambda i: (0, 0)) for n in blocks],
        out_shape=[shape_of(n * BLOCK, BF16) for n in blocks],
        scratch_shapes=[
            pltpu.VMEM((2, len(PEERS), 2 * CAP, TILE, TILE), BF16),
            pltpu.VMEM((len(PEERS), 16, TILE), F32),
            pltpu.SMEM((len(PEERS),), jnp.int32),
        ],
        compiler_params=PARAMS,
        name="place",
    )(targets.T, positions.T, scales, col_tiles)


def spread(blocks, s_ref, half):
    for n, (ref, o) in enumerate(blocks):
        spots = ref[o + TILES : o + BLOCK, :].astype(F32)
        for slot in range(CAP):
            at = TILE * (n * CAP + slot)
            tiles = []
            for k in range(2):
                s = o + TILE * (2 * slot + k)
                tiles.append(ref[s : s + TILE, :].reshape(8, 16, TILE))
            row = 4 * slot + 2 * half
            picks = [jnp.broadcast_to(spots[row + k : row + k + 1, :], (16, TILE)) for k in range(2)]
            for i in range(4):
                total = None
                for tile, pick in zip(tiles, picks):
                    flag = jnp.where(pick == 4.0 * half + i, 1.0, 0.0).astype(BF16)
                    part = tile * flag[None]
                    total = part if total is None else total + part
                s_ref[TILE * i : TILE * (i + 1), at : at + TILE] = total.reshape(TILE, TILE)


def gram(s_ref, j):
    o = 256 * j
    return lax.dot_general(s_ref[o:, :], s_ref[o : o + 256, :], NT, preferred_element_type=F32)


def add_ridge(m_ref):
    row = lax.broadcasted_iota(jnp.int32, (TILE, TILE), 0)
    col = lax.broadcasted_iota(jnp.int32, (TILE, TILE), 1)
    ridge = jnp.where(row == col, jnp.float32(RIDGE), 0.0)
    for j in range(4):
        m_ref[j, TILE * j : TILE * (j + 1), :] += ridge


def leaf_kernel(*refs):
    blocks, (l_ref, x_ref, m_ref, s_ref) = refs[:-4], refs[-4:]
    spread([(ref, 0) for ref in blocks], s_ref, 0)
    for j in range(2):
        got = gram(s_ref, j)
        m_ref[2 * j, 256 * j :, :] = got[:, :TILE]
        m_ref[2 * j + 1, 256 * j :, :] = got[:, TILE:]
    add_ridge(m_ref)
    factor(m_ref, l_ref, x_ref)


def leaf(blocks):
    return pl.pallas_call(
        leaf_kernel,
        in_specs=[VMEM] * len(blocks),
        out_specs=[VMEM, VMEM],
        out_shape=[shape_of(SUPER, F32, SUPER)] * 2,
        scratch_shapes=[
            pltpu.VMEM((4, SUPER, TILE), F32),
            pltpu.VMEM((SUPER, WIDTH), BF16),
        ],
        compiler_params=PARAMS,
        cost_estimate=pl.CostEstimate(flops=20 * 10**9, bytes_accessed=5 << 20, transcendentals=0),
        name="leaf",
    )(*blocks)


def singles(refs):
    return [(ref, o) for ref in refs for o in range(0, ref.shape[0], BLOCK)]


def early_kernel(after_ref, *refs):
    del after_ref
    first, second = refs[:4], refs[4:7]
    f_ref, g_ref, s1_ref, s2_ref = refs[7:]
    spread(singles(first), s1_ref, 0)
    spread(singles(second), s2_ref, 1)
    f_ref[...] = lax.dot_general(s2_ref[...], s1_ref[...], NT, preferred_element_type=F32)
    for j in range(2):
        g_ref[256 * j :, 256 * j : 256 * (j + 1)] = gram(s2_ref, j)


def early(first, second, after):
    return pl.pallas_call(
        early_kernel,
        in_specs=[pl.BlockSpec(memory_space=pl.ANY)] + [VMEM] * 7,
        out_specs=[VMEM] * 2,
        out_shape=[shape_of(SUPER, F32, SUPER)] * 2,
        scratch_shapes=[pltpu.VMEM((SUPER, WIDTH // 2), BF16)] * 2,
        compiler_params=PARAMS,
        cost_estimate=pl.CostEstimate(flops=4 * 10**9, bytes_accessed=5 << 20, transcendentals=0),
        name="early",
    )(after, *first, *second)


def panel_kernel(parent_ref, *refs):
    first, second, fronts = refs[:4], refs[4:6], refs[6:8]
    x_ref, p_ref, a_ref, b_ref, s1_ref, s2_ref = refs[8:]
    spread(singles(first), s1_ref, 0)
    spread(singles(second), s2_ref, 1)
    late = lax.dot_general(s2_ref[...], s1_ref[...], NT, preferred_element_type=F32)
    front = split(fronts[0][...] + late)
    left = tuple(part[:, :256] for part in front)
    panels = [dot3(left, split(x_ref[:256, :256])), dot3(front, split(x_ref[256:, :]))]
    panel = jnp.concatenate(panels, axis=1)
    p_ref[...] = panel
    whole = split(panel)
    for j in range(2):
        o = 256 * j
        update = fronts[1][o:, o : o + 256] + gram(s2_ref, j)
        update = update - dot3(rows_of(whole, o), rows_of(whole, o, o + 256))
        for n, (row, col) in enumerate(LOWER):
            if col // 2 == j:
                out, at = (a_ref, n) if n < len(FIRST) else (b_ref, n - len(FIRST))
                r, c = TILE * row - o, TILE * col - o
                part = update[r : r + TILE, c : c + TILE]
                out[TILE * at : TILE * (at + 1), :] = part.astype(BF16)
    parent = jnp.full((16, TILE), parent_ref[0, 0].astype(F32)).astype(BF16)
    for out in (a_ref, b_ref):
        out[out.shape[0] - 16 :, :] = parent


def panel(parents, first, second, fronts, inverse):
    return pl.pallas_call(
        panel_kernel,
        in_specs=[SMEM] + [VMEM] * 9,
        out_specs=[VMEM] * 3,
        out_shape=[
            shape_of(SUPER, F32, SUPER),
            shape_of(TILE * len(FIRST) + 16, BF16),
            shape_of(TILE * len(SECOND) + 16, BF16),
        ],
        scratch_shapes=[pltpu.VMEM((SUPER, WIDTH // 2), BF16)] * 2,
        compiler_params=PARAMS,
        name="panel",
    )(parents, *first, *second, *fronts, inverse)


def sort_kernel(x_first, a0, a1, a2, a3, keep_ref, b1, b2, b3):
    c = lax.axis_index("col")
    x, z = c // RING, lax.rem(c, RING)
    rows = keep_ref.shape[0]
    came = (a0, a1, a2, a3)
    parents = [ref[rows:, :].astype(F32)[:8] for ref in came]
    flags = []
    for step in range(RING):
        if x_first:
            wanted = x * RING + lax.rem(z + step, RING)
        else:
            wanted = lax.rem(x + step, RING) * RING + z
        wanted = wanted.astype(F32)
        flags.append([jnp.where(parent == wanted, 1.0, 0.0)[None] for parent in parents])
    for r in range(0, rows, TILE):
        parts = [ref[r : r + TILE, :].astype(F32).reshape(16, 8, TILE) for ref in came]
        for flag, out in zip(flags, (keep_ref, b1, b2, b3)):
            total = parts[0] * flag[0]
            for s in range(1, RING):
                total = total + parts[s] * flag[s]
            out[r : r + TILE, :] = total.reshape(TILE, TILE).astype(out.dtype)


def whole_of(array):
    return pl.BlockSpec(array.shape, lambda i: (0, 0))


def sort(x_first, came):
    rows = came[0].shape[0] - 16

    def kernel(*refs):
        sort_kernel(x_first, *refs)

    return pl.pallas_call(
        kernel,
        grid=(1,),
        in_specs=[whole_of(part) for part in came],
        out_specs=[pl.BlockSpec((rows, TILE), lambda i: (0, 0))] * 4,
        out_shape=[shape_of(rows, t) for t in (F32, BF16, BF16, BF16)],
        compiler_params=PARAMS,
        name="sort_x" if x_first else "sort_z",
    )(*came)


def total_of(parts, at):
    total = None
    for ref in parts:
        part = ref[TILE * at : TILE * (at + 1), :].astype(F32)
        total = part if total is None else total + part
    return total


def parent_kernel(*refs):
    first, second, (l_ref, m_ref) = refs[:4], refs[4:8], refs[8:]
    for n, (i, j) in enumerate(LOWER):
        parts, at = (first, n) if n < len(FIRST) else (second, n - len(FIRST))
        m_ref[j, TILE * i : TILE * (i + 1), :] = total_of(parts, at)
    add_ridge(m_ref)
    factor(m_ref, l_ref)


def parent(parts):
    return pl.pallas_call(
        parent_kernel,
        grid=(1,),
        in_specs=[whole_of(part) for part in parts],
        out_specs=pl.BlockSpec((SUPER, SUPER), lambda i: (0, 0)),
        out_shape=shape_of(SUPER, F32, SUPER),
        scratch_shapes=[pltpu.VMEM((4, SUPER, TILE), F32)],
        compiler_params=PARAMS,
        name="parent",
    )(*parts)


def shift(value, along_x, step):
    pairs = []
    for x in range(RING):
        for z in range(RING):
            to = ((x + step) % RING, z) if along_x else (x, (z + step) % RING)
            pairs.append((x * RING + z, to[0] * RING + to[1]))
    return lax.ppermute(value, "col", pairs)


def hand(value, dy, dc):
    pairs = [(y * 2 + c, (y + dy) % RING * 2 + (c ^ dc)) for y in range(RING) for c in range(2)]
    return lax.ppermute(value, "blk", pairs)


def gather(value, x_first):
    return [value] + [shift(value, x_first, s) for s in (1, 2, 3)]


def scatter(came, x_first):
    own, *sends = sort(x_first, came)
    return [own] + [shift(send, not x_first, s + 1) for s, send in enumerate(sends)]


def on_device(col_tiles, scales, positions, targets, parents):
    *blocks, give = place(col_tiles, scales, positions, targets)
    in1, keep = blocks[:8], blocks[8:]
    order = ((1, 0), (3, 0), (2, 0), (1, 1), (3, 1), (2, 1), (0, 1))
    for dy, dc in order:
        in1[2 * dy + dc] = hand(in1[2 * dy + dc], dy, dc)
    got = hand(give, 0, 1)
    pairs = [
        jnp.concatenate([keep[dy], got[BLOCK * dy : BLOCK * (dy + 1)]]) for dy in range(1, RING)
    ]
    landed = [in1[2 * dy + dc] for dy, dc in order[:6]]
    landed, pairs = lax.optimization_barrier((landed, pairs))
    for (dy, dc), value in zip(order[:6], landed):
        in1[2 * dy + dc] = value
    in2 = [hand(pairs[dy - 1], dy, 0) for dy in (1, 2, 3)]
    leaf_factor, inverse = leaf(in1)
    fronts = early(in1[:4], [keep[0], got[:BLOCK], in2[0]], inverse)
    leaf_panel, first, second = panel(parents, in1[4:], in2[1:], fronts, inverse)
    came = gather(first, True)
    came2 = gather(second, False)
    parent_factor = parent(scatter(came, True) + scatter(came2, False))
    return (leaf_factor[None], leaf_panel[None], parent_factor[None])


def solution(mesh):
    in_specs = (
        P(("col", "blk"), None, None, None),
        P(("col", "blk"), None),
        P(("col", "blk"), None),
        P(("col", "blk"), None),
        P("col", "blk"),
    )
    out_specs = (
        P(("col", "blk"), None, None),
        P(("col", "blk"), None, None),
        P(("col", "blk"), None, None),
    )
    return jax.shard_map(
        on_device, mesh=mesh, in_specs=in_specs, out_specs=out_specs, check_vma=False
    )
```

```python
import jax
import jax.numpy as jnp
from jax import lax
from jax.experimental import pallas as pl
from jax.experimental.pallas import tpu as pltpu
from jax.sharding import PartitionSpec as P

TILE = 128
SUPER = 512
RIDGE = 1.0
CAP = 4
CT_DEV = 16
RING = 4
PEERS = [(dy, dc) for dy in range(RING) for dc in range(2)]
TILES = CAP * 2 * TILE
BLOCK = TILES + 16
WIDTH = len(PEERS) * CAP * TILE
LOWER = [(i, j) for j in range(4) for i in range(j, 4)]
FIRST = LOWER[:5]
SECOND = LOWER[5:]

F32 = jnp.float32
BF16 = jnp.bfloat16
NT = (((1,), (1,)), ((), ()))
NN = (((1,), (0,)), ((), ()))

HBM = pl.BlockSpec(memory_space=pltpu.HBM)
ANY = pl.BlockSpec(memory_space=pl.ANY)
SMEM = pl.BlockSpec(memory_space=pltpu.SMEM)
PARAMS = pltpu.CompilerParams(vmem_limit_bytes=64 << 20)


def start_copies(sources, targets, sems, first=0):
    copies = []
    for n, (source, target) in enumerate(zip(sources, targets)):
        copies.append(pltpu.make_async_copy(source, target, sems.at[first + n]))
        copies[-1].start()
    return copies


def wait_all(copies):
    for copy in copies:
        copy.wait()


def buffers(arrays):
    return [pltpu.VMEM(array.shape, array.dtype) for array in arrays]


def dma(number):
    return pltpu.SemaphoreType.DMA((number,))


def shape_of(rows, dtype, columns=TILE):
    return jax.ShapeDtypeStruct((rows, columns), dtype)


def split(a):
    high = a.astype(BF16)
    return high, (a - high.astype(F32)).astype(BF16)


def dot3(a, b, dims=NT):
    x = jnp.concatenate([a[0], a[1], a[0]], axis=1)
    y = jnp.concatenate([b[0], b[0], b[1]], axis=1 if dims is NT else 0)
    return lax.dot_general(x, y, dims, preferred_element_type=F32)


def rows_of(pair, start, stop=None):
    return tuple(part[start:stop] for part in pair)


def on_top(pair):
    return tuple(jnp.concatenate([part, jnp.zeros_like(part)], axis=0) for part in pair)


def below(pair):
    return tuple(jnp.concatenate([jnp.zeros_like(part), part], axis=0) for part in pair)


def lane(v, j):
    return jnp.broadcast_to(v[:, j : j + 1], (8, TILE))


def sub(v, i):
    return jnp.broadcast_to(v[i : i + 1, :], (8, TILE))


def eliminate64(aug, base):
    w = [aug[8 * q : 8 * q + 8] for q in range(8)]
    out = []
    sid = lax.broadcasted_iota(jnp.int32, (8, TILE), 0)
    own = [lane(w[0], base + k) for k in range(8)]
    for p in range(8):
        at = base + 8 * p
        cols = [[lane(w[q], at + k) for k in range(8)] for q in range(p + 1, 8)]
        last = p == 7
        if not last:
            ahead = [lane(w[p + 1], at + 8 + k) for k in range(8)]
        rows = [sub(w[p], k) for k in range(8)]
        scale = None
        for k in range(8):
            if k % 2 == 0:
                a, b, c = sub(own[k], k), sub(own[k], k + 1), sub(own[k + 1], k + 1)
                r = lax.rsqrt(a)
                scale = lax.rsqrt(a * c - b * b) * (a * r)
            else:
                r = scale
            low = own[k] * r
            mult = [sub(low, i) if i > k else None for i in range(8)]
            for j in range(k + 1, 8):
                own[j] = own[j] - low * mult[j]
            rows[k] = rows[k] * r
            for i in range(k + 1, 8):
                rows[i] = rows[i] - mult[i] * rows[k]
            for q in range(p + 1, 8):
                col = cols[q - p - 1]
                lq = col[k] * r
                for j in range(k + 1, 8):
                    col[j] = col[j] - lq * mult[j]
                w[q] = w[q] - lq * rows[k]
                if q == p + 1:
                    for j in range(8):
                        ahead[j] = ahead[j] - lq * sub(lq, j)
        block = rows[0]
        for k in range(1, 8):
            block = jnp.where(sid == k, rows[k], block)
        out.append(block)
        if not last:
            own = ahead
    return jnp.concatenate(out, axis=0)


def trail(m_ref, kb, panels):
    for j in range(kb + 1, 4):
        s = TILE * (j - kb - 1)
        m_ref[j, TILE * j :, :] -= dot3(rows_of(panels, s), rows_of(panels, s, s + TILE))


def factor(m_ref, l_ref, x_ref=None, finished=lambda kb: None):
    col_id = lax.broadcasted_iota(jnp.int32, (64, TILE), 1)
    row_id = lax.broadcasted_iota(jnp.int32, (64, TILE), 0)
    eye = (col_id % 64 == row_id).astype(F32)
    left = col_id < 64
    lower = row_id >= col_id % 64
    zero = jnp.zeros((), F32)

    def keep_left(v):
        return jnp.where(lax.broadcasted_iota(jnp.int32, v.shape, 1) < 64, v, zero)

    def keep_right(v):
        return jnp.where(lax.broadcasted_iota(jnp.int32, v.shape, 1) < 64, zero, v)

    corner = pltpu.roll(m_ref[0, :64, :], 64, 1)
    for kb in range(4):
        o = TILE * kb
        if kb:
            l_ref[:o, o : o + TILE] = jnp.zeros((o, TILE), F32)
        corner_b = pltpu.roll(m_ref[kb, o + 64 : o + TILE, :], 64, 1)
        lhs = split(keep_left(m_ref[kb, o + 64 :, :]))
        w1 = eliminate64(jnp.where(left, eye, corner), 64)
        x1 = on_top(split(w1))
        l21 = dot3(rows_of(lhs, 0, 64), x1)
        l21s = split(l21)
        w2 = eliminate64(jnp.where(left, corner_b - dot3(l21s, on_top(l21s)), eye), 0)
        if kb < 3:
            pa = dot3(rows_of(lhs, 64), x1)
            pas = split(pa)
            rest = split(keep_right(m_ref[kb, o + TILE :, :] - dot3(pas, below(l21s))))
            x2 = below(split(w2))
            n = o + TILE
            pa_d = rows_of(pas, 0, 64)
            corner = pltpu.roll(m_ref[kb + 1, n : n + 64, :], 64, 1) - dot3(pa_d, below(pa_d))
            pb_d = dot3(rows_of(rest, 0, 64), x2)
            pb_ds = split(pb_d)
            corner = corner - dot3(pb_ds, below(pb_ds))
            pb = jnp.concatenate([pb_d, dot3(rows_of(rest, 64), x2)], axis=0)
            panel = pa + pb
            l_ref[n:, o:n] = panel
            trail(m_ref, kb, split(panel))
        flip = jnp.concatenate([w1, w2], axis=0).T
        l_ref[o : o + 64, o : o + TILE] = jnp.where(left & lower, flip[64:], zero)
        l_ref[o + 64 : o + TILE, o : o + TILE] = jnp.where(left, l21, jnp.where(lower, flip[:64], zero))
        if x_ref is not None:
            x1f = jnp.where(left, w1, zero)
            x2f = jnp.where(left, zero, w2)
            t = dot3(l21s, on_top(split(x1f)), NN)
            x21 = -dot3(split(x2f), below(split(t)), NN)
            x = jnp.concatenate([x1f, jnp.where(left, x21, x2f)], axis=0)
            x_ref[o : o + TILE, o : o + TILE] = x
            if kb < 3:
                x_ref[o : o + TILE, o + TILE :] = jnp.zeros((TILE, SUPER - TILE - o), F32)
            if kb:
                before = dot3(split(l_ref[o : o + TILE, :o]), split(x_ref[:o, :o]), NN)
                x_ref[o : o + TILE, :o] = -dot3(split(x), split(before), NN)
        finished(kb)


def place_kernel(target_ref, spot_ref, scale_ref, tile_ref, *refs):
    outs, (in_ref, block_ref, spots_ref, count_ref, in_sems, out_sems) = refs[:13], refs[13:]
    fetches = [tile_ref.at[:, 2 * half : 2 * half + 2] for half in range(2)]
    fetches = start_copies(fetches, [in_ref.at[half] for half in range(2)], in_sems)
    me = lax.axis_index("blk")
    for peer in range(len(PEERS)):
        count_ref[peer] = 0
    block_ref[...] = jnp.zeros(block_ref.shape, BF16)
    spots_ref[...] = jnp.zeros(spots_ref.shape, F32)
    places = []
    for t in range(CT_DEV):
        owner = target_ref[0, t]
        peer = lax.rem(owner // 2 - me // 2 + RING, RING) * 2 + lax.rem(owner + me, 2)
        rank = count_ref[peer]
        count_ref[peer] = rank + 1
        places.append((peer, rank))
        for k in range(4):
            spot = jnp.broadcast_to(spot_ref[k : k + 1, t : t + 1].astype(F32), (1, TILE))
            spots_ref[peer, pl.ds(4 * rank + k, 1), :] = spot
    pieces = [(out, 0, 0, peer) for peer, out in enumerate(outs[:8])]
    pieces += [(out, 0, 1, 2 * dy) for dy, out in enumerate(outs[8:12])]
    pieces += [(outs[12], BLOCK * dy, 1, 2 * dy + 1) for dy in range(RING)]
    stores = []
    for half in range(2):
        for peer in range(len(PEERS)):
            block_ref[half, peer, TILES:, :] = spots_ref[peer].astype(BF16)
        fetches[half].wait()
        for t, (peer, rank) in enumerate(places):
            root = jnp.sqrt(scale_ref[t : t + 1, :])
            for k in range(2):
                scaled = in_ref[half, t, k].astype(F32) * root
                at = pl.multiple_of((2 * rank + k) * TILE, TILE)
                block_ref[half, peer, pl.ds(at, TILE), :] = scaled.astype(BF16)
        for n, (out, o, of, peer) in enumerate(pieces):
            if of == half:
                target = out.at[o : o + BLOCK] if out.shape[0] > BLOCK else out
                stores += start_copies([block_ref.at[half, peer]], [target], out_sems, n)
    wait_all(stores)


def place(col_tiles, scales, positions, targets):
    blocks = [1] * 12 + [4]
    return pl.pallas_call(
        place_kernel,
        grid=(1,),
        in_specs=[
            SMEM,
            pl.BlockSpec((4, CT_DEV), lambda i: (0, 0)),
            pl.BlockSpec((CT_DEV, TILE), lambda i: (0, 0)),
            HBM,
        ],
        out_specs=[ANY] * len(blocks),
        out_shape=[shape_of(n * BLOCK, BF16) for n in blocks],
        scratch_shapes=[
            pltpu.VMEM((2, CT_DEV, 2, TILE, TILE), BF16),
            pltpu.VMEM((2, len(PEERS), BLOCK, TILE), BF16),
            pltpu.VMEM((len(PEERS), 16, TILE), F32),
            pltpu.SMEM((len(PEERS),), jnp.int32),
            dma(2),
            dma(16),
        ],
        compiler_params=PARAMS,
        name="place",
    )(targets.T, positions.T, scales, col_tiles)


def spread(refs, copies, s_ref, half):
    blocks = [(ref, o, copy) for ref, copy in zip(refs, copies) for o in range(0, ref.shape[0], BLOCK)]
    for n, (ref, o, copy) in enumerate(blocks):
        if o == 0:
            copy.wait()
        spots = ref[o + TILES : o + BLOCK, :].astype(F32)
        for slot in range(CAP):
            at = TILE * (n * CAP + slot)
            tiles = []
            for k in range(2):
                s = o + TILE * (2 * slot + k)
                tiles.append(ref[s : s + TILE, :].reshape(8, 16, TILE))
            row = 4 * slot + 2 * half
            picks = [jnp.broadcast_to(spots[row + k : row + k + 1, :], (16, TILE)) for k in range(2)]
            for i in range(4):
                total = None
                for tile, pick in zip(tiles, picks):
                    flag = jnp.where(pick == 4.0 * half + i, 1.0, 0.0).astype(BF16)
                    part = tile * flag[None]
                    total = part if total is None else total + part
                s_ref[TILE * i : TILE * (i + 1), at : at + TILE] = total.reshape(TILE, TILE)


def gram(s_ref, j):
    o = 256 * j
    return lax.dot_general(s_ref[o:, :], s_ref[o : o + 256, :], NT, preferred_element_type=F32)


def add_ridge(m_ref):
    row = lax.broadcasted_iota(jnp.int32, (TILE, TILE), 0)
    col = lax.broadcasted_iota(jnp.int32, (TILE, TILE), 1)
    ridge = jnp.where(row == col, jnp.float32(RIDGE), 0.0)
    for j in range(4):
        m_ref[j, TILE * j : TILE * (j + 1), :] += ridge


def leaf_kernel(*refs):
    blocks, (l_out, x_out), held = refs[:8], refs[8:10], refs[10:18]
    l_ref, x_ref, m_ref, s_ref, sems, out_sems = refs[18:]
    spread(held, start_copies(blocks, held, sems), s_ref, 0)
    for j in range(2):
        got = gram(s_ref, j)
        m_ref[2 * j, 256 * j :, :] = got[:, :TILE]
        m_ref[2 * j + 1, 256 * j :, :] = got[:, TILE:]
    add_ridge(m_ref)
    stores = []

    def finished(kb):
        strip = pl.ds(TILE * kb, TILE)
        sources = [l_ref.at[:, strip], x_ref.at[strip, :]]
        stores.extend(start_copies(sources, [l_out.at[:, strip], x_out.at[strip, :]], out_sems, 2 * kb))

    factor(m_ref, l_ref, x_ref, finished)
    wait_all(stores)


def leaf(blocks):
    return pl.pallas_call(
        leaf_kernel,
        in_specs=[HBM] * len(blocks),
        out_specs=[ANY] * 2,
        out_shape=[shape_of(SUPER, F32, SUPER)] * 2,
        scratch_shapes=buffers(blocks)
        + [
            pltpu.VMEM((SUPER, SUPER), F32),
            pltpu.VMEM((SUPER, SUPER), F32),
            pltpu.VMEM((4, SUPER, TILE), F32),
            pltpu.VMEM((SUPER, WIDTH), BF16),
            dma(8),
            dma(8),
        ],
        compiler_params=PARAMS,
        cost_estimate=pl.CostEstimate(flops=20 * 10**9, bytes_accessed=5 << 20, transcendentals=0),
        name="leaf",
    )(*blocks)


def early_kernel(after_ref, *refs):
    del after_ref
    blocks, (f_out, g_out), held = refs[:7], refs[7:9], refs[9:16]
    f_ref, g_ref, s1_ref, s2_ref, sems, out_sems = refs[16:]
    copies = start_copies(blocks, held, sems)
    spread(held[4:], copies[4:], s2_ref, 1)
    spread(held[:4], copies[:4], s1_ref, 0)
    f_ref[...] = lax.dot_general(s2_ref[...], s1_ref[...], NT, preferred_element_type=F32)
    stores = start_copies([f_ref], [f_out], out_sems)
    for j in range(2):
        g_ref[256 * j :, 256 * j : 256 * (j + 1)] = gram(s2_ref, j)
    wait_all(stores + start_copies([g_ref], [g_out], out_sems, 1))


def early(first, second, after):
    blocks = [*first, *second]
    return pl.pallas_call(
        early_kernel,
        in_specs=[ANY] + [HBM] * 7,
        out_specs=[ANY] * 2,
        out_shape=[shape_of(SUPER, F32, SUPER)] * 2,
        scratch_shapes=buffers(blocks)
        + [pltpu.VMEM((SUPER, SUPER), F32)] * 2
        + [pltpu.VMEM((SUPER, WIDTH // 2), BF16)] * 2
        + [dma(7), dma(2)],
        compiler_params=PARAMS,
        cost_estimate=pl.CostEstimate(flops=4 * 10**9, bytes_accessed=5 << 20, transcendentals=0),
        name="early",
    )(after, *blocks)


def panel_kernel(parent_ref, *refs):
    operands, (p_out, a_out, b_out), held = refs[:9], refs[9:12], refs[12:21]
    p_ref, a_ref, b_ref, s1_ref, s2_ref, sems, out_sems = refs[21:]
    copies = start_copies(operands, held, sems)
    f_ref, g_ref, x_ref = held[6:]
    spread(held[4:6], copies[4:6], s2_ref, 1)
    spread(held[:4], copies[:4], s1_ref, 0)
    late = lax.dot_general(s2_ref[...], s1_ref[...], NT, preferred_element_type=F32)
    wait_all(copies[6:])
    front = split(f_ref[...] + late)
    left = tuple(part[:, :256] for part in front)
    panels = [dot3(left, split(x_ref[:256, :256])), dot3(front, split(x_ref[256:, :]))]
    panel = jnp.concatenate(panels, axis=1)
    p_ref[...] = panel
    stores = start_copies([p_ref], [p_out], out_sems)
    whole = split(panel)
    for j in range(2):
        o = 256 * j
        update = g_ref[o:, o : o + 256] + gram(s2_ref, j)
        update = update - dot3(rows_of(whole, o), rows_of(whole, o, o + 256))
        for n, (row, col) in enumerate(LOWER):
            if col // 2 == j:
                out, at = (a_ref, n) if n < len(FIRST) else (b_ref, n - len(FIRST))
                r, c = TILE * row - o, TILE * col - o
                part = update[r : r + TILE, c : c + TILE]
                out[TILE * at : TILE * (at + 1), :] = part.astype(BF16)
    parent = jnp.full((16, TILE), parent_ref[0, 0].astype(F32)).astype(BF16)
    for out in (a_ref, b_ref):
        out[out.shape[0] - 16 :, :] = parent
    wait_all(stores + start_copies([a_ref, b_ref], [a_out, b_out], out_sems, 1))


def panel(parents, first, second, fronts, inverse):
    operands = [*first, *second, *fronts, inverse]
    outs = [
        shape_of(SUPER, F32, SUPER),
        shape_of(TILE * len(FIRST) + 16, BF16),
        shape_of(TILE * len(SECOND) + 16, BF16),
    ]
    return pl.pallas_call(
        panel_kernel,
        in_specs=[SMEM] + [HBM] * len(operands),
        out_specs=[ANY] * 3,
        out_shape=outs,
        scratch_shapes=buffers(operands)
        + buffers(outs)
        + [pltpu.VMEM((SUPER, WIDTH // 2), BF16)] * 2
        + [dma(len(operands)), dma(3)],
        compiler_params=PARAMS,
        name="panel",
    )(parents, *operands)


def sort_kernel(*refs):
    operands, outs, held, made = refs[:8], refs[8:16], refs[16:24], refs[24:32]
    sems, out_sems = refs[32:]
    c = lax.axis_index("col")
    x, z = c // RING, lax.rem(c, RING)
    copies = start_copies(operands, held, sems)
    stores = []
    for route in range(2):
        wait_all(copies[4 * route : 4 * route + 4])
        came, sums = held[4 * route : 4 * route + 4], made[4 * route : 4 * route + 4]
        rows = sums[0].shape[0]
        parents = [ref[rows:, :].astype(F32)[:8] for ref in came]
        flags = []
        for step in range(RING):
            if route == 0:
                wanted = x * RING + lax.rem(z + step, RING)
            else:
                wanted = lax.rem(x + step, RING) * RING + z
            wanted = wanted.astype(F32)
            flags.append([jnp.where(parent == wanted, 1.0, 0.0)[None] for parent in parents])
        for r in range(0, rows, TILE):
            parts = [ref[r : r + TILE, :].astype(F32).reshape(16, 8, TILE) for ref in came]
            for flag, out in zip(flags, sums):
                total = parts[0] * flag[0]
                for s in range(1, RING):
                    total = total + parts[s] * flag[s]
                out[r : r + TILE, :] = total.reshape(TILE, TILE).astype(out.dtype)
        stores += start_copies(sums, outs[4 * route : 4 * route + 4], out_sems, 4 * route)
    wait_all(stores)


def sort(came):
    rows = [TILE * len(part) for part in (FIRST, SECOND)]
    outs = [shape_of(n, t) for n in rows for t in (F32, BF16, BF16, BF16)]
    return pl.pallas_call(
        sort_kernel,
        in_specs=[HBM] * 8,
        out_specs=[ANY] * 8,
        out_shape=outs,
        scratch_shapes=buffers(came) + buffers(outs) + [dma(8), dma(8)],
        compiler_params=PARAMS,
        name="sort",
    )(*came)


def total_of(parts, at):
    total = None
    for ref in parts:
        part = ref[TILE * at : TILE * (at + 1), :].astype(F32)
        total = part if total is None else total + part
    return total


def parent_kernel(*refs):
    operands, l_out, held, (l_ref, m_ref, sems, out_sems) = refs[:8], refs[8], refs[9:17], refs[17:]
    wait_all(start_copies(operands, held, sems))
    first, second = held[:4], held[4:]
    for n, (i, j) in enumerate(LOWER):
        parts, at = (first, n) if n < len(FIRST) else (second, n - len(FIRST))
        m_ref[j, TILE * i : TILE * (i + 1), :] = total_of(parts, at)
    add_ridge(m_ref)
    stores = []

    def finished(kb):
        strip = pl.ds(TILE * kb, TILE)
        stores.extend(start_copies([l_ref.at[:, strip]], [l_out.at[:, strip]], out_sems, kb))

    factor(m_ref, l_ref, finished=finished)
    wait_all(stores)


def parent(parts):
    return pl.pallas_call(
        parent_kernel,
        in_specs=[HBM] * 8,
        out_specs=ANY,
        out_shape=shape_of(SUPER, F32, SUPER),
        scratch_shapes=buffers(parts)
        + [pltpu.VMEM((SUPER, SUPER), F32), pltpu.VMEM((4, SUPER, TILE), F32), dma(8), dma(4)],
        compiler_params=PARAMS,
        name="parent",
    )(*parts)


def shift(value, along_x, step):
    pairs = []
    for x in range(RING):
        for z in range(RING):
            to = ((x + step) % RING, z) if along_x else (x, (z + step) % RING)
            pairs.append((x * RING + z, to[0] * RING + to[1]))
    return lax.ppermute(value, "col", pairs)


def hand(value, dy, dc):
    pairs = [(y * 2 + c, (y + dy) % RING * 2 + (c ^ dc)) for y in range(RING) for c in range(2)]
    return lax.ppermute(value, "blk", pairs)


def gather(value, x_first):
    return [value] + [shift(value, x_first, s) for s in (1, 2, 3)]


def on_device(col_tiles, scales, positions, targets, parents):
    *blocks, give = place(col_tiles, scales, positions, targets)
    in1, keep = blocks[:8], blocks[8:]
    order = ((1, 0), (3, 0), (2, 0), (1, 1), (3, 1), (2, 1), (0, 1))
    for dy, dc in order:
        in1[2 * dy + dc] = hand(in1[2 * dy + dc], dy, dc)
    got = hand(give, 0, 1)
    pairs = [
        jnp.concatenate([keep[dy], got[BLOCK * dy : BLOCK * (dy + 1)]]) for dy in range(1, RING)
    ]
    landed = [in1[2 * dy + dc] for dy, dc in order[:6]]
    landed, pairs = lax.optimization_barrier((landed, pairs))
    for (dy, dc), value in zip(order[:6], landed):
        in1[2 * dy + dc] = value
    in2 = [hand(pairs[dy - 1], dy, 0) for dy in (1, 2, 3)]
    leaf_factor, inverse = leaf(in1)
    fronts = early(in1[:4], [keep[0], got[:BLOCK], in2[0]], inverse)
    leaf_panel, first, second = panel(parents, in1[4:], in2[1:], fronts, inverse)
    sums = list(sort(gather(first, True) + gather(second, False)))
    for n in (1, 2, 3):
        sums[n] = shift(sums[n], False, n)
        sums[4 + n] = shift(sums[4 + n], True, n)
    parent_factor = parent(sums)
    return (leaf_factor[None], leaf_panel[None], parent_factor[None])


def solution(mesh):
    in_specs = (
        P(("col", "blk"), None, None, None),
        P(("col", "blk"), None),
        P(("col", "blk"), None),
        P(("col", "blk"), None),
        P("col", "blk"),
    )
    out_specs = (
        P(("col", "blk"), None, None),
        P(("col", "blk"), None, None),
        P(("col", "blk"), None, None),
    )
    return jax.shard_map(
        on_device, mesh=mesh, in_specs=in_specs, out_specs=out_specs, check_vma=False
    )
```

```python
import jax
import jax.numpy as jnp
from jax import lax
from jax.experimental import pallas as pl
from jax.experimental.pallas import tpu as pltpu
from jax.sharding import PartitionSpec as P

TILE = 128
SUPER = 512
RIDGE = 1.0
CAP = 4
CT_DEV = 16
RING = 4
PEERS = [(dy, dc) for dy in range(RING) for dc in range(2)]
TILES = CAP * 2 * TILE
BLOCK = TILES + 16
WIDTH = len(PEERS) * CAP * TILE
ROUTES = (((0, 1), ((1, 0), (2, 0), (3, 0))), ((2, 3), ((2, 1), (3, 1), (3, 2))))
ROWS = 4 * TILE
MESSAGE = ROWS + 16

F32 = jnp.float32
BF16 = jnp.bfloat16
NT = (((1,), (1,)), ((), ()))
NN = (((1,), (0,)), ((), ()))

HBM = pl.BlockSpec(memory_space=pltpu.HBM)
ANY = pl.BlockSpec(memory_space=pl.ANY)
SMEM = pl.BlockSpec(memory_space=pltpu.SMEM)
PARAMS = pltpu.CompilerParams(vmem_limit_bytes=64 << 20)


def start_copies(sources, targets, sems, first=0):
    copies = []
    for n, (source, target) in enumerate(zip(sources, targets)):
        copies.append(pltpu.make_async_copy(source, target, sems.at[first + n]))
        copies[-1].start()
    return copies


def wait_all(copies):
    for copy in copies:
        copy.wait()


def buffers(arrays):
    return [pltpu.VMEM(array.shape, array.dtype) for array in arrays]


def dma(number):
    return pltpu.SemaphoreType.DMA((number,))


def shape_of(rows, dtype, columns=TILE):
    return jax.ShapeDtypeStruct((rows, columns), dtype)


def split(a):
    high = a.astype(BF16)
    return high, (a - high.astype(F32)).astype(BF16)


def dot3(a, b, dims=NT):
    x = jnp.concatenate([a[0], a[1], a[0]], axis=1)
    y = jnp.concatenate([b[0], b[0], b[1]], axis=1 if dims is NT else 0)
    return lax.dot_general(x, y, dims, preferred_element_type=F32)


def rows_of(pair, start, stop=None):
    return tuple(part[start:stop] for part in pair)


def on_top(pair):
    return tuple(jnp.concatenate([part, jnp.zeros_like(part)], axis=0) for part in pair)


def below(pair):
    return tuple(jnp.concatenate([jnp.zeros_like(part), part], axis=0) for part in pair)


def lane(v, j):
    return jnp.broadcast_to(v[:, j : j + 1], (8, TILE))


def sub(v, i):
    return jnp.broadcast_to(v[i : i + 1, :], (8, TILE))


def eliminate64(aug, base):
    w = [aug[8 * q : 8 * q + 8] for q in range(8)]
    out = []
    sid = lax.broadcasted_iota(jnp.int32, (8, TILE), 0)
    own = [lane(w[0], base + k) for k in range(8)]
    for p in range(8):
        at = base + 8 * p
        cols = [[lane(w[q], at + k) for k in range(8)] for q in range(p + 1, 8)]
        last = p == 7
        if not last:
            ahead = [lane(w[p + 1], at + 8 + k) for k in range(8)]
        rows = [sub(w[p], k) for k in range(8)]
        scale = None
        for k in range(8):
            if k % 2 == 0:
                a, b, c = sub(own[k], k), sub(own[k], k + 1), sub(own[k + 1], k + 1)
                r = lax.rsqrt(a)
                scale = lax.rsqrt(a * c - b * b) * (a * r)
            else:
                r = scale
            low = own[k] * r
            mult = [sub(low, i) if i > k else None for i in range(8)]
            for j in range(k + 1, 8):
                own[j] = own[j] - low * mult[j]
            rows[k] = rows[k] * r
            for i in range(k + 1, 8):
                rows[i] = rows[i] - mult[i] * rows[k]
            for q in range(p + 1, 8):
                col = cols[q - p - 1]
                lq = col[k] * r
                for j in range(k + 1, 8):
                    col[j] = col[j] - lq * mult[j]
                w[q] = w[q] - lq * rows[k]
                if q == p + 1:
                    for j in range(8):
                        ahead[j] = ahead[j] - lq * sub(lq, j)
        block = rows[0]
        for k in range(1, 8):
            block = jnp.where(sid == k, rows[k], block)
        out.append(block)
        if not last:
            own = ahead
    return jnp.concatenate(out, axis=0)


def trail(m_ref, kb, panels):
    for j in range(kb + 1, 4):
        s = TILE * (j - kb - 1)
        m_ref[j, TILE * j :, :] -= dot3(rows_of(panels, s), rows_of(panels, s, s + TILE))


def factor(m_ref, l_ref, x_ref=None, finished=lambda kb: None, steps=range(4)):
    col_id = lax.broadcasted_iota(jnp.int32, (64, TILE), 1)
    row_id = lax.broadcasted_iota(jnp.int32, (64, TILE), 0)
    eye = (col_id % 64 == row_id).astype(F32)
    left = col_id < 64
    lower = row_id >= col_id % 64
    zero = jnp.zeros((), F32)

    def keep_left(v):
        return jnp.where(lax.broadcasted_iota(jnp.int32, v.shape, 1) < 64, v, zero)

    def keep_right(v):
        return jnp.where(lax.broadcasted_iota(jnp.int32, v.shape, 1) < 64, zero, v)

    o = TILE * steps[0]
    corner = pltpu.roll(m_ref[steps[0], o : o + 64, :], 64, 1)
    for kb in steps:
        o = TILE * kb
        if kb:
            l_ref[:o, o : o + TILE] = jnp.zeros((o, TILE), F32)
        corner_b = pltpu.roll(m_ref[kb, o + 64 : o + TILE, :], 64, 1)
        lhs = split(keep_left(m_ref[kb, o + 64 :, :]))
        w1 = eliminate64(jnp.where(left, eye, corner), 64)
        x1 = on_top(split(w1))
        l21 = dot3(rows_of(lhs, 0, 64), x1)
        l21s = split(l21)
        w2 = eliminate64(jnp.where(left, corner_b - dot3(l21s, on_top(l21s)), eye), 0)
        if kb < 3:
            pa = dot3(rows_of(lhs, 64), x1)
            pas = split(pa)
            rest = split(keep_right(m_ref[kb, o + TILE :, :] - dot3(pas, below(l21s))))
            x2 = below(split(w2))
            n = o + TILE
            last = kb == steps[-1]
            pb_d = dot3(rows_of(rest, 0, 64), x2)
            if not last:
                pa_d, pb_ds = rows_of(pas, 0, 64), split(pb_d)
                corner = pltpu.roll(m_ref[kb + 1, n : n + 64, :], 64, 1) - dot3(pa_d, below(pa_d))
                corner = corner - dot3(pb_ds, below(pb_ds))
            pb = jnp.concatenate([pb_d, dot3(rows_of(rest, 64), x2)], axis=0)
            panel = pa + pb
            l_ref[n:, o:n] = panel
            if not last:
                trail(m_ref, kb, split(panel))
        flip = jnp.concatenate([w1, w2], axis=0).T
        l_ref[o : o + 64, o : o + TILE] = jnp.where(left & lower, flip[64:], zero)
        l_ref[o + 64 : o + TILE, o : o + TILE] = jnp.where(left, l21, jnp.where(lower, flip[:64], zero))
        if x_ref is not None:
            x1f = jnp.where(left, w1, zero)
            x2f = jnp.where(left, zero, w2)
            t = dot3(l21s, on_top(split(x1f)), NN)
            x21 = -dot3(split(x2f), below(split(t)), NN)
            x = jnp.concatenate([x1f, jnp.where(left, x21, x2f)], axis=0)
            x_ref[o : o + TILE, o : o + TILE] = x
            if kb < 3:
                x_ref[o : o + TILE, o + TILE :] = jnp.zeros((TILE, SUPER - TILE - o), F32)
            if kb:
                before = dot3(split(l_ref[o : o + TILE, :o]), split(x_ref[:o, :o]), NN)
                x_ref[o : o + TILE, :o] = -dot3(split(x), split(before), NN)
        finished(kb)


def place_kernel(target_ref, spot_ref, scale_ref, tile_ref, *refs):
    outs, (in_ref, block_ref, spots_ref, count_ref, in_sems, out_sems) = refs[:13], refs[13:]
    fetches = [tile_ref.at[:, 2 * half : 2 * half + 2] for half in range(2)]
    fetches = start_copies(fetches, [in_ref.at[half] for half in range(2)], in_sems)
    me = lax.axis_index("blk")
    for peer in range(len(PEERS)):
        count_ref[peer] = 0
    block_ref[...] = jnp.zeros(block_ref.shape, BF16)
    spots_ref[...] = jnp.zeros(spots_ref.shape, F32)
    places = []
    for t in range(CT_DEV):
        owner = target_ref[0, t]
        peer = lax.rem(owner // 2 - me // 2 + RING, RING) * 2 + lax.rem(owner + me, 2)
        rank = count_ref[peer]
        count_ref[peer] = rank + 1
        places.append((peer, rank))
        for k in range(4):
            spot = jnp.broadcast_to(spot_ref[k : k + 1, t : t + 1].astype(F32), (1, TILE))
            spots_ref[peer, pl.ds(4 * rank + k, 1), :] = spot
    pieces = [(out, 0, 0, peer) for peer, out in enumerate(outs[:8])]
    pieces += [(out, 0, 1, 2 * dy) for dy, out in enumerate(outs[8:12])]
    pieces += [(outs[12], BLOCK * dy, 1, 2 * dy + 1) for dy in range(RING)]
    stores = []
    for half in range(2):
        for peer in range(len(PEERS)):
            block_ref[half, peer, TILES:, :] = spots_ref[peer].astype(BF16)
        fetches[half].wait()
        for t, (peer, rank) in enumerate(places):
            root = jnp.sqrt(scale_ref[t : t + 1, :])
            for k in range(2):
                scaled = in_ref[half, t, k].astype(F32) * root
                at = pl.multiple_of((2 * rank + k) * TILE, TILE)
                block_ref[half, peer, pl.ds(at, TILE), :] = scaled.astype(BF16)
        for n, (out, o, of, peer) in enumerate(pieces):
            if of == half:
                target = out.at[o : o + BLOCK] if out.shape[0] > BLOCK else out
                stores += start_copies([block_ref.at[half, peer]], [target], out_sems, n)
    wait_all(stores)


def place(col_tiles, scales, positions, targets):
    blocks = [1] * 12 + [4]
    return pl.pallas_call(
        place_kernel,
        grid=(1,),
        in_specs=[
            SMEM,
            pl.BlockSpec((4, CT_DEV), lambda i: (0, 0)),
            pl.BlockSpec((CT_DEV, TILE), lambda i: (0, 0)),
            HBM,
        ],
        out_specs=[ANY] * len(blocks),
        out_shape=[shape_of(n * BLOCK, BF16) for n in blocks],
        scratch_shapes=[
            pltpu.VMEM((2, CT_DEV, 2, TILE, TILE), BF16),
            pltpu.VMEM((2, len(PEERS), BLOCK, TILE), BF16),
            pltpu.VMEM((len(PEERS), 16, TILE), F32),
            pltpu.SMEM((len(PEERS),), jnp.int32),
            dma(2),
            dma(16),
        ],
        compiler_params=PARAMS,
        name="place",
    )(targets.T, positions.T, scales, col_tiles)


def spread(refs, copies, s_ref, half):
    blocks = [(ref, o, copy) for ref, copy in zip(refs, copies) for o in range(0, ref.shape[0], BLOCK)]
    for n, (ref, o, copy) in enumerate(blocks):
        if o == 0:
            copy.wait()
        spots = ref[o + TILES : o + BLOCK, :].astype(F32)
        for slot in range(CAP):
            at = TILE * (n * CAP + slot)
            tiles = []
            for k in range(2):
                s = o + TILE * (2 * slot + k)
                tiles.append(ref[s : s + TILE, :].reshape(8, 16, TILE))
            row = 4 * slot + 2 * half
            picks = [jnp.broadcast_to(spots[row + k : row + k + 1, :], (16, TILE)) for k in range(2)]
            for i in range(4):
                total = None
                for tile, pick in zip(tiles, picks):
                    flag = jnp.where(pick == 4.0 * half + i, 1.0, 0.0).astype(BF16)
                    part = tile * flag[None]
                    total = part if total is None else total + part
                s_ref[TILE * i : TILE * (i + 1), at : at + TILE] = total.reshape(TILE, TILE)


def gram(s_ref, j):
    o = 256 * j
    return lax.dot_general(s_ref[o:, :], s_ref[o : o + 256, :], NT, preferred_element_type=F32)


def tile_ids():
    row = lax.broadcasted_iota(jnp.int32, (TILE, TILE), 0)
    return row, lax.broadcasted_iota(jnp.int32, (TILE, TILE), 1)


def add_ridge(m_ref, columns=range(4)):
    row, col = tile_ids()
    ridge = jnp.where(row == col, jnp.float32(RIDGE), 0.0)
    for j in columns:
        m_ref[j, TILE * j : TILE * (j + 1), :] += ridge


def leaf_kernel(*refs):
    blocks, (l_out, x_out), held = refs[:8], refs[8:10], refs[10:18]
    l_ref, x_ref, m_ref, s_ref, sems, out_sems = refs[18:]
    spread(held, start_copies(blocks, held, sems), s_ref, 0)
    for j in range(2):
        got = gram(s_ref, j)
        m_ref[2 * j, 256 * j :, :] = got[:, :TILE]
        m_ref[2 * j + 1, 256 * j :, :] = got[:, TILE:]
    add_ridge(m_ref)
    stores = []

    def finished(kb):
        strip = pl.ds(TILE * kb, TILE)
        sources = [l_ref.at[:, strip], x_ref.at[strip, :]]
        stores.extend(start_copies(sources, [l_out.at[:, strip], x_out.at[strip, :]], out_sems, 2 * kb))

    factor(m_ref, l_ref, x_ref, finished)
    wait_all(stores)


def leaf(blocks):
    return pl.pallas_call(
        leaf_kernel,
        in_specs=[HBM] * len(blocks),
        out_specs=[ANY] * 2,
        out_shape=[shape_of(SUPER, F32, SUPER)] * 2,
        scratch_shapes=buffers(blocks)
        + [
            pltpu.VMEM((SUPER, SUPER), F32),
            pltpu.VMEM((SUPER, SUPER), F32),
            pltpu.VMEM((4, SUPER, TILE), F32),
            pltpu.VMEM((SUPER, WIDTH), BF16),
            dma(8),
            dma(8),
        ],
        compiler_params=PARAMS,
        cost_estimate=pl.CostEstimate(flops=20 * 10**9, bytes_accessed=5 << 20, transcendentals=0),
        name="leaf",
    )(*blocks)


def early_kernel(after_ref, *refs):
    del after_ref
    blocks, (f_out, g_out), held = refs[:7], refs[7:9], refs[9:16]
    f_ref, g_ref, s1_ref, s2_ref, sems, out_sems = refs[16:]
    copies = start_copies(blocks, held, sems)
    spread(held[4:], copies[4:], s2_ref, 1)
    spread(held[:4], copies[:4], s1_ref, 0)
    f_ref[...] = lax.dot_general(s2_ref[...], s1_ref[...], NT, preferred_element_type=F32)
    stores = start_copies([f_ref], [f_out], out_sems)
    for j in range(2):
        g_ref[256 * j :, 256 * j : 256 * (j + 1)] = gram(s2_ref, j)
    wait_all(stores + start_copies([g_ref], [g_out], out_sems, 1))


def early(first, second, after):
    blocks = [*first, *second]
    return pl.pallas_call(
        early_kernel,
        in_specs=[ANY] + [HBM] * 7,
        out_specs=[ANY] * 2,
        out_shape=[shape_of(SUPER, F32, SUPER)] * 2,
        scratch_shapes=buffers(blocks)
        + [pltpu.VMEM((SUPER, SUPER), F32)] * 2
        + [pltpu.VMEM((SUPER, WIDTH // 2), BF16)] * 2
        + [dma(7), dma(2)],
        compiler_params=PARAMS,
        cost_estimate=pl.CostEstimate(flops=4 * 10**9, bytes_accessed=5 << 20, transcendentals=0),
        name="early",
    )(after, *blocks)


def panel_kernel(parent_ref, *refs):
    operands, (p_out, a_out, b_out), held = refs[:9], refs[9:12], refs[12:21]
    p_ref, a_ref, b_ref, s1_ref, s2_ref, sems, out_sems = refs[21:]
    copies = start_copies(operands, held, sems)
    f_ref, g_ref, x_ref = held[6:]
    spread(held[4:6], copies[4:6], s2_ref, 1)
    spread(held[:4], copies[:4], s1_ref, 0)
    late = lax.dot_general(s2_ref[...], s1_ref[...], NT, preferred_element_type=F32)
    wait_all(copies[6:])
    front = split(f_ref[...] + late)
    left = tuple(part[:, :256] for part in front)
    panels = [dot3(left, split(x_ref[:256, :256])), dot3(front, split(x_ref[256:, :]))]
    panel = jnp.concatenate(panels, axis=1)
    p_ref[...] = panel
    stores = start_copies([p_ref], [p_out], out_sems)
    whole = split(panel)
    tiles = {}
    for j in range(2):
        o = 256 * j
        update = g_ref[o:, o : o + 256] + gram(s2_ref, j)
        update = update - dot3(rows_of(whole, o), rows_of(whole, o, o + 256))
        for row in range(2 * j, 4):
            for col in range(2 * j, min(row, 2 * j + 1) + 1):
                r, c = TILE * row - o, TILE * col - o
                tiles[row, col] = update[r : r + TILE, c : c + TILE]
    row, col = tile_ids()
    parent = jnp.full((8, TILE), parent_ref[0, 0].astype(F32))
    for out, ((one, other), below_diagonal) in zip((a_ref, b_ref), ROUTES):
        one, other = tiles[one, one], tiles[other, other]
        out[:TILE, :] = jnp.where(row >= col, one, other).astype(BF16)
        for n, key in enumerate(below_diagonal):
            out[TILE * (n + 1) : TILE * (n + 2), :] = tiles[key].astype(BF16)
        diagonal = jnp.sum(jnp.where(row == col, other, 0.0), axis=0, keepdims=True)
        diagonal = jnp.broadcast_to(diagonal, (8, TILE))
        out[ROWS:, :] = jnp.concatenate([parent, diagonal], axis=0).astype(BF16)
    wait_all(stores + start_copies([a_ref, b_ref], [a_out, b_out], out_sems, 1))


def panel(parents, first, second, fronts, inverse):
    operands = [*first, *second, *fronts, inverse]
    outs = [
        shape_of(SUPER, F32, SUPER),
        shape_of(MESSAGE, BF16),
        shape_of(MESSAGE, BF16),
    ]
    return pl.pallas_call(
        panel_kernel,
        in_specs=[SMEM] + [HBM] * len(operands),
        out_specs=[ANY] * 3,
        out_shape=outs,
        scratch_shapes=buffers(operands)
        + buffers(outs)
        + [pltpu.VMEM((SUPER, WIDTH // 2), BF16)] * 2
        + [dma(len(operands)), dma(3)],
        compiler_params=PARAMS,
        name="panel",
    )(parents, *operands)


def sort_kernel(*refs):
    operands, outs, held, made = refs[:8], refs[8:16], refs[16:24], refs[24:32]
    sems, out_sems = refs[32:]
    c = lax.axis_index("col")
    x, z = c // RING, lax.rem(c, RING)
    copies = start_copies(operands, held, sems)
    stores = []
    for route in range(2):
        wait_all(copies[4 * route : 4 * route + 4])
        came, sums = held[4 * route : 4 * route + 4], made[4 * route : 4 * route + 4]
        tails = [ref[ROWS:, :].astype(F32) for ref in came]
        parents = [tail[:8] for tail in tails]
        flags = []
        for step in range(RING):
            if route == 0:
                wanted = x * RING + lax.rem(z + step, RING)
            else:
                wanted = lax.rem(x + step, RING) * RING + z
            wanted = wanted.astype(F32)
            flags.append([jnp.where(parent == wanted, 1.0, 0.0)[None] for parent in parents])
        for flag, out in zip(flags, sums):
            total = tails[0][8:] * flag[0][0]
            for s in range(1, RING):
                total = total + tails[s][8:] * flag[s][0]
            out[ROWS:, :] = jnp.concatenate([total, total], axis=0).astype(out.dtype)
        for r in range(0, ROWS, TILE):
            parts = [ref[r : r + TILE, :].astype(F32).reshape(16, 8, TILE) for ref in came]
            for flag, out in zip(flags, sums):
                total = parts[0] * flag[0]
                for s in range(1, RING):
                    total = total + parts[s] * flag[s]
                out[r : r + TILE, :] = total.reshape(TILE, TILE).astype(out.dtype)
        stores += start_copies(sums, outs[4 * route : 4 * route + 4], out_sems, 4 * route)
    wait_all(stores)


def sort(came):
    outs = [shape_of(MESSAGE, t) for t in (F32, BF16, BF16, BF16)] * 2
    return pl.pallas_call(
        sort_kernel,
        in_specs=[HBM] * 8,
        out_specs=[ANY] * 8,
        out_shape=outs,
        scratch_shapes=buffers(came) + buffers(outs) + [dma(8), dma(8)],
        compiler_params=PARAMS,
        name="sort",
    )(*came)


def total_of(parts, start, stop):
    total = None
    for ref in parts:
        part = ref[start:stop, :].astype(F32)
        total = part if total is None else total + part
    return total


def lower_tile(packed):
    row, col = tile_ids()
    return jnp.where(row >= col, packed, 0.0) + jnp.where(row > col, packed, 0.0).T


def upper_tile(packed, tail):
    row, col = tile_ids()
    upper = jnp.where(row < col, packed, 0.0)
    return upper + upper.T + jnp.where(row == col, jnp.broadcast_to(tail[:1], (TILE, TILE)), 0.0)


def start_kernel(*refs):
    operands, l_out, held, (l_ref, m_ref, sems, out_sems) = refs[:4], refs[4], refs[5:9], refs[9:]
    wait_all(start_copies(operands, held, sems))
    m_ref[0, :TILE, :] = lower_tile(total_of(held, 0, TILE))
    m_ref[0, TILE:, :] = total_of(held, TILE, ROWS)
    add_ridge(m_ref, (0,))
    factor(m_ref, l_ref, steps=(0,))
    wait_all(start_copies([l_ref], [l_out], out_sems))


def start(parts):
    return pl.pallas_call(
        start_kernel,
        in_specs=[HBM] * 4,
        out_specs=ANY,
        out_shape=shape_of(SUPER, F32),
        scratch_shapes=buffers(parts)
        + [pltpu.VMEM((SUPER, TILE), F32), pltpu.VMEM((1, SUPER, TILE), F32), dma(4), dma(1)],
        compiler_params=PARAMS,
        cost_estimate=pl.CostEstimate(flops=4 * 10**9, bytes_accessed=1 << 20, transcendentals=0),
        name="start",
    )(*parts)


def rest_kernel(*refs):
    operands, l_out, held, (l_ref, m_ref, sems, out_sems) = refs[:9], refs[9], refs[10:19], refs[19:]
    copies = start_copies(operands, held, sems)
    column, first, second = held[0], held[1:5], held[5:]
    wait_all(copies)
    l_ref[:, :TILE] = column[...]
    stores = start_copies([l_ref.at[:, pl.ds(0, TILE)]], [l_out.at[:, pl.ds(0, TILE)]], out_sems)
    for parts, ((_, other), below_diagonal) in zip((first, second), ROUTES):
        packed, tail = total_of(parts, 0, TILE), total_of(parts, ROWS, MESSAGE)
        m_ref[other, TILE * other : TILE * (other + 1), :] = upper_tile(packed, tail)
        if other == 3:
            m_ref[2, 2 * TILE : 3 * TILE, :] = lower_tile(packed)
            for n, (i, j) in enumerate(below_diagonal):
                got = total_of(parts, TILE * (n + 1), TILE * (n + 2))
                m_ref[j, TILE * i : TILE * (i + 1), :] = got
    add_ridge(m_ref, (1, 2, 3))
    trail(m_ref, 0, split(column[TILE:, :]))

    def finished(kb):
        strip = pl.ds(TILE * kb, TILE)
        stores.extend(start_copies([l_ref.at[:, strip]], [l_out.at[:, strip]], out_sems, kb))

    factor(m_ref, l_ref, finished=finished, steps=(1, 2, 3))
    wait_all(stores)


def rest(column, parts):
    operands = [column, *parts]
    return pl.pallas_call(
        rest_kernel,
        in_specs=[HBM] * 9,
        out_specs=ANY,
        out_shape=shape_of(SUPER, F32, SUPER),
        scratch_shapes=buffers(operands)
        + [pltpu.VMEM((SUPER, SUPER), F32), pltpu.VMEM((4, SUPER, TILE), F32), dma(9), dma(4)],
        compiler_params=PARAMS,
        name="rest",
    )(*operands)


def shift(value, along_x, step):
    pairs = []
    for x in range(RING):
        for z in range(RING):
            to = ((x + step) % RING, z) if along_x else (x, (z + step) % RING)
            pairs.append((x * RING + z, to[0] * RING + to[1]))
    return lax.ppermute(value, "col", pairs)


def hand(value, dy, dc):
    pairs = [(y * 2 + c, (y + dy) % RING * 2 + (c ^ dc)) for y in range(RING) for c in range(2)]
    return lax.ppermute(value, "blk", pairs)


def gather(value, x_first):
    return [value] + [shift(value, x_first, s) for s in (1, 2, 3)]


def on_device(col_tiles, scales, positions, targets, parents):
    *blocks, give = place(col_tiles, scales, positions, targets)
    in1, keep = blocks[:8], blocks[8:]
    order = ((2, 0), (2, 1), (1, 0), (3, 0), (1, 1), (3, 1), (0, 1))
    for dy, dc in order:
        in1[2 * dy + dc] = hand(in1[2 * dy + dc], dy, dc)
    got = hand(give, 0, 1)
    pairs = [
        jnp.concatenate([keep[dy], got[BLOCK * dy : BLOCK * (dy + 1)]]) for dy in range(1, RING)
    ]
    landed = [in1[2 * dy + dc] for dy, dc in order[:6]]
    landed, pairs = lax.optimization_barrier((landed, pairs))
    for (dy, dc), value in zip(order[:6], landed):
        in1[2 * dy + dc] = value
    in2 = [hand(pairs[dy - 1], dy, 0) for dy in (1, 2, 3)]
    leaf_factor, inverse = leaf(in1)
    fronts = early(in1[:4], [keep[0], got[:BLOCK], in2[0]], inverse)
    leaf_panel, first, second = panel(parents, in1[4:], in2[1:], fronts, inverse)
    sums = list(sort(gather(first, True) + gather(second, False)))
    for n in (1, 2, 3):
        sums[n] = shift(sums[n], False, n)
        sums[4 + n] = shift(sums[4 + n], True, n)
    parent_factor = rest(start(sums[:4]), sums)
    return (leaf_factor[None], leaf_panel[None], parent_factor[None])


def solution(mesh):
    in_specs = (
        P(("col", "blk"), None, None, None),
        P(("col", "blk"), None),
        P(("col", "blk"), None),
        P(("col", "blk"), None),
        P("col", "blk"),
    )
    out_specs = (
        P(("col", "blk"), None, None),
        P(("col", "blk"), None, None),
        P(("col", "blk"), None, None),
    )
    return jax.shard_map(
        on_device, mesh=mesh, in_specs=in_specs, out_specs=out_specs, check_vma=False
    )
```

```python
import jax
import jax.numpy as jnp
from jax import lax
from jax.experimental import pallas as pl
from jax.experimental.pallas import tpu as pltpu
from jax.sharding import PartitionSpec as P

TILE = 128
SUPER = 512
RIDGE = 1.0
CAP = 4
CT_DEV = 16
RING = 4
PEERS = [(dy, dc) for dy in range(RING) for dc in range(2)]
TILES = CAP * 2 * TILE
BLOCK = TILES + 16
WIDTH = len(PEERS) * CAP * TILE
ROUTES = (((0, 1), ((1, 0), (2, 0), (3, 0))), ((2, 3), ((2, 1), (3, 1), (3, 2))))
ROWS = 4 * TILE
MESSAGE = ROWS + 16

F32 = jnp.float32
BF16 = jnp.bfloat16
NT = (((1,), (1,)), ((), ()))
NN = (((1,), (0,)), ((), ()))

VMEM = pl.BlockSpec(memory_space=pltpu.VMEM)
ANY = pl.BlockSpec(memory_space=pl.ANY)
SMEM = pl.BlockSpec(memory_space=pltpu.SMEM)
PARAMS = pltpu.CompilerParams(vmem_limit_bytes=32 << 20)


def start_copies(sources, targets, sems, first=0):
    copies = []
    for n, (source, target) in enumerate(zip(sources, targets)):
        copies.append(pltpu.make_async_copy(source, target, sems.at[first + n]))
        copies[-1].start()
    return copies


def wait_all(copies):
    for copy in copies:
        copy.wait()


def dma(number):
    return pltpu.SemaphoreType.DMA((number,))


def shape_of(rows, dtype, columns=TILE):
    return jax.ShapeDtypeStruct((rows, columns), dtype)


def split(a):
    high = a.astype(BF16)
    return high, (a - high.astype(F32)).astype(BF16)


def dot3(a, b, dims=NT):
    x = jnp.concatenate([a[0], a[1], a[0]], axis=1)
    y = jnp.concatenate([b[0], b[0], b[1]], axis=1 if dims is NT else 0)
    return lax.dot_general(x, y, dims, preferred_element_type=F32)


def rows_of(pair, start, stop=None):
    return tuple(part[start:stop] for part in pair)


def on_top(pair):
    return tuple(jnp.concatenate([part, jnp.zeros_like(part)], axis=0) for part in pair)


def below(pair):
    return tuple(jnp.concatenate([jnp.zeros_like(part), part], axis=0) for part in pair)


def lane(v, j):
    return jnp.broadcast_to(v[:, j : j + 1], (8, TILE))


def sub(v, i):
    return jnp.broadcast_to(v[i : i + 1, :], (8, TILE))


def eliminate64(aug, base):
    w = [aug[8 * q : 8 * q + 8] for q in range(8)]
    out = []
    sid = lax.broadcasted_iota(jnp.int32, (8, TILE), 0)
    own = [lane(w[0], base + k) for k in range(8)]
    for p in range(8):
        at = base + 8 * p
        cols = [[lane(w[q], at + k) for k in range(8)] for q in range(p + 1, 8)]
        last = p == 7
        if not last:
            ahead = [lane(w[p + 1], at + 8 + k) for k in range(8)]
        rows = [sub(w[p], k) for k in range(8)]
        scale = None
        for k in range(8):
            if k % 2 == 0:
                a, b, c = sub(own[k], k), sub(own[k], k + 1), sub(own[k + 1], k + 1)
                r = lax.rsqrt(a)
                scale = lax.rsqrt(a * c - b * b) * (a * r)
            else:
                r = scale
            low = own[k] * r
            mult = [sub(low, i) if i > k else None for i in range(8)]
            for j in range(k + 1, 8):
                own[j] = own[j] - low * mult[j]
            rows[k] = rows[k] * r
            for i in range(k + 1, 8):
                rows[i] = rows[i] - mult[i] * rows[k]
            for q in range(p + 1, 8):
                col = cols[q - p - 1]
                lq = col[k] * r
                for j in range(k + 1, 8):
                    col[j] = col[j] - lq * mult[j]
                w[q] = w[q] - lq * rows[k]
                if q == p + 1:
                    for j in range(8):
                        ahead[j] = ahead[j] - lq * sub(lq, j)
        block = rows[0]
        for k in range(1, 8):
            block = jnp.where(sid == k, rows[k], block)
        out.append(block)
        if not last:
            own = ahead
    return jnp.concatenate(out, axis=0)


def trail(m_ref, kb, panels):
    for j in range(kb + 1, 4):
        s = TILE * (j - kb - 1)
        m_ref[j, TILE * j :, :] -= dot3(rows_of(panels, s), rows_of(panels, s, s + TILE))


def factor(m_ref, l_ref, x_ref=None, finished=lambda kb: None, steps=range(4)):
    col_id = lax.broadcasted_iota(jnp.int32, (64, TILE), 1)
    row_id = lax.broadcasted_iota(jnp.int32, (64, TILE), 0)
    eye = (col_id % 64 == row_id).astype(F32)
    left = col_id < 64
    lower = row_id >= col_id % 64
    zero = jnp.zeros((), F32)

    def keep_left(v):
        return jnp.where(lax.broadcasted_iota(jnp.int32, v.shape, 1) < 64, v, zero)

    def keep_right(v):
        return jnp.where(lax.broadcasted_iota(jnp.int32, v.shape, 1) < 64, zero, v)

    o = TILE * steps[0]
    corner = pltpu.roll(m_ref[steps[0], o : o + 64, :], 64, 1)
    for kb in steps:
        o = TILE * kb
        if kb:
            l_ref[:o, o : o + TILE] = jnp.zeros((o, TILE), F32)
        corner_b = pltpu.roll(m_ref[kb, o + 64 : o + TILE, :], 64, 1)
        lhs = split(keep_left(m_ref[kb, o + 64 :, :]))
        w1 = eliminate64(jnp.where(left, eye, corner), 64)
        x1 = on_top(split(w1))
        l21 = dot3(rows_of(lhs, 0, 64), x1)
        l21s = split(l21)
        w2 = eliminate64(jnp.where(left, corner_b - dot3(l21s, on_top(l21s)), eye), 0)
        if kb < 3:
            pa = dot3(rows_of(lhs, 64), x1)
            pas = split(pa)
            rest = split(keep_right(m_ref[kb, o + TILE :, :] - dot3(pas, below(l21s))))
            x2 = below(split(w2))
            n = o + TILE
            last = kb == steps[-1]
            pb_d = dot3(rows_of(rest, 0, 64), x2)
            if not last:
                pa_d, pb_ds = rows_of(pas, 0, 64), split(pb_d)
                corner = pltpu.roll(m_ref[kb + 1, n : n + 64, :], 64, 1) - dot3(pa_d, below(pa_d))
                corner = corner - dot3(pb_ds, below(pb_ds))
            pb = jnp.concatenate([pb_d, dot3(rows_of(rest, 64), x2)], axis=0)
            panel = pa + pb
            l_ref[n:, o:n] = panel
            if not last:
                trail(m_ref, kb, split(panel))
        flip = jnp.concatenate([w1, w2], axis=0).T
        l_ref[o : o + 64, o : o + TILE] = jnp.where(left & lower, flip[64:], zero)
        l_ref[o + 64 : o + TILE, o : o + TILE] = jnp.where(left, l21, jnp.where(lower, flip[:64], zero))
        if x_ref is not None:
            x1f = jnp.where(left, w1, zero)
            x2f = jnp.where(left, zero, w2)
            t = dot3(l21s, on_top(split(x1f)), NN)
            x21 = -dot3(split(x2f), below(split(t)), NN)
            x = jnp.concatenate([x1f, jnp.where(left, x21, x2f)], axis=0)
            x_ref[o : o + TILE, o : o + TILE] = x
            if kb < 3:
                x_ref[o : o + TILE, o + TILE :] = jnp.zeros((TILE, SUPER - TILE - o), F32)
            if kb:
                before = dot3(split(l_ref[o : o + TILE, :o]), split(x_ref[:o, :o]), NN)
                x_ref[o : o + TILE, :o] = -dot3(split(x), split(before), NN)
        finished(kb)


def place_kernel(target_ref, spot_ref, scale_ref, tile_ref, *refs):
    outs, (block_ref, spots_ref, count_ref) = refs[:13], refs[13:]
    me = lax.axis_index("blk")
    for peer in range(len(PEERS)):
        count_ref[peer] = 0
    block_ref[...] = jnp.zeros(block_ref.shape, BF16)
    spots_ref[...] = jnp.zeros(spots_ref.shape, F32)
    places = []
    for t in range(CT_DEV):
        owner = target_ref[0, t]
        peer = lax.rem(owner // 2 - me // 2 + RING, RING) * 2 + lax.rem(owner + me, 2)
        rank = count_ref[peer]
        count_ref[peer] = rank + 1
        places.append((peer, rank))
        for k in range(4):
            spot = jnp.broadcast_to(spot_ref[k : k + 1, t : t + 1].astype(F32), (1, TILE))
            spots_ref[peer, pl.ds(4 * rank + k, 1), :] = spot
    pieces = [(out, 0, 0, peer) for peer, out in enumerate(outs[:8])]
    pieces += [(out, 0, 1, 2 * dy) for dy, out in enumerate(outs[8:12])]
    pieces += [(outs[12], BLOCK * dy, 1, 2 * dy + 1) for dy in range(RING)]
    for half in range(2):
        for t, (peer, rank) in enumerate(places):
            root = jnp.sqrt(scale_ref[t : t + 1, :])
            for k in range(2):
                scaled = tile_ref[t, 2 * half + k].astype(F32) * root
                at = pl.multiple_of((2 * rank + k) * TILE, TILE)
                block_ref[half, peer, pl.ds(at, TILE), :] = scaled.astype(BF16)
        for out, o, of, peer in pieces:
            if of == half:
                out[o : o + TILES, :] = block_ref[half, peer]
                out[o + TILES : o + BLOCK, :] = spots_ref[peer].astype(BF16)


def place(col_tiles, scales, positions, targets):
    blocks = [1] * 12 + [4]
    return pl.pallas_call(
        place_kernel,
        in_specs=[SMEM, VMEM, VMEM, VMEM],
        out_specs=[VMEM] * len(blocks),
        out_shape=[shape_of(n * BLOCK, BF16) for n in blocks],
        scratch_shapes=[
            pltpu.VMEM((2, len(PEERS), TILES, TILE), BF16),
            pltpu.VMEM((len(PEERS), 16, TILE), F32),
            pltpu.SMEM((len(PEERS),), jnp.int32),
        ],
        compiler_params=PARAMS,
        name="place",
    )(targets.T, positions.T, scales, col_tiles)


def spread(refs, s_ref, half):
    blocks = [(ref, o) for ref in refs for o in range(0, ref.shape[0], BLOCK)]
    for n, (ref, o) in enumerate(blocks):
        spots = ref[o + TILES : o + BLOCK, :].astype(F32)
        for slot in range(CAP):
            at = TILE * (n * CAP + slot)
            tiles = []
            for k in range(2):
                s = o + TILE * (2 * slot + k)
                tiles.append(ref[s : s + TILE, :].reshape(8, 16, TILE))
            row = 4 * slot + 2 * half
            picks = [jnp.broadcast_to(spots[row + k : row + k + 1, :], (16, TILE)) for k in range(2)]
            for i in range(4):
                total = None
                for tile, pick in zip(tiles, picks):
                    flag = jnp.where(pick == 4.0 * half + i, 1.0, 0.0).astype(BF16)
                    part = tile * flag[None]
                    total = part if total is None else total + part
                s_ref[TILE * i : TILE * (i + 1), at : at + TILE] = total.reshape(TILE, TILE)


def gram(s_ref, j):
    o = 256 * j
    return lax.dot_general(s_ref[o:, :], s_ref[o : o + 256, :], NT, preferred_element_type=F32)


def tile_ids():
    row = lax.broadcasted_iota(jnp.int32, (TILE, TILE), 0)
    return row, lax.broadcasted_iota(jnp.int32, (TILE, TILE), 1)


def add_ridge(m_ref, columns=range(4)):
    row, col = tile_ids()
    ridge = jnp.where(row == col, jnp.float32(RIDGE), 0.0)
    for j in columns:
        m_ref[j, TILE * j : TILE * (j + 1), :] += ridge


def leaf_kernel(*refs):
    blocks, (l_out, x_ref, l_ref, m_ref, s_ref, out_sems) = refs[:8], refs[8:]
    spread(blocks, s_ref, 0)
    for j in range(2):
        got = gram(s_ref, j)
        m_ref[2 * j, 256 * j :, :] = got[:, :TILE]
        m_ref[2 * j + 1, 256 * j :, :] = got[:, TILE:]
    add_ridge(m_ref)
    stores = []

    def finished(kb):
        strip = pl.ds(TILE * kb, TILE)
        stores.extend(start_copies([l_ref.at[:, strip]], [l_out.at[:, strip]], out_sems, kb))

    factor(m_ref, l_ref, x_ref, finished)
    wait_all(stores)


def leaf(blocks):
    return pl.pallas_call(
        leaf_kernel,
        in_specs=[VMEM] * len(blocks),
        out_specs=[ANY, VMEM],
        out_shape=[shape_of(SUPER, F32, SUPER)] * 2,
        scratch_shapes=[
            pltpu.VMEM((SUPER, SUPER), F32),
            pltpu.VMEM((4, SUPER, TILE), F32),
            pltpu.VMEM((SUPER, WIDTH), BF16),
            dma(4),
        ],
        compiler_params=PARAMS,
        cost_estimate=pl.CostEstimate(flops=20 * 10**9, bytes_accessed=5 << 20, transcendentals=0),
        name="leaf",
    )(*blocks)


def early_kernel(after_ref, *refs):
    del after_ref
    blocks, (f_ref, g_ref, s1_ref, s2_ref) = refs[:7], refs[7:]
    spread(blocks[4:], s2_ref, 1)
    spread(blocks[:4], s1_ref, 0)
    f_ref[...] = lax.dot_general(s2_ref[...], s1_ref[...], NT, preferred_element_type=F32)
    for j in range(2):
        g_ref[256 * j :, 256 * j : 256 * (j + 1)] = gram(s2_ref, j)


def early(first, second, after):
    blocks = [*first, *second]
    return pl.pallas_call(
        early_kernel,
        in_specs=[ANY] + [VMEM] * 7,
        out_specs=[VMEM] * 2,
        out_shape=[shape_of(SUPER, F32, SUPER)] * 2,
        scratch_shapes=[pltpu.VMEM((SUPER, WIDTH // 2), BF16)] * 2,
        compiler_params=PARAMS,
        cost_estimate=pl.CostEstimate(flops=4 * 10**9, bytes_accessed=5 << 20, transcendentals=0),
        name="early",
    )(after, *blocks)


def panel_kernel(parent_ref, *refs):
    blocks, (f_ref, g_ref, x_ref, p_out, a_ref, b_ref) = refs[:6], refs[6:12]
    p_ref, s1_ref, s2_ref, out_sems = refs[12:]
    spread(blocks[4:], s2_ref, 1)
    spread(blocks[:4], s1_ref, 0)
    late = lax.dot_general(s2_ref[...], s1_ref[...], NT, preferred_element_type=F32)
    front = split(f_ref[...] + late)
    left = tuple(part[:, :256] for part in front)
    panels = [dot3(left, split(x_ref[:256, :256])), dot3(front, split(x_ref[256:, :]))]
    panel = jnp.concatenate(panels, axis=1)
    p_ref[...] = panel
    stores = start_copies([p_ref], [p_out], out_sems)
    whole = split(panel)
    tiles = {}
    for j in range(2):
        o = 256 * j
        update = g_ref[o:, o : o + 256] + gram(s2_ref, j)
        update = update - dot3(rows_of(whole, o), rows_of(whole, o, o + 256))
        for row in range(2 * j, 4):
            for col in range(2 * j, min(row, 2 * j + 1) + 1):
                r, c = TILE * row - o, TILE * col - o
                tiles[row, col] = update[r : r + TILE, c : c + TILE]
    row, col = tile_ids()
    parent = jnp.full((8, TILE), parent_ref[0, 0].astype(F32))
    for out, ((one, other), below_diagonal) in zip((a_ref, b_ref), ROUTES):
        one, other = tiles[one, one], tiles[other, other]
        out[:TILE, :] = jnp.where(row >= col, one, other).astype(BF16)
        for n, key in enumerate(below_diagonal):
            out[TILE * (n + 1) : TILE * (n + 2), :] = tiles[key].astype(BF16)
        diagonal = jnp.sum(jnp.where(row == col, other, 0.0), axis=0, keepdims=True)
        diagonal = jnp.broadcast_to(diagonal, (8, TILE))
        out[ROWS:, :] = jnp.concatenate([parent, diagonal], axis=0).astype(BF16)
    wait_all(stores)


def panel(parents, first, second, fronts, inverse):
    operands = [*first, *second, *fronts, inverse]
    outs = [shape_of(SUPER, F32, SUPER), shape_of(MESSAGE, BF16), shape_of(MESSAGE, BF16)]
    return pl.pallas_call(
        panel_kernel,
        in_specs=[SMEM] + [VMEM] * len(operands),
        out_specs=[ANY, VMEM, VMEM],
        out_shape=outs,
        scratch_shapes=[pltpu.VMEM((SUPER, SUPER), F32)]
        + [pltpu.VMEM((SUPER, WIDTH // 2), BF16)] * 2
        + [dma(1)],
        compiler_params=PARAMS,
        name="panel",
    )(parents, *operands)


def sort_kernel(*refs):
    held, made = refs[:8], refs[8:]
    c = lax.axis_index("col")
    x, z = c // RING, lax.rem(c, RING)
    for route in range(2):
        came, sums = held[4 * route : 4 * route + 4], made[4 * route : 4 * route + 4]
        tails = [ref[ROWS:, :].astype(F32) for ref in came]
        parents = [tail[:8] for tail in tails]
        flags = []
        for step in range(RING):
            if route == 0:
                wanted = x * RING + lax.rem(z + step, RING)
            else:
                wanted = lax.rem(x + step, RING) * RING + z
            wanted = wanted.astype(F32)
            flags.append([jnp.where(parent == wanted, 1.0, 0.0)[None] for parent in parents])
        for flag, out in zip(flags, sums):
            total = tails[0][8:] * flag[0][0]
            for s in range(1, RING):
                total = total + tails[s][8:] * flag[s][0]
            out[ROWS:, :] = jnp.concatenate([total, total], axis=0).astype(out.dtype)
        for r in range(0, ROWS, TILE):
            parts = [ref[r : r + TILE, :].astype(F32).reshape(16, 8, TILE) for ref in came]
            for flag, out in zip(flags, sums):
                total = parts[0] * flag[0]
                for s in range(1, RING):
                    total = total + parts[s] * flag[s]
                out[r : r + TILE, :] = total.reshape(TILE, TILE).astype(out.dtype)


def sort(came):
    outs = [shape_of(MESSAGE, t) for t in (F32, BF16, BF16, BF16)] * 2
    return pl.pallas_call(
        sort_kernel,
        in_specs=[VMEM] * 8,
        out_specs=[VMEM] * 8,
        out_shape=outs,
        compiler_params=PARAMS,
        name="sort",
    )(*came)


def total_of(parts, start, stop):
    total = None
    for ref in parts:
        part = ref[start:stop, :].astype(F32)
        total = part if total is None else total + part
    return total


def lower_tile(packed):
    row, col = tile_ids()
    return jnp.where(row >= col, packed, 0.0) + jnp.where(row > col, packed, 0.0).T


def upper_tile(packed, tail):
    row, col = tile_ids()
    upper = jnp.where(row < col, packed, 0.0)
    return upper + upper.T + jnp.where(row == col, jnp.broadcast_to(tail[:1], (TILE, TILE)), 0.0)


def start_kernel(*refs):
    held, (l_ref, m_ref) = refs[:4], refs[4:]
    m_ref[0, :TILE, :] = lower_tile(total_of(held, 0, TILE))
    m_ref[0, TILE:, :] = total_of(held, TILE, ROWS)
    add_ridge(m_ref, (0,))
    factor(m_ref, l_ref, steps=(0,))


def start(parts):
    return pl.pallas_call(
        start_kernel,
        in_specs=[VMEM] * 4,
        out_specs=VMEM,
        out_shape=shape_of(SUPER, F32),
        scratch_shapes=[pltpu.VMEM((1, SUPER, TILE), F32)],
        compiler_params=PARAMS,
        cost_estimate=pl.CostEstimate(flops=4 * 10**9, bytes_accessed=1 << 20, transcendentals=0),
        name="start",
    )(*parts)


def rest_kernel(*refs):
    column, first, second, (l_out, l_ref, m_ref, out_sems) = refs[0], refs[1:5], refs[5:9], refs[9:]
    l_ref[:, :TILE] = column[...]
    stores = start_copies([l_ref.at[:, pl.ds(0, TILE)]], [l_out.at[:, pl.ds(0, TILE)]], out_sems)
    for parts, ((_, other), below_diagonal) in zip((first, second), ROUTES):
        packed, tail = total_of(parts, 0, TILE), total_of(parts, ROWS, MESSAGE)
        m_ref[other, TILE * other : TILE * (other + 1), :] = upper_tile(packed, tail)
        if other == 3:
            m_ref[2, 2 * TILE : 3 * TILE, :] = lower_tile(packed)
            for n, (i, j) in enumerate(below_diagonal):
                got = total_of(parts, TILE * (n + 1), TILE * (n + 2))
                m_ref[j, TILE * i : TILE * (i + 1), :] = got
    add_ridge(m_ref, (1, 2, 3))
    trail(m_ref, 0, split(column[TILE:, :]))

    def finished(kb):
        strip = pl.ds(TILE * kb, TILE)
        stores.extend(start_copies([l_ref.at[:, strip]], [l_out.at[:, strip]], out_sems, kb))

    factor(m_ref, l_ref, finished=finished, steps=(1, 2, 3))
    wait_all(stores)


def rest(column, parts):
    operands = [column, *parts]
    return pl.pallas_call(
        rest_kernel,
        in_specs=[VMEM] * 9,
        out_specs=ANY,
        out_shape=shape_of(SUPER, F32, SUPER),
        scratch_shapes=[pltpu.VMEM((SUPER, SUPER), F32), pltpu.VMEM((4, SUPER, TILE), F32), dma(4)],
        compiler_params=PARAMS,
        name="rest",
    )(*operands)


def shift(value, along_x, step):
    pairs = []
    for x in range(RING):
        for z in range(RING):
            to = ((x + step) % RING, z) if along_x else (x, (z + step) % RING)
            pairs.append((x * RING + z, to[0] * RING + to[1]))
    return lax.ppermute(value, "col", pairs)


def hand(value, dy, dc):
    pairs = [(y * 2 + c, (y + dy) % RING * 2 + (c ^ dc)) for y in range(RING) for c in range(2)]
    return lax.ppermute(value, "blk", pairs)


def gather(value, x_first):
    return [value] + [shift(value, x_first, s) for s in (1, 2, 3)]


def on_device(col_tiles, scales, positions, targets, parents):
    *blocks, give = place(col_tiles, scales, positions, targets)
    in1, keep = blocks[:8], blocks[8:]
    order = ((2, 0), (2, 1), (1, 0), (3, 0), (1, 1), (3, 1), (0, 1))
    for dy, dc in order:
        in1[2 * dy + dc] = hand(in1[2 * dy + dc], dy, dc)
    got = hand(give, 0, 1)
    pairs = [
        jnp.concatenate([keep[dy], got[BLOCK * dy : BLOCK * (dy + 1)]]) for dy in range(1, RING)
    ]
    landed = [in1[2 * dy + dc] for dy, dc in order[:6]]
    landed, pairs = lax.optimization_barrier((landed, pairs))
    for (dy, dc), value in zip(order[:6], landed):
        in1[2 * dy + dc] = value
    in2 = [hand(pairs[dy - 1], dy, 0) for dy in (1, 2, 3)]
    leaf_factor, inverse = leaf(in1)
    fronts = early(in1[:4], [keep[0], got[:BLOCK], in2[0]], inverse)
    leaf_panel, first, second = panel(parents, in1[4:], in2[1:], fronts, inverse)
    sums = list(sort(gather(first, True) + gather(second, False)))
    for n in (1, 2, 3):
        sums[n] = shift(sums[n], False, n)
        sums[4 + n] = shift(sums[4 + n], True, n)
    parent_factor = rest(start(sums[:4]), sums)
    return (leaf_factor[None], leaf_panel[None], parent_factor[None])


def solution(mesh):
    in_specs = (
        P(("col", "blk"), None, None, None),
        P(("col", "blk"), None),
        P(("col", "blk"), None),
        P(("col", "blk"), None),
        P("col", "blk"),
    )
    out_specs = (
        P(("col", "blk"), None, None),
        P(("col", "blk"), None, None),
        P(("col", "blk"), None, None),
    )
    return jax.shard_map(
        on_device, mesh=mesh, in_specs=in_specs, out_specs=out_specs, check_vma=False
    )
```

```python
import jax
import jax.numpy as jnp
from jax import lax
from jax.experimental import pallas as pl
from jax.experimental.pallas import tpu as pltpu
from jax.sharding import PartitionSpec as P

TILE = 128
SUPER = 512
RIDGE = 1.0
CAP = 4
CT_DEV = 16
RING = 4
PEERS = [(dy, dc) for dy in range(RING) for dc in range(2)]
TILES = CAP * 2 * TILE
BLOCK = TILES + 16
WIDTH = len(PEERS) * CAP * TILE
ROUTES = (((0, 1), ((1, 0), (2, 0), (3, 0))), ((2, 3), ((2, 1), (3, 1), (3, 2))))
ROWS = 4 * TILE
MESSAGE = ROWS + 16

F32 = jnp.float32
BF16 = jnp.bfloat16
NT = (((1,), (1,)), ((), ()))
NN = (((1,), (0,)), ((), ()))

VMEM = pl.BlockSpec(memory_space=pltpu.VMEM)
ANY = pl.BlockSpec(memory_space=pl.ANY)
SMEM = pl.BlockSpec(memory_space=pltpu.SMEM)
PARAMS = pltpu.CompilerParams(vmem_limit_bytes=32 << 20)


def start_copies(sources, targets, sems, first=0):
    copies = []
    for n, (source, target) in enumerate(zip(sources, targets)):
        copies.append(pltpu.make_async_copy(source, target, sems.at[first + n]))
        copies[-1].start()
    return copies


def wait_all(copies):
    for copy in copies:
        copy.wait()


def dma(number):
    return pltpu.SemaphoreType.DMA((number,))


def shape_of(rows, dtype, columns=TILE):
    return jax.ShapeDtypeStruct((rows, columns), dtype)


def split(a):
    high = a.astype(BF16)
    return high, (a - high.astype(F32)).astype(BF16)


def dot3(a, b, dims=NT):
    x = jnp.concatenate([a[0], a[1], a[0]], axis=1)
    y = jnp.concatenate([b[0], b[0], b[1]], axis=1 if dims is NT else 0)
    return lax.dot_general(x, y, dims, preferred_element_type=F32)


def rows_of(pair, start, stop=None):
    return tuple(part[start:stop] for part in pair)


def on_top(pair):
    return tuple(jnp.concatenate([part, jnp.zeros_like(part)], axis=0) for part in pair)


def below(pair):
    return tuple(jnp.concatenate([jnp.zeros_like(part), part], axis=0) for part in pair)


def lane(v, j):
    return jnp.broadcast_to(v[:, j : j + 1], (8, TILE))


def sub(v, i):
    return jnp.broadcast_to(v[i : i + 1, :], (8, TILE))


def eliminate64(aug, base):
    w = [aug[8 * q : 8 * q + 8] for q in range(8)]
    out = []
    sid = lax.broadcasted_iota(jnp.int32, (8, TILE), 0)
    own = [lane(w[0], base + k) for k in range(8)]
    for p in range(8):
        at = base + 8 * p
        cols = [[lane(w[q], at + k) for k in range(8)] for q in range(p + 1, 8)]
        last = p == 7
        if not last:
            ahead = [lane(w[p + 1], at + 8 + k) for k in range(8)]
        rows = [sub(w[p], k) for k in range(8)]
        scale = None
        for k in range(8):
            if k % 2 == 0:
                a, b, c = sub(own[k], k), sub(own[k], k + 1), sub(own[k + 1], k + 1)
                r = lax.rsqrt(a)
                scale = lax.rsqrt(a * c - b * b) * (a * r)
            else:
                r = scale
            low = own[k] * r
            mult = [sub(low, i) if i > k else None for i in range(8)]
            for j in range(k + 1, 8):
                own[j] = own[j] - low * mult[j]
            rows[k] = rows[k] * r
            for i in range(k + 1, 8):
                rows[i] = rows[i] - mult[i] * rows[k]
            for q in range(p + 1, 8):
                col = cols[q - p - 1]
                lq = col[k] * r
                for j in range(k + 1, 8):
                    col[j] = col[j] - lq * mult[j]
                w[q] = w[q] - lq * rows[k]
                if q == p + 1:
                    for j in range(8):
                        ahead[j] = ahead[j] - lq * sub(lq, j)
        block = rows[0]
        for k in range(1, 8):
            block = jnp.where(sid == k, rows[k], block)
        out.append(block)
        if not last:
            own = ahead
    return jnp.concatenate(out, axis=0)


def trail(m_ref, kb, panels):
    for j in range(kb + 1, 4):
        s = TILE * (j - kb - 1)
        m_ref[j, TILE * j :, :] -= dot3(rows_of(panels, s), rows_of(panels, s, s + TILE))


def factor(m_ref, l_ref, x_ref=None, finished=lambda kb: None, steps=range(4)):
    col_id = lax.broadcasted_iota(jnp.int32, (64, TILE), 1)
    row_id = lax.broadcasted_iota(jnp.int32, (64, TILE), 0)
    eye = (col_id % 64 == row_id).astype(F32)
    left = col_id < 64
    lower = row_id >= col_id % 64
    zero = jnp.zeros((), F32)

    def keep_left(v):
        return jnp.where(lax.broadcasted_iota(jnp.int32, v.shape, 1) < 64, v, zero)

    def keep_right(v):
        return jnp.where(lax.broadcasted_iota(jnp.int32, v.shape, 1) < 64, zero, v)

    o = TILE * steps[0]
    corner = pltpu.roll(m_ref[steps[0], o : o + 64, :], 64, 1)
    for kb in steps:
        o = TILE * kb
        if kb:
            l_ref[:o, o : o + TILE] = jnp.zeros((o, TILE), F32)
        corner_b = pltpu.roll(m_ref[kb, o + 64 : o + TILE, :], 64, 1)
        lhs = split(keep_left(m_ref[kb, o + 64 :, :]))
        w1 = eliminate64(jnp.where(left, eye, corner), 64)
        x1 = on_top(split(w1))
        l21 = dot3(rows_of(lhs, 0, 64), x1)
        l21s = split(l21)
        w2 = eliminate64(jnp.where(left, corner_b - dot3(l21s, on_top(l21s)), eye), 0)
        if kb < 3:
            pa = dot3(rows_of(lhs, 64), x1)
            pas = split(pa)
            rest = split(keep_right(m_ref[kb, o + TILE :, :] - dot3(pas, below(l21s))))
            x2 = below(split(w2))
            n = o + TILE
            last = kb == steps[-1]
            pb_d = dot3(rows_of(rest, 0, 64), x2)
            if not last:
                pa_d, pb_ds = rows_of(pas, 0, 64), split(pb_d)
                corner = pltpu.roll(m_ref[kb + 1, n : n + 64, :], 64, 1) - dot3(pa_d, below(pa_d))
                corner = corner - dot3(pb_ds, below(pb_ds))
            pb = jnp.concatenate([pb_d, dot3(rows_of(rest, 64), x2)], axis=0)
            panel = pa + pb
            l_ref[n:, o:n] = panel
            if not last:
                trail(m_ref, kb, split(panel))
        flip = jnp.concatenate([w1, w2], axis=0).T
        l_ref[o : o + 64, o : o + TILE] = jnp.where(left & lower, flip[64:], zero)
        l_ref[o + 64 : o + TILE, o : o + TILE] = jnp.where(left, l21, jnp.where(lower, flip[:64], zero))
        if x_ref is not None:
            x1f = jnp.where(left, w1, zero)
            x2f = jnp.where(left, zero, w2)
            t = dot3(l21s, on_top(split(x1f)), NN)
            x21 = -dot3(split(x2f), below(split(t)), NN)
            x = jnp.concatenate([x1f, jnp.where(left, x21, x2f)], axis=0)
            x_ref[o : o + TILE, o : o + TILE] = x
            if kb < 3:
                x_ref[o : o + TILE, o + TILE :] = jnp.zeros((TILE, SUPER - TILE - o), F32)
            if kb:
                before = dot3(split(l_ref[o : o + TILE, :o]), split(x_ref[:o, :o]), NN)
                x_ref[o : o + TILE, :o] = -dot3(split(x), split(before), NN)
        finished(kb)


def place_kernel(target_ref, spot_ref, scale_ref, tile_ref, *refs):
    outs, (block_ref, spots_ref, count_ref) = refs[:13], refs[13:]
    me = lax.axis_index("blk")
    for peer in range(len(PEERS)):
        count_ref[peer] = 0
    block_ref[...] = jnp.zeros(block_ref.shape, BF16)
    spots_ref[...] = jnp.zeros(spots_ref.shape, F32)
    places = []
    for t in range(CT_DEV):
        owner = target_ref[0, t]
        peer = lax.rem(owner // 2 - me // 2 + RING, RING) * 2 + lax.rem(owner + me, 2)
        rank = count_ref[peer]
        count_ref[peer] = rank + 1
        places.append((peer, rank))
        for k in range(4):
            spot = jnp.broadcast_to(spot_ref[k : k + 1, t : t + 1].astype(F32), (1, TILE))
            spots_ref[peer, pl.ds(4 * rank + k, 1), :] = spot
    pieces = [(out, 0, 0, peer) for peer, out in enumerate(outs[:8])]
    pieces += [(out, 0, 1, 2 * dy) for dy, out in enumerate(outs[8:12])]
    pieces += [(outs[12], BLOCK * dy, 1, 2 * dy + 1) for dy in range(RING)]
    for half in range(2):
        for t, (peer, rank) in enumerate(places):
            root = jnp.sqrt(scale_ref[t : t + 1, :])
            for k in range(2):
                scaled = tile_ref[t, 2 * half + k].astype(F32) * root
                at = pl.multiple_of((2 * rank + k) * TILE, TILE)
                block_ref[half, peer, pl.ds(at, TILE), :] = scaled.astype(BF16)
        for out, o, of, peer in pieces:
            if of == half:
                out[o : o + TILES, :] = block_ref[half, peer]
                out[o + TILES : o + BLOCK, :] = spots_ref[peer].astype(BF16)


def place(col_tiles, scales, positions, targets):
    blocks = [1] * 12 + [4]
    return pl.pallas_call(
        place_kernel,
        in_specs=[SMEM, VMEM, VMEM, VMEM],
        out_specs=[VMEM] * len(blocks),
        out_shape=[shape_of(n * BLOCK, BF16) for n in blocks],
        scratch_shapes=[
            pltpu.VMEM((2, len(PEERS), TILES, TILE), BF16),
            pltpu.VMEM((len(PEERS), 16, TILE), F32),
            pltpu.SMEM((len(PEERS),), jnp.int32),
        ],
        compiler_params=PARAMS,
        name="place",
    )(targets.T, positions.T, scales, col_tiles)


def spread(refs, s_ref, half):
    blocks = [(ref, o) for ref in refs for o in range(0, ref.shape[0], BLOCK)]
    for n, (ref, o) in enumerate(blocks):
        spots = ref[o + TILES : o + BLOCK, :].astype(F32)
        for slot in range(CAP):
            at = TILE * (n * CAP + slot)
            tiles = []
            for k in range(2):
                s = o + TILE * (2 * slot + k)
                tiles.append(ref[s : s + TILE, :].reshape(8, 16, TILE))
            row = 4 * slot + 2 * half
            picks = [jnp.broadcast_to(spots[row + k : row + k + 1, :], (16, TILE)) for k in range(2)]
            for i in range(4):
                total = None
                for tile, pick in zip(tiles, picks):
                    flag = jnp.where(pick == 4.0 * half + i, 1.0, 0.0).astype(BF16)
                    part = tile * flag[None]
                    total = part if total is None else total + part
                s_ref[TILE * i : TILE * (i + 1), at : at + TILE] = total.reshape(TILE, TILE)


def gram(s_ref, j):
    o = 256 * j
    return lax.dot_general(s_ref[o:, :], s_ref[o : o + 256, :], NT, preferred_element_type=F32)


def tile_ids():
    row = lax.broadcasted_iota(jnp.int32, (TILE, TILE), 0)
    return row, lax.broadcasted_iota(jnp.int32, (TILE, TILE), 1)


def add_ridge(m_ref, columns=range(4)):
    row, col = tile_ids()
    ridge = jnp.where(row == col, jnp.float32(RIDGE), 0.0)
    for j in columns:
        m_ref[j, TILE * j : TILE * (j + 1), :] += ridge


def leaf_kernel(*refs):
    blocks, (l_out, x_ref, l_ref, m_ref, s_ref, out_sems) = refs[:8], refs[8:]
    spread(blocks, s_ref, 0)
    for j in range(2):
        got = gram(s_ref, j)
        m_ref[2 * j, 256 * j :, :] = got[:, :TILE]
        m_ref[2 * j + 1, 256 * j :, :] = got[:, TILE:]
    add_ridge(m_ref)
    stores = []

    def finished(kb):
        strip = pl.ds(TILE * kb, TILE)
        stores.extend(start_copies([l_ref.at[:, strip]], [l_out.at[:, strip]], out_sems, kb))

    factor(m_ref, l_ref, x_ref, finished)
    wait_all(stores)


def leaf(blocks):
    return pl.pallas_call(
        leaf_kernel,
        in_specs=[VMEM] * len(blocks),
        out_specs=[ANY, VMEM],
        out_shape=[shape_of(SUPER, F32, SUPER)] * 2,
        scratch_shapes=[
            pltpu.VMEM((SUPER, SUPER), F32),
            pltpu.VMEM((4, SUPER, TILE), F32),
            pltpu.VMEM((SUPER, WIDTH), BF16),
            dma(4),
        ],
        compiler_params=PARAMS,
        cost_estimate=pl.CostEstimate(flops=20 * 10**9, bytes_accessed=5 << 20, transcendentals=0),
        name="leaf",
    )(*blocks)


def early_kernel(after_ref, *refs):
    del after_ref
    blocks, (f_ref, g_ref, s1_ref, s2_ref) = refs[:7], refs[7:]
    spread(blocks[4:], s2_ref, 1)
    spread(blocks[:4], s1_ref, 0)
    f_ref[...] = lax.dot_general(s2_ref[...], s1_ref[...], NT, preferred_element_type=F32)
    for j in range(2):
        g_ref[256 * j :, 256 * j : 256 * (j + 1)] = gram(s2_ref, j)


def early(first, second, after):
    blocks = [*first, *second]
    return pl.pallas_call(
        early_kernel,
        in_specs=[ANY] + [VMEM] * 7,
        out_specs=[VMEM] * 2,
        out_shape=[shape_of(SUPER, F32, SUPER)] * 2,
        scratch_shapes=[pltpu.VMEM((SUPER, WIDTH // 2), BF16)] * 2,
        compiler_params=PARAMS,
        cost_estimate=pl.CostEstimate(flops=4 * 10**9, bytes_accessed=5 << 20, transcendentals=0),
        name="early",
    )(after, *blocks)


def panel_kernel(parent_ref, *refs):
    blocks, (f_ref, g_ref, x_ref, p_out, a_ref, b_ref) = refs[:6], refs[6:12]
    p_ref, s1_ref, s2_ref, out_sems = refs[12:]
    spread(blocks[4:], s2_ref, 1)
    spread(blocks[:4], s1_ref, 0)
    late = lax.dot_general(s2_ref[...], s1_ref[...], NT, preferred_element_type=F32)
    front = split(f_ref[...] + late)
    left = tuple(part[:, :256] for part in front)
    panels = [dot3(left, split(x_ref[:256, :256])), dot3(front, split(x_ref[256:, :]))]
    panel = jnp.concatenate(panels, axis=1)
    p_ref[...] = panel
    stores = start_copies([p_ref], [p_out], out_sems)
    whole = split(panel)
    tiles = {}
    for j in range(2):
        o = 256 * j
        update = g_ref[o:, o : o + 256] + gram(s2_ref, j)
        update = update - dot3(rows_of(whole, o), rows_of(whole, o, o + 256))
        for row in range(2 * j, 4):
            for col in range(2 * j, min(row, 2 * j + 1) + 1):
                r, c = TILE * row - o, TILE * col - o
                tiles[row, col] = update[r : r + TILE, c : c + TILE]
    row, col = tile_ids()
    parent = jnp.full((8, TILE), parent_ref[0, 0].astype(F32))
    for out, ((one, other), below_diagonal) in zip((a_ref, b_ref), ROUTES):
        one, other = tiles[one, one], tiles[other, other]
        out[:TILE, :] = jnp.where(row >= col, one, other).astype(BF16)
        for n, key in enumerate(below_diagonal):
            out[TILE * (n + 1) : TILE * (n + 2), :] = tiles[key].astype(BF16)
        diagonal = jnp.sum(jnp.where(row == col, other, 0.0), axis=0, keepdims=True)
        diagonal = jnp.broadcast_to(diagonal, (8, TILE))
        out[ROWS:, :] = jnp.concatenate([parent, diagonal], axis=0).astype(BF16)
    wait_all(stores)


def panel(parents, first, second, fronts, inverse):
    operands = [*first, *second, *fronts, inverse]
    outs = [shape_of(SUPER, F32, SUPER), shape_of(MESSAGE, BF16), shape_of(MESSAGE, BF16)]
    return pl.pallas_call(
        panel_kernel,
        in_specs=[SMEM] + [VMEM] * len(operands),
        out_specs=[ANY, VMEM, VMEM],
        out_shape=outs,
        scratch_shapes=[pltpu.VMEM((SUPER, SUPER), F32)]
        + [pltpu.VMEM((SUPER, WIDTH // 2), BF16)] * 2
        + [dma(1)],
        compiler_params=PARAMS,
        name="panel",
    )(parents, *operands)


def sort_kernel(route, *refs):
    came, sums = refs[:4], refs[4:]
    c = lax.axis_index("col")
    x, z = c // RING, lax.rem(c, RING)
    tails = [ref[ROWS:, :].astype(F32) for ref in came]
    parents = [tail[:8] for tail in tails]
    flags = []
    for step in range(RING):
        if route == 0:
            wanted = x * RING + lax.rem(z + step, RING)
        else:
            wanted = lax.rem(x + step, RING) * RING + z
        wanted = wanted.astype(F32)
        flags.append([jnp.where(parent == wanted, 1.0, 0.0)[None] for parent in parents])
    for flag, out in zip(flags, sums):
        total = tails[0][8:] * flag[0][0]
        for s in range(1, RING):
            total = total + tails[s][8:] * flag[s][0]
        out[ROWS:, :] = jnp.concatenate([total, total], axis=0).astype(out.dtype)
    for r in range(0, ROWS, TILE):
        parts = [ref[r : r + TILE, :].astype(F32).reshape(16, 8, TILE) for ref in came]
        for flag, out in zip(flags, sums):
            total = parts[0] * flag[0]
            for s in range(1, RING):
                total = total + parts[s] * flag[s]
            out[r : r + TILE, :] = total.reshape(TILE, TILE).astype(out.dtype)


def sort(route, came):
    def kernel(*refs):
        sort_kernel(route, *refs)

    return pl.pallas_call(
        kernel,
        in_specs=[VMEM] * 4,
        out_specs=[VMEM] * 4,
        out_shape=[shape_of(MESSAGE, t) for t in (F32, BF16, BF16, BF16)],
        compiler_params=PARAMS,
        name=f"sort{route}",
    )(*came)


def total_of(parts, start, stop):
    total = None
    for ref in parts:
        part = ref[start:stop, :].astype(F32)
        total = part if total is None else total + part
    return total


def lower_tile(packed):
    row, col = tile_ids()
    return jnp.where(row >= col, packed, 0.0) + jnp.where(row > col, packed, 0.0).T


def upper_tile(packed, tail):
    row, col = tile_ids()
    upper = jnp.where(row < col, packed, 0.0)
    return upper + upper.T + jnp.where(row == col, jnp.broadcast_to(tail[:1], (TILE, TILE)), 0.0)


def start_kernel(*refs):
    held, (l_ref, m_ref) = refs[:4], refs[4:]
    m_ref[0, :TILE, :] = lower_tile(total_of(held, 0, TILE))
    m_ref[0, TILE:, :] = total_of(held, TILE, ROWS)
    add_ridge(m_ref, (0,))
    factor(m_ref, l_ref, steps=(0,))


def start(parts):
    return pl.pallas_call(
        start_kernel,
        in_specs=[VMEM] * 4,
        out_specs=VMEM,
        out_shape=shape_of(SUPER, F32),
        scratch_shapes=[pltpu.VMEM((1, SUPER, TILE), F32)],
        compiler_params=PARAMS,
        cost_estimate=pl.CostEstimate(flops=4 * 10**9, bytes_accessed=1 << 20, transcendentals=0),
        name="start",
    )(*parts)


def rest_kernel(*refs):
    column, first, second, (l_out, l_ref, m_ref, out_sems) = refs[0], refs[1:5], refs[5:9], refs[9:]
    l_ref[:, :TILE] = column[...]
    stores = start_copies([l_ref.at[:, pl.ds(0, TILE)]], [l_out.at[:, pl.ds(0, TILE)]], out_sems)
    for parts, ((_, other), below_diagonal) in zip((first, second), ROUTES):
        packed, tail = total_of(parts, 0, TILE), total_of(parts, ROWS, MESSAGE)
        m_ref[other, TILE * other : TILE * (other + 1), :] = upper_tile(packed, tail)
        if other == 3:
            m_ref[2, 2 * TILE : 3 * TILE, :] = lower_tile(packed)
            for n, (i, j) in enumerate(below_diagonal):
                got = total_of(parts, TILE * (n + 1), TILE * (n + 2))
                m_ref[j, TILE * i : TILE * (i + 1), :] = got
    add_ridge(m_ref, (1, 2, 3))
    trail(m_ref, 0, split(column[TILE:, :]))

    def finished(kb):
        strip = pl.ds(TILE * kb, TILE)
        stores.extend(start_copies([l_ref.at[:, strip]], [l_out.at[:, strip]], out_sems, kb))

    factor(m_ref, l_ref, finished=finished, steps=(1, 2, 3))
    wait_all(stores)


def rest(column, parts):
    operands = [column, *parts]
    return pl.pallas_call(
        rest_kernel,
        in_specs=[VMEM] * 9,
        out_specs=ANY,
        out_shape=shape_of(SUPER, F32, SUPER),
        scratch_shapes=[pltpu.VMEM((SUPER, SUPER), F32), pltpu.VMEM((4, SUPER, TILE), F32), dma(4)],
        compiler_params=PARAMS,
        name="rest",
    )(*operands)


def shift(value, along_x, step):
    pairs = []
    for x in range(RING):
        for z in range(RING):
            to = ((x + step) % RING, z) if along_x else (x, (z + step) % RING)
            pairs.append((x * RING + z, to[0] * RING + to[1]))
    return lax.ppermute(value, "col", pairs)


def hand(value, dy, dc):
    pairs = [(y * 2 + c, (y + dy) % RING * 2 + (c ^ dc)) for y in range(RING) for c in range(2)]
    return lax.ppermute(value, "blk", pairs)


def gather(value, x_first):
    return [value] + [shift(value, x_first, s) for s in (1, 2, 3)]


def on_device(col_tiles, scales, positions, targets, parents):
    *blocks, give = place(col_tiles, scales, positions, targets)
    in1, keep = blocks[:8], blocks[8:]
    order = ((2, 0), (2, 1), (1, 0), (3, 0), (1, 1), (3, 1), (0, 1))
    for dy, dc in order:
        in1[2 * dy + dc] = hand(in1[2 * dy + dc], dy, dc)
    got = hand(give, 0, 1)
    pairs = [
        jnp.concatenate([keep[dy], got[BLOCK * dy : BLOCK * (dy + 1)]]) for dy in range(1, RING)
    ]
    landed = [in1[2 * dy + dc] for dy, dc in order[:5]]
    landed, pairs = lax.optimization_barrier((landed, pairs))
    for (dy, dc), value in zip(order[:5], landed):
        in1[2 * dy + dc] = value
    in2 = [hand(pairs[dy - 1], dy, 0) for dy in (1, 2, 3)]
    leaf_factor, inverse = leaf(in1)
    fronts = early(in1[:4], [keep[0], got[:BLOCK], in2[0]], inverse)
    leaf_panel, first, second = panel(parents, in1[4:], in2[1:], fronts, inverse)
    sums = []
    for route, value in enumerate((first, second)):
        own, *sends = sort(route, gather(value, route == 0))
        sums += [own] + [shift(send, route == 1, n + 1) for n, send in enumerate(sends)]
    parent_factor = rest(start(sums[:4]), sums)
    return (leaf_factor[None], leaf_panel[None], parent_factor[None])


def solution(mesh):
    in_specs = (
        P(("col", "blk"), None, None, None),
        P(("col", "blk"), None),
        P(("col", "blk"), None),
        P(("col", "blk"), None),
        P("col", "blk"),
    )
    out_specs = (
        P(("col", "blk"), None, None),
        P(("col", "blk"), None, None),
        P(("col", "blk"), None, None),
    )
    return jax.shard_map(
        on_device, mesh=mesh, in_specs=in_specs, out_specs=out_specs, check_vma=False
    )
```

```python
import jax
import jax.numpy as jnp
from jax import lax
from jax.experimental import pallas as pl
from jax.experimental.pallas import tpu as pltpu
from jax.sharding import PartitionSpec as P

TILE = 128
SUPER = 512
RIDGE = 1.0
CAP = 4
CT_DEV = 16
RING = 4
PEERS = [(dy, dc) for dy in range(RING) for dc in range(2)]
TILES = CAP * 2 * TILE
BLOCK = TILES + 16
WIDTH = len(PEERS) * CAP * TILE
ROUTES = (((0, 1), ((1, 0), (2, 0), (3, 0))), ((2, 3), ((2, 1), (3, 1), (3, 2))))
ROWS = 4 * TILE
MESSAGE = ROWS + 16

F32 = jnp.float32
BF16 = jnp.bfloat16
NT = (((1,), (1,)), ((), ()))
NN = (((1,), (0,)), ((), ()))

VMEM = pl.BlockSpec(memory_space=pltpu.VMEM)
ANY = pl.BlockSpec(memory_space=pl.ANY)
SMEM = pl.BlockSpec(memory_space=pltpu.SMEM)
HBM = pl.BlockSpec(memory_space=pltpu.HBM)
PARAMS = pltpu.CompilerParams(vmem_limit_bytes=32 << 20)


def start_copies(sources, targets, sems, first=0):
    copies = []
    for n, (source, target) in enumerate(zip(sources, targets)):
        copies.append(pltpu.make_async_copy(source, target, sems.at[first + n]))
        copies[-1].start()
    return copies


def wait_all(copies):
    for copy in copies:
        copy.wait()


def dma(number):
    return pltpu.SemaphoreType.DMA((number,))


def shape_of(rows, dtype, columns=TILE):
    return jax.ShapeDtypeStruct((rows, columns), dtype)


def split(a):
    high = a.astype(BF16)
    return high, (a - high.astype(F32)).astype(BF16)


def dot3(a, b, dims=NT):
    x = jnp.concatenate([a[0], a[1], a[0]], axis=1)
    y = jnp.concatenate([b[0], b[0], b[1]], axis=1 if dims is NT else 0)
    return lax.dot_general(x, y, dims, preferred_element_type=F32)


def rows_of(pair, start, stop=None):
    return tuple(part[start:stop] for part in pair)


def on_top(pair):
    return tuple(jnp.concatenate([part, jnp.zeros_like(part)], axis=0) for part in pair)


def below(pair):
    return tuple(jnp.concatenate([jnp.zeros_like(part), part], axis=0) for part in pair)


def lane(v, j):
    return jnp.broadcast_to(v[:, j : j + 1], (8, TILE))


def sub(v, i):
    return jnp.broadcast_to(v[i : i + 1, :], (8, TILE))


def eliminate64(aug, base):
    w = [aug[8 * q : 8 * q + 8] for q in range(8)]
    out = []
    sid = lax.broadcasted_iota(jnp.int32, (8, TILE), 0)
    own = [lane(w[0], base + k) for k in range(8)]
    for p in range(8):
        at = base + 8 * p
        cols = [[lane(w[q], at + k) for k in range(8)] for q in range(p + 1, 8)]
        last = p == 7
        if not last:
            ahead = [lane(w[p + 1], at + 8 + k) for k in range(8)]
        rows = [sub(w[p], k) for k in range(8)]
        scale = None
        for k in range(8):
            if k % 2 == 0:
                a, b, c = sub(own[k], k), sub(own[k], k + 1), sub(own[k + 1], k + 1)
                r = lax.rsqrt(a)
                scale = lax.rsqrt(a * c - b * b) * (a * r)
            else:
                r = scale
            low = own[k] * r
            mult = [sub(low, i) if i > k else None for i in range(8)]
            for j in range(k + 1, 8):
                own[j] = own[j] - low * mult[j]
            rows[k] = rows[k] * r
            for i in range(k + 1, 8):
                rows[i] = rows[i] - mult[i] * rows[k]
            for q in range(p + 1, 8):
                col = cols[q - p - 1]
                lq = col[k] * r
                for j in range(k + 1, 8):
                    col[j] = col[j] - lq * mult[j]
                w[q] = w[q] - lq * rows[k]
                if q == p + 1:
                    for j in range(8):
                        ahead[j] = ahead[j] - lq * sub(lq, j)
        block = rows[0]
        for k in range(1, 8):
            block = jnp.where(sid == k, rows[k], block)
        out.append(block)
        if not last:
            own = ahead
    return jnp.concatenate(out, axis=0)


def trail(m_ref, kb, panels):
    for j in range(kb + 1, 4):
        s = TILE * (j - kb - 1)
        m_ref[j, TILE * j :, :] -= dot3(rows_of(panels, s), rows_of(panels, s, s + TILE))


def factor(m_ref, l_ref, x_ref=None, finished=lambda kb: None, steps=range(4)):
    col_id = lax.broadcasted_iota(jnp.int32, (64, TILE), 1)
    row_id = lax.broadcasted_iota(jnp.int32, (64, TILE), 0)
    eye = (col_id % 64 == row_id).astype(F32)
    left = col_id < 64
    lower = row_id >= col_id % 64
    zero = jnp.zeros((), F32)

    def keep_left(v):
        return jnp.where(lax.broadcasted_iota(jnp.int32, v.shape, 1) < 64, v, zero)

    def keep_right(v):
        return jnp.where(lax.broadcasted_iota(jnp.int32, v.shape, 1) < 64, zero, v)

    o = TILE * steps[0]
    corner = pltpu.roll(m_ref[steps[0], o : o + 64, :], 64, 1)
    for kb in steps:
        o = TILE * kb
        if kb:
            l_ref[:o, o : o + TILE] = jnp.zeros((o, TILE), F32)
        corner_b = pltpu.roll(m_ref[kb, o + 64 : o + TILE, :], 64, 1)
        lhs = split(keep_left(m_ref[kb, o + 64 :, :]))
        w1 = eliminate64(jnp.where(left, eye, corner), 64)
        x1 = on_top(split(w1))
        l21 = dot3(rows_of(lhs, 0, 64), x1)
        l21s = split(l21)
        w2 = eliminate64(jnp.where(left, corner_b - dot3(l21s, on_top(l21s)), eye), 0)
        if kb < 3:
            pa = dot3(rows_of(lhs, 64), x1)
            pas = split(pa)
            rest = split(keep_right(m_ref[kb, o + TILE :, :] - dot3(pas, below(l21s))))
            x2 = below(split(w2))
            n = o + TILE
            last = kb == steps[-1]
            pb_d = dot3(rows_of(rest, 0, 64), x2)
            if not last:
                pa_d, pb_ds = rows_of(pas, 0, 64), split(pb_d)
                corner = pltpu.roll(m_ref[kb + 1, n : n + 64, :], 64, 1) - dot3(pa_d, below(pa_d))
                corner = corner - dot3(pb_ds, below(pb_ds))
            pb = jnp.concatenate([pb_d, dot3(rows_of(rest, 64), x2)], axis=0)
            panel = pa + pb
            l_ref[n:, o:n] = panel
            if not last:
                trail(m_ref, kb, split(panel))
        flip = jnp.concatenate([w1, w2], axis=0).T
        l_ref[o : o + 64, o : o + TILE] = jnp.where(left & lower, flip[64:], zero)
        l_ref[o + 64 : o + TILE, o : o + TILE] = jnp.where(left, l21, jnp.where(lower, flip[:64], zero))
        if x_ref is not None:
            x1f = jnp.where(left, w1, zero)
            x2f = jnp.where(left, zero, w2)
            t = dot3(l21s, on_top(split(x1f)), NN)
            x21 = -dot3(split(x2f), below(split(t)), NN)
            x = jnp.concatenate([x1f, jnp.where(left, x21, x2f)], axis=0)
            x_ref[o : o + TILE, o : o + TILE] = x
            if kb < 3:
                x_ref[o : o + TILE, o + TILE :] = jnp.zeros((TILE, SUPER - TILE - o), F32)
            if kb:
                before = dot3(split(l_ref[o : o + TILE, :o]), split(x_ref[:o, :o]), NN)
                x_ref[o : o + TILE, :o] = -dot3(split(x), split(before), NN)
        finished(kb)


def place_kernel(target_ref, spot_ref, scale_ref, tile_ref, *refs):
    outs, (in_ref, block_ref, spots_ref, count_ref, in_sems) = refs[:13], refs[13:]
    fetches = [tile_ref.at[:, 2 * half : 2 * half + 2] for half in range(2)]
    fetches = start_copies(fetches, [in_ref.at[half] for half in range(2)], in_sems)
    me = lax.axis_index("blk")
    for peer in range(len(PEERS)):
        count_ref[peer] = 0
    block_ref[...] = jnp.zeros(block_ref.shape, BF16)
    spots_ref[...] = jnp.zeros(spots_ref.shape, F32)
    places = []
    for t in range(CT_DEV):
        owner = target_ref[0, t]
        peer = lax.rem(owner // 2 - me // 2 + RING, RING) * 2 + lax.rem(owner + me, 2)
        rank = count_ref[peer]
        count_ref[peer] = rank + 1
        places.append((peer, rank))
        for k in range(4):
            spot = jnp.broadcast_to(spot_ref[k : k + 1, t : t + 1].astype(F32), (1, TILE))
            spots_ref[peer, pl.ds(4 * rank + k, 1), :] = spot
    pieces = [(out, 0, 0, peer) for peer, out in enumerate(outs[:8])]
    pieces += [(out, 0, 1, 2 * dy) for dy, out in enumerate(outs[8:12])]
    pieces += [(outs[12], BLOCK * dy, 1, 2 * dy + 1) for dy in range(RING)]
    for half in range(2):
        fetches[half].wait()
        for t, (peer, rank) in enumerate(places):
            root = jnp.sqrt(scale_ref[t : t + 1, :])
            for k in range(2):
                scaled = in_ref[half, t, k].astype(F32) * root
                at = pl.multiple_of((2 * rank + k) * TILE, TILE)
                block_ref[half, peer, pl.ds(at, TILE), :] = scaled.astype(BF16)
        for out, o, of, peer in pieces:
            if of == half:
                out[o : o + TILES, :] = block_ref[half, peer]
                out[o + TILES : o + BLOCK, :] = spots_ref[peer].astype(BF16)


def place(col_tiles, scales, positions, targets):
    blocks = [1] * 12 + [4]
    return pl.pallas_call(
        place_kernel,
        in_specs=[SMEM, VMEM, VMEM, HBM],
        out_specs=[VMEM] * len(blocks),
        out_shape=[shape_of(n * BLOCK, BF16) for n in blocks],
        scratch_shapes=[
            pltpu.VMEM((2, CT_DEV, 2, TILE, TILE), BF16),
            pltpu.VMEM((2, len(PEERS), TILES, TILE), BF16),
            pltpu.VMEM((len(PEERS), 16, TILE), F32),
            pltpu.SMEM((len(PEERS),), jnp.int32),
            dma(2),
        ],
        compiler_params=pltpu.CompilerParams(vmem_limit_bytes=49 << 20),
        name="place",
    )(targets.T, positions.T, scales, col_tiles)


def spread(refs, s_ref, half):
    blocks = [(ref, o) for ref in refs for o in range(0, ref.shape[0], BLOCK)]
    for n, (ref, o) in enumerate(blocks):
        spots = ref[o + TILES : o + BLOCK, :].astype(F32)
        for slot in range(CAP):
            at = TILE * (n * CAP + slot)
            tiles = []
            for k in range(2):
                s = o + TILE * (2 * slot + k)
                tiles.append(ref[s : s + TILE, :].reshape(8, 16, TILE))
            row = 4 * slot + 2 * half
            picks = [jnp.broadcast_to(spots[row + k : row + k + 1, :], (16, TILE)) for k in range(2)]
            for i in range(4):
                total = None
                for tile, pick in zip(tiles, picks):
                    flag = jnp.where(pick == 4.0 * half + i, 1.0, 0.0).astype(BF16)
                    part = tile * flag[None]
                    total = part if total is None else total + part
                s_ref[TILE * i : TILE * (i + 1), at : at + TILE] = total.reshape(TILE, TILE)


def gram(s_ref, j):
    o = 256 * j
    return lax.dot_general(s_ref[o:, :], s_ref[o : o + 256, :], NT, preferred_element_type=F32)


def tile_ids():
    row = lax.broadcasted_iota(jnp.int32, (TILE, TILE), 0)
    return row, lax.broadcasted_iota(jnp.int32, (TILE, TILE), 1)


def add_ridge(m_ref, columns=range(4)):
    row, col = tile_ids()
    ridge = jnp.where(row == col, jnp.float32(RIDGE), 0.0)
    for j in columns:
        m_ref[j, TILE * j : TILE * (j + 1), :] += ridge


def leaf_kernel(*refs):
    blocks, (l_out, x_ref, l_ref, m_ref, s_ref, out_sems) = refs[:8], refs[8:]
    spread(blocks, s_ref, 0)
    for j in range(2):
        got = gram(s_ref, j)
        m_ref[2 * j, 256 * j :, :] = got[:, :TILE]
        m_ref[2 * j + 1, 256 * j :, :] = got[:, TILE:]
    add_ridge(m_ref)
    stores = []

    def finished(kb):
        strip = pl.ds(TILE * kb, TILE)
        stores.extend(start_copies([l_ref.at[:, strip]], [l_out.at[:, strip]], out_sems, kb))

    factor(m_ref, l_ref, x_ref, finished)
    wait_all(stores)


def leaf(blocks):
    return pl.pallas_call(
        leaf_kernel,
        in_specs=[VMEM] * len(blocks),
        out_specs=[ANY, VMEM],
        out_shape=[shape_of(SUPER, F32, SUPER)] * 2,
        scratch_shapes=[
            pltpu.VMEM((SUPER, SUPER), F32),
            pltpu.VMEM((4, SUPER, TILE), F32),
            pltpu.VMEM((SUPER, WIDTH), BF16),
            dma(4),
        ],
        compiler_params=PARAMS,
        cost_estimate=pl.CostEstimate(flops=20 * 10**9, bytes_accessed=5 << 20, transcendentals=0),
        name="leaf",
    )(*blocks)


def early_kernel(after_ref, *refs):
    del after_ref
    blocks, (f_ref, g_ref, s1_ref, s2_ref) = refs[:7], refs[7:]
    spread(blocks[4:], s2_ref, 1)
    spread(blocks[:4], s1_ref, 0)
    f_ref[...] = lax.dot_general(s2_ref[...], s1_ref[...], NT, preferred_element_type=F32)
    for j in range(2):
        g_ref[256 * j :, 256 * j : 256 * (j + 1)] = gram(s2_ref, j)


def early(first, second, after):
    blocks = [*first, *second]
    return pl.pallas_call(
        early_kernel,
        in_specs=[ANY] + [VMEM] * 7,
        out_specs=[VMEM] * 2,
        out_shape=[shape_of(SUPER, F32, SUPER)] * 2,
        scratch_shapes=[pltpu.VMEM((SUPER, WIDTH // 2), BF16)] * 2,
        compiler_params=PARAMS,
        cost_estimate=pl.CostEstimate(flops=4 * 10**9, bytes_accessed=5 << 20, transcendentals=0),
        name="early",
    )(after, *blocks)


def panel_kernel(parent_ref, *refs):
    blocks, (f_ref, g_ref, x_ref, p_out, a_ref, b_ref) = refs[:6], refs[6:12]
    p_ref, s1_ref, s2_ref, out_sems = refs[12:]
    spread(blocks[4:], s2_ref, 1)
    spread(blocks[:4], s1_ref, 0)
    late = lax.dot_general(s2_ref[...], s1_ref[...], NT, preferred_element_type=F32)
    front = split(f_ref[...] + late)
    left = tuple(part[:, :256] for part in front)
    panels = [dot3(left, split(x_ref[:256, :256])), dot3(front, split(x_ref[256:, :]))]
    panel = jnp.concatenate(panels, axis=1)
    p_ref[...] = panel
    stores = start_copies([p_ref], [p_out], out_sems)
    whole = split(panel)
    tiles = {}
    for j in range(2):
        o = 256 * j
        update = g_ref[o:, o : o + 256] + gram(s2_ref, j)
        update = update - dot3(rows_of(whole, o), rows_of(whole, o, o + 256))
        for row in range(2 * j, 4):
            for col in range(2 * j, min(row, 2 * j + 1) + 1):
                r, c = TILE * row - o, TILE * col - o
                tiles[row, col] = update[r : r + TILE, c : c + TILE]
    row, col = tile_ids()
    parent = jnp.full((8, TILE), parent_ref[0, 0].astype(F32))
    for out, ((one, other), below_diagonal) in zip((a_ref, b_ref), ROUTES):
        one, other = tiles[one, one], tiles[other, other]
        out[:TILE, :] = jnp.where(row >= col, one, other).astype(BF16)
        for n, key in enumerate(below_diagonal):
            out[TILE * (n + 1) : TILE * (n + 2), :] = tiles[key].astype(BF16)
        diagonal = jnp.sum(jnp.where(row == col, other, 0.0), axis=0, keepdims=True)
        diagonal = jnp.broadcast_to(diagonal, (8, TILE))
        out[ROWS:, :] = jnp.concatenate([parent, diagonal], axis=0).astype(BF16)
    wait_all(stores)


def panel(parents, first, second, fronts, inverse):
    operands = [*first, *second, *fronts, inverse]
    outs = [shape_of(SUPER, F32, SUPER), shape_of(MESSAGE, BF16), shape_of(MESSAGE, BF16)]
    return pl.pallas_call(
        panel_kernel,
        in_specs=[SMEM] + [VMEM] * len(operands),
        out_specs=[ANY, VMEM, VMEM],
        out_shape=outs,
        scratch_shapes=[pltpu.VMEM((SUPER, SUPER), F32)]
        + [pltpu.VMEM((SUPER, WIDTH // 2), BF16)] * 2
        + [dma(1)],
        compiler_params=PARAMS,
        name="panel",
    )(parents, *operands)


def sort_kernel(route, *refs):
    came, sums = refs[:4], refs[4:]
    c = lax.axis_index("col")
    x, z = c // RING, lax.rem(c, RING)
    tails = [ref[ROWS:, :].astype(F32) for ref in came]
    parents = [tail[:8] for tail in tails]
    flags = []
    for step in range(RING):
        if route == 0:
            wanted = x * RING + lax.rem(z + step, RING)
        else:
            wanted = lax.rem(x + step, RING) * RING + z
        wanted = wanted.astype(F32)
        flags.append([jnp.where(parent == wanted, 1.0, 0.0)[None] for parent in parents])
    for flag, out in zip(flags, sums):
        total = tails[0][8:] * flag[0][0]
        for s in range(1, RING):
            total = total + tails[s][8:] * flag[s][0]
        out[ROWS:, :] = jnp.concatenate([total, total], axis=0).astype(out.dtype)
    for r in range(0, ROWS, TILE):
        parts = [ref[r : r + TILE, :].astype(F32).reshape(16, 8, TILE) for ref in came]
        for flag, out in zip(flags, sums):
            total = parts[0] * flag[0]
            for s in range(1, RING):
                total = total + parts[s] * flag[s]
            out[r : r + TILE, :] = total.reshape(TILE, TILE).astype(out.dtype)


def sort(route, came):
    def kernel(*refs):
        sort_kernel(route, *refs)

    return pl.pallas_call(
        kernel,
        in_specs=[VMEM] * 4,
        out_specs=[VMEM] * 4,
        out_shape=[shape_of(MESSAGE, t) for t in (F32, BF16, BF16, BF16)],
        compiler_params=PARAMS,
        name=f"sort{route}",
    )(*came)


def total_of(parts, start, stop):
    total = None
    for ref in parts:
        part = ref[start:stop, :].astype(F32)
        total = part if total is None else total + part
    return total


def lower_tile(packed):
    row, col = tile_ids()
    return jnp.where(row >= col, packed, 0.0) + jnp.where(row > col, packed, 0.0).T


def upper_tile(packed, tail):
    row, col = tile_ids()
    upper = jnp.where(row < col, packed, 0.0)
    return upper + upper.T + jnp.where(row == col, jnp.broadcast_to(tail[:1], (TILE, TILE)), 0.0)


def start_kernel(*refs):
    held, (l_ref, m_ref) = refs[:4], refs[4:]
    m_ref[0, :TILE, :] = lower_tile(total_of(held, 0, TILE))
    m_ref[0, TILE:, :] = total_of(held, TILE, ROWS)
    add_ridge(m_ref, (0,))
    factor(m_ref, l_ref, steps=(0,))


def start(parts):
    return pl.pallas_call(
        start_kernel,
        in_specs=[VMEM] * 4,
        out_specs=VMEM,
        out_shape=shape_of(SUPER, F32),
        scratch_shapes=[pltpu.VMEM((1, SUPER, TILE), F32)],
        compiler_params=PARAMS,
        cost_estimate=pl.CostEstimate(flops=4 * 10**9, bytes_accessed=1 << 20, transcendentals=0),
        name="start",
    )(*parts)


def rest_kernel(*refs):
    column, first, second, (l_out, l_ref, m_ref, out_sems) = refs[0], refs[1:5], refs[5:9], refs[9:]
    l_ref[:, :TILE] = column[...]
    stores = start_copies([l_ref.at[:, pl.ds(0, TILE)]], [l_out.at[:, pl.ds(0, TILE)]], out_sems)
    for parts, ((_, other), below_diagonal) in zip((first, second), ROUTES):
        packed, tail = total_of(parts, 0, TILE), total_of(parts, ROWS, MESSAGE)
        m_ref[other, TILE * other : TILE * (other + 1), :] = upper_tile(packed, tail)
        if other == 3:
            m_ref[2, 2 * TILE : 3 * TILE, :] = lower_tile(packed)
            for n, (i, j) in enumerate(below_diagonal):
                got = total_of(parts, TILE * (n + 1), TILE * (n + 2))
                m_ref[j, TILE * i : TILE * (i + 1), :] = got
    add_ridge(m_ref, (1, 2, 3))
    trail(m_ref, 0, split(column[TILE:, :]))

    def finished(kb):
        strip = pl.ds(TILE * kb, TILE)
        stores.extend(start_copies([l_ref.at[:, strip]], [l_out.at[:, strip]], out_sems, kb))

    factor(m_ref, l_ref, finished=finished, steps=(1, 2, 3))
    wait_all(stores)


def rest(column, parts):
    operands = [column, *parts]
    return pl.pallas_call(
        rest_kernel,
        in_specs=[VMEM] * 9,
        out_specs=ANY,
        out_shape=shape_of(SUPER, F32, SUPER),
        scratch_shapes=[pltpu.VMEM((SUPER, SUPER), F32), pltpu.VMEM((4, SUPER, TILE), F32), dma(4)],
        compiler_params=PARAMS,
        name="rest",
    )(*operands)


def shift(value, along_x, step):
    pairs = []
    for x in range(RING):
        for z in range(RING):
            to = ((x + step) % RING, z) if along_x else (x, (z + step) % RING)
            pairs.append((x * RING + z, to[0] * RING + to[1]))
    return lax.ppermute(value, "col", pairs)


def hand(value, dy, dc):
    pairs = [(y * 2 + c, (y + dy) % RING * 2 + (c ^ dc)) for y in range(RING) for c in range(2)]
    return lax.ppermute(value, "blk", pairs)


def gather(value, x_first):
    return [value] + [shift(value, x_first, s) for s in (1, 2, 3)]


def on_device(col_tiles, scales, positions, targets, parents):
    *blocks, give = place(col_tiles, scales, positions, targets)
    in1, keep = blocks[:8], blocks[8:]
    order = ((2, 0), (2, 1), (1, 0), (3, 0), (1, 1), (3, 1), (0, 1))
    for dy, dc in order:
        in1[2 * dy + dc] = hand(in1[2 * dy + dc], dy, dc)
    got = hand(give, 0, 1)
    pairs = [
        jnp.concatenate([keep[dy], got[BLOCK * dy : BLOCK * (dy + 1)]]) for dy in range(1, RING)
    ]
    landed = [in1[2 * dy + dc] for dy, dc in order[:4]]
    landed, pairs = lax.optimization_barrier((landed, pairs))
    for (dy, dc), value in zip(order[:4], landed):
        in1[2 * dy + dc] = value
    in2 = [hand(pairs[dy - 1], dy, 0) for dy in (1, 2, 3)]
    leaf_factor, inverse = leaf(in1)
    fronts = early(in1[:4], [keep[0], got[:BLOCK], in2[0]], inverse)
    leaf_panel, first, second = panel(parents, in1[4:], in2[1:], fronts, inverse)
    sums = []
    for route, value in enumerate((first, second)):
        own, *sends = sort(route, gather(value, route == 0))
        sums += [own] + [shift(send, route == 1, n + 1) for n, send in enumerate(sends)]
    parent_factor = rest(start(sums[:4]), sums)
    return (leaf_factor[None], leaf_panel[None], parent_factor[None])


def solution(mesh):
    in_specs = (
        P(("col", "blk"), None, None, None),
        P(("col", "blk"), None),
        P(("col", "blk"), None),
        P(("col", "blk"), None),
        P("col", "blk"),
    )
    out_specs = (
        P(("col", "blk"), None, None),
        P(("col", "blk"), None, None),
        P(("col", "blk"), None, None),
    )
    return jax.shard_map(
        on_device, mesh=mesh, in_specs=in_specs, out_specs=out_specs, check_vma=False
    )
```

```python
import jax
import jax.numpy as jnp
from jax import lax
from jax.experimental import pallas as pl
from jax.experimental.pallas import tpu as pltpu
from jax.sharding import PartitionSpec as P

TILE = 128
SUPER = 512
RIDGE = 1.0
CAP = 4
CT_DEV = 16
RING = 4
PEERS = [(dy, dc) for dy in range(RING) for dc in range(2)]
TILES = CAP * 2 * TILE
BLOCK = TILES + 16
WIDTH = len(PEERS) * CAP * TILE
ROUTES = (((0, 1), ((1, 0), (2, 0), (3, 0))), ((2, 3), ((2, 1), (3, 1), (3, 2))))
ROWS = 4 * TILE
MESSAGE = ROWS + 16

F32 = jnp.float32
BF16 = jnp.bfloat16
NT = (((1,), (1,)), ((), ()))
NN = (((1,), (0,)), ((), ()))

VMEM = pl.BlockSpec(memory_space=pltpu.VMEM)
ANY = pl.BlockSpec(memory_space=pl.ANY)
SMEM = pl.BlockSpec(memory_space=pltpu.SMEM)
HBM = pl.BlockSpec(memory_space=pltpu.HBM)
PARAMS = pltpu.CompilerParams(vmem_limit_bytes=32 << 20)


def start_copies(sources, targets, sems, first=0):
    copies = []
    for n, (source, target) in enumerate(zip(sources, targets)):
        copies.append(pltpu.make_async_copy(source, target, sems.at[first + n]))
        copies[-1].start()
    return copies


def wait_all(copies):
    for copy in copies:
        copy.wait()


def dma(number):
    return pltpu.SemaphoreType.DMA((number,))


def shape_of(rows, dtype, columns=TILE):
    return jax.ShapeDtypeStruct((rows, columns), dtype)


def split(a):
    high = a.astype(BF16)
    return high, (a - high.astype(F32)).astype(BF16)


def dot3(a, b, dims=NT):
    x = jnp.concatenate([a[0], a[1], a[0]], axis=1)
    y = jnp.concatenate([b[0], b[0], b[1]], axis=1 if dims is NT else 0)
    return lax.dot_general(x, y, dims, preferred_element_type=F32)


def rows_of(pair, start, stop=None):
    return tuple(part[start:stop] for part in pair)


def on_top(pair):
    return tuple(jnp.concatenate([part, jnp.zeros_like(part)], axis=0) for part in pair)


def below(pair):
    return tuple(jnp.concatenate([jnp.zeros_like(part), part], axis=0) for part in pair)


def lane(v, j):
    return jnp.broadcast_to(v[:, j : j + 1], (8, TILE))


def sub(v, i):
    return jnp.broadcast_to(v[i : i + 1, :], (8, TILE))


def eliminate64(aug, base):
    w = [aug[8 * q : 8 * q + 8] for q in range(8)]
    out = []
    sid = lax.broadcasted_iota(jnp.int32, (8, TILE), 0)
    own = [lane(w[0], base + k) for k in range(8)]
    for p in range(8):
        at = base + 8 * p
        cols = [[lane(w[q], at + k) for k in range(8)] for q in range(p + 1, 8)]
        last = p == 7
        if not last:
            ahead = [lane(w[p + 1], at + 8 + k) for k in range(8)]
        rows = [sub(w[p], k) for k in range(8)]
        scale = None
        for k in range(8):
            if k % 2 == 0:
                a, b, c = sub(own[k], k), sub(own[k], k + 1), sub(own[k + 1], k + 1)
                r = lax.rsqrt(a)
                scale = lax.rsqrt(a * c - b * b) * (a * r)
            else:
                r = scale
            low = own[k] * r
            mult = [sub(low, i) if i > k else None for i in range(8)]
            for j in range(k + 1, 8):
                own[j] = own[j] - low * mult[j]
            rows[k] = rows[k] * r
            for i in range(k + 1, 8):
                rows[i] = rows[i] - mult[i] * rows[k]
            for q in range(p + 1, 8):
                col = cols[q - p - 1]
                lq = col[k] * r
                for j in range(k + 1, 8):
                    col[j] = col[j] - lq * mult[j]
                w[q] = w[q] - lq * rows[k]
                if q == p + 1:
                    for j in range(8):
                        ahead[j] = ahead[j] - lq * sub(lq, j)
        block = rows[0]
        for k in range(1, 8):
            block = jnp.where(sid == k, rows[k], block)
        out.append(block)
        if not last:
            own = ahead
    return jnp.concatenate(out, axis=0)


def trail(m_ref, kb, panels):
    for j in range(kb + 1, 4):
        s = TILE * (j - kb - 1)
        m_ref[j, TILE * j :, :] -= dot3(rows_of(panels, s), rows_of(panels, s, s + TILE))


def factor(m_ref, l_ref, x_ref=None, finished=lambda kb: None, steps=range(4)):
    col_id = lax.broadcasted_iota(jnp.int32, (64, TILE), 1)
    row_id = lax.broadcasted_iota(jnp.int32, (64, TILE), 0)
    eye = (col_id % 64 == row_id).astype(F32)
    left = col_id < 64
    lower = row_id >= col_id % 64
    zero = jnp.zeros((), F32)

    def keep_left(v):
        return jnp.where(lax.broadcasted_iota(jnp.int32, v.shape, 1) < 64, v, zero)

    def keep_right(v):
        return jnp.where(lax.broadcasted_iota(jnp.int32, v.shape, 1) < 64, zero, v)

    o = TILE * steps[0]
    corner = pltpu.roll(m_ref[steps[0], o : o + 64, :], 64, 1)
    for kb in steps:
        o = TILE * kb
        if kb:
            l_ref[:o, o : o + TILE] = jnp.zeros((o, TILE), F32)
        corner_b = pltpu.roll(m_ref[kb, o + 64 : o + TILE, :], 64, 1)
        lhs = split(keep_left(m_ref[kb, o + 64 :, :]))
        w1 = eliminate64(jnp.where(left, eye, corner), 64)
        x1 = on_top(split(w1))
        l21 = dot3(rows_of(lhs, 0, 64), x1)
        l21s = split(l21)
        w2 = eliminate64(jnp.where(left, corner_b - dot3(l21s, on_top(l21s)), eye), 0)
        if kb < 3:
            pa = dot3(rows_of(lhs, 64), x1)
            pas = split(pa)
            rest = split(keep_right(m_ref[kb, o + TILE :, :] - dot3(pas, below(l21s))))
            x2 = below(split(w2))
            n = o + TILE
            last = kb == steps[-1]
            pb_d = dot3(rows_of(rest, 0, 64), x2)
            if not last:
                pa_d, pb_ds = rows_of(pas, 0, 64), split(pb_d)
                corner = pltpu.roll(m_ref[kb + 1, n : n + 64, :], 64, 1) - dot3(pa_d, below(pa_d))
                corner = corner - dot3(pb_ds, below(pb_ds))
            pb = jnp.concatenate([pb_d, dot3(rows_of(rest, 64), x2)], axis=0)
            panel = pa + pb
            l_ref[n:, o:n] = panel
            if not last:
                trail(m_ref, kb, split(panel))
        flip = jnp.concatenate([w1, w2], axis=0).T
        l_ref[o : o + 64, o : o + TILE] = jnp.where(left & lower, flip[64:], zero)
        l_ref[o + 64 : o + TILE, o : o + TILE] = jnp.where(left, l21, jnp.where(lower, flip[:64], zero))
        if x_ref is not None:
            x1f = jnp.where(left, w1, zero)
            x2f = jnp.where(left, zero, w2)
            t = dot3(l21s, on_top(split(x1f)), NN)
            x21 = -dot3(split(x2f), below(split(t)), NN)
            x = jnp.concatenate([x1f, jnp.where(left, x21, x2f)], axis=0)
            x_ref[o : o + TILE, o : o + TILE] = x
            if kb < 3:
                x_ref[o : o + TILE, o + TILE :] = jnp.zeros((TILE, SUPER - TILE - o), F32)
            if kb:
                before = dot3(split(l_ref[o : o + TILE, :o]), split(x_ref[:o, :o]), NN)
                x_ref[o : o + TILE, :o] = -dot3(split(x), split(before), NN)
        finished(kb)


def place_kernel(target_ref, spot_ref, scale_ref, tile_ref, *refs):
    outs, (in_ref, block_ref, spots_ref, count_ref, in_sems) = refs[:13], refs[13:]
    fetches = [tile_ref.at[:, 2 * half : 2 * half + 2] for half in range(2)]
    fetches = start_copies(fetches, [in_ref.at[half] for half in range(2)], in_sems)
    me = lax.axis_index("blk")
    for peer in range(len(PEERS)):
        count_ref[peer] = 0
    block_ref[...] = jnp.zeros(block_ref.shape, BF16)
    spots_ref[...] = jnp.zeros(spots_ref.shape, F32)
    places = []
    for t in range(CT_DEV):
        owner = target_ref[0, t]
        peer = lax.rem(owner // 2 - me // 2 + RING, RING) * 2 + lax.rem(owner + me, 2)
        rank = count_ref[peer]
        count_ref[peer] = rank + 1
        places.append((peer, rank))
        for k in range(4):
            spot = jnp.broadcast_to(spot_ref[k : k + 1, t : t + 1].astype(F32), (1, TILE))
            spots_ref[peer, pl.ds(4 * rank + k, 1), :] = spot
    pieces = [(out, 0, 0, peer) for peer, out in enumerate(outs[:8])]
    pieces += [(out, 0, 1, 2 * dy) for dy, out in enumerate(outs[8:12])]
    pieces += [(outs[12], BLOCK * dy, 1, 2 * dy + 1) for dy in range(RING)]
    for half in range(2):
        fetches[half].wait()
        for t, (peer, rank) in enumerate(places):
            root = jnp.sqrt(scale_ref[t : t + 1, :])
            for k in range(2):
                scaled = in_ref[half, t, k].astype(F32) * root
                at = pl.multiple_of((2 * rank + k) * TILE, TILE)
                block_ref[half, peer, pl.ds(at, TILE), :] = scaled.astype(BF16)
        for out, o, of, peer in pieces:
            if of == half:
                out[o : o + TILES, :] = block_ref[half, peer]
                out[o + TILES : o + BLOCK, :] = spots_ref[peer].astype(BF16)


def place(col_tiles, scales, positions, targets):
    blocks = [1] * 12 + [4]
    return pl.pallas_call(
        place_kernel,
        in_specs=[SMEM, VMEM, VMEM, HBM],
        out_specs=[VMEM] * len(blocks),
        out_shape=[shape_of(n * BLOCK, BF16) for n in blocks],
        scratch_shapes=[
            pltpu.VMEM((2, CT_DEV, 2, TILE, TILE), BF16),
            pltpu.VMEM((2, len(PEERS), TILES, TILE), BF16),
            pltpu.VMEM((len(PEERS), 16, TILE), F32),
            pltpu.SMEM((len(PEERS),), jnp.int32),
            dma(2),
        ],
        compiler_params=pltpu.CompilerParams(vmem_limit_bytes=49 << 20),
        name="place",
    )(targets.T, positions.T, scales, col_tiles)


def spread(refs, s_ref, half):
    blocks = [(ref, o) for ref in refs for o in range(0, ref.shape[0], BLOCK)]
    for n, (ref, o) in enumerate(blocks):
        spots = ref[o + TILES : o + BLOCK, :].astype(F32)
        for slot in range(CAP):
            at = TILE * (n * CAP + slot)
            tiles = []
            for k in range(2):
                s = o + TILE * (2 * slot + k)
                tiles.append(ref[s : s + TILE, :].reshape(8, 16, TILE))
            row = 4 * slot + 2 * half
            picks = [jnp.broadcast_to(spots[row + k : row + k + 1, :], (16, TILE)) for k in range(2)]
            for i in range(4):
                total = None
                for tile, pick in zip(tiles, picks):
                    flag = jnp.where(pick == 4.0 * half + i, 1.0, 0.0).astype(BF16)
                    part = tile * flag[None]
                    total = part if total is None else total + part
                s_ref[TILE * i : TILE * (i + 1), at : at + TILE] = total.reshape(TILE, TILE)


def gram(s_ref, j):
    o = 256 * j
    return lax.dot_general(s_ref[o:, :], s_ref[o : o + 256, :], NT, preferred_element_type=F32)


def tile_ids():
    row = lax.broadcasted_iota(jnp.int32, (TILE, TILE), 0)
    return row, lax.broadcasted_iota(jnp.int32, (TILE, TILE), 1)


def add_ridge(m_ref, columns=range(4)):
    row, col = tile_ids()
    ridge = jnp.where(row == col, jnp.float32(RIDGE), 0.0)
    for j in columns:
        m_ref[j, TILE * j : TILE * (j + 1), :] += ridge


def leaf_kernel(*refs):
    blocks, (l_out, x_ref, l_ref, m_ref, s_ref, out_sems) = refs[:8], refs[8:]
    spread(blocks, s_ref, 0)
    for j in range(2):
        got = gram(s_ref, j)
        m_ref[2 * j, 256 * j :, :] = got[:, :TILE]
        m_ref[2 * j + 1, 256 * j :, :] = got[:, TILE:]
    add_ridge(m_ref)
    stores = []

    def finished(kb):
        strip = pl.ds(TILE * kb, TILE)
        stores.extend(start_copies([l_ref.at[:, strip]], [l_out.at[:, strip]], out_sems, kb))

    factor(m_ref, l_ref, x_ref, finished)
    wait_all(stores)


def leaf(blocks):
    return pl.pallas_call(
        leaf_kernel,
        in_specs=[VMEM] * len(blocks),
        out_specs=[ANY, VMEM],
        out_shape=[shape_of(SUPER, F32, SUPER)] * 2,
        scratch_shapes=[
            pltpu.VMEM((SUPER, SUPER), F32),
            pltpu.VMEM((4, SUPER, TILE), F32),
            pltpu.VMEM((SUPER, WIDTH), BF16),
            dma(4),
        ],
        compiler_params=PARAMS,
        cost_estimate=pl.CostEstimate(flops=20 * 10**9, bytes_accessed=5 << 20, transcendentals=0),
        name="leaf",
    )(*blocks)


def early_kernel(after_ref, *refs):
    del after_ref
    blocks, (f_ref, g_ref, s1_ref, s2_ref) = refs[:7], refs[7:]
    spread(blocks[4:], s2_ref, 1)
    spread(blocks[:4], s1_ref, 0)
    f_ref[...] = lax.dot_general(s2_ref[...], s1_ref[...], NT, preferred_element_type=F32)
    for j in range(2):
        g_ref[256 * j :, 256 * j : 256 * (j + 1)] = gram(s2_ref, j)


def early(first, second, after):
    blocks = [*first, *second]
    return pl.pallas_call(
        early_kernel,
        in_specs=[ANY] + [VMEM] * 7,
        out_specs=[VMEM] * 2,
        out_shape=[shape_of(SUPER, F32, SUPER)] * 2,
        scratch_shapes=[pltpu.VMEM((SUPER, WIDTH // 2), BF16)] * 2,
        compiler_params=PARAMS,
        cost_estimate=pl.CostEstimate(flops=4 * 10**9, bytes_accessed=5 << 20, transcendentals=0),
        name="early",
    )(after, *blocks)


def panel_kernel(parent_ref, *refs):
    blocks, (f_ref, g_ref, x_ref, p_out, a_ref, b_ref) = refs[:6], refs[6:12]
    p_ref, s1_ref, s2_ref, out_sems = refs[12:]
    spread(blocks[4:], s2_ref, 1)
    spread(blocks[:4], s1_ref, 0)
    late = lax.dot_general(s2_ref[...], s1_ref[...], NT, preferred_element_type=F32)
    front = split(f_ref[...] + late)
    left = tuple(part[:, :256] for part in front)
    panels = [dot3(left, split(x_ref[:256, :256])), dot3(front, split(x_ref[256:, :]))]
    panel = jnp.concatenate(panels, axis=1)
    p_ref[...] = panel
    stores = start_copies([p_ref], [p_out], out_sems)
    whole = split(panel)
    tiles = {}
    for j in range(2):
        o = 256 * j
        update = g_ref[o:, o : o + 256] + gram(s2_ref, j)
        update = update - dot3(rows_of(whole, o), rows_of(whole, o, o + 256))
        for row in range(2 * j, 4):
            for col in range(2 * j, min(row, 2 * j + 1) + 1):
                r, c = TILE * row - o, TILE * col - o
                tiles[row, col] = update[r : r + TILE, c : c + TILE]
    row, col = tile_ids()
    parent = jnp.full((8, TILE), parent_ref[0, 0].astype(F32))
    for out, ((one, other), below_diagonal) in zip((a_ref, b_ref), ROUTES):
        one, other = tiles[one, one], tiles[other, other]
        out[:TILE, :] = jnp.where(row >= col, one, other).astype(BF16)
        for n, key in enumerate(below_diagonal):
            out[TILE * (n + 1) : TILE * (n + 2), :] = tiles[key].astype(BF16)
        diagonal = jnp.sum(jnp.where(row == col, other, 0.0), axis=0, keepdims=True)
        diagonal = jnp.broadcast_to(diagonal, (8, TILE))
        out[ROWS:, :] = jnp.concatenate([parent, diagonal], axis=0).astype(BF16)
    wait_all(stores)


def panel(parents, first, second, fronts, inverse):
    operands = [*first, *second, *fronts, inverse]
    outs = [shape_of(SUPER, F32, SUPER), shape_of(MESSAGE, BF16), shape_of(MESSAGE, BF16)]
    return pl.pallas_call(
        panel_kernel,
        in_specs=[SMEM] + [VMEM] * len(operands),
        out_specs=[ANY, VMEM, VMEM],
        out_shape=outs,
        scratch_shapes=[pltpu.VMEM((SUPER, SUPER), F32)]
        + [pltpu.VMEM((SUPER, WIDTH // 2), BF16)] * 2
        + [dma(1)],
        compiler_params=PARAMS,
        name="panel",
    )(parents, *operands)


def sort_kernel(route, *refs):
    came, sums = refs[:4], refs[4:]
    c = lax.axis_index("col")
    x, z = c // RING, lax.rem(c, RING)
    tails = [ref[ROWS:, :].astype(F32) for ref in came]
    parents = [tail[:8] for tail in tails]
    flags = []
    for step in range(RING):
        if route == 0:
            wanted = x * RING + lax.rem(z + step, RING)
        else:
            wanted = lax.rem(x + step, RING) * RING + z
        wanted = wanted.astype(F32)
        flags.append([jnp.where(parent == wanted, 1.0, 0.0)[None] for parent in parents])
    for flag, out in zip(flags, sums):
        total = tails[0][8:] * flag[0][0]
        for s in range(1, RING):
            total = total + tails[s][8:] * flag[s][0]
        out[ROWS:, :] = jnp.concatenate([total, total], axis=0).astype(out.dtype)
    for r in range(0, ROWS, TILE):
        parts = [ref[r : r + TILE, :].astype(F32).reshape(16, 8, TILE) for ref in came]
        for flag, out in zip(flags, sums):
            total = parts[0] * flag[0]
            for s in range(1, RING):
                total = total + parts[s] * flag[s]
            out[r : r + TILE, :] = total.reshape(TILE, TILE).astype(out.dtype)


def sort(route, came):
    def kernel(*refs):
        sort_kernel(route, *refs)

    return pl.pallas_call(
        kernel,
        in_specs=[VMEM] * 4,
        out_specs=[VMEM] * 4,
        out_shape=[shape_of(MESSAGE, t) for t in (F32, BF16, BF16, BF16)],
        compiler_params=PARAMS,
        name=f"sort{route}",
    )(*came)


def total_of(parts, start, stop):
    total = None
    for ref in parts:
        part = ref[start:stop, :].astype(F32)
        total = part if total is None else total + part
    return total


def lower_tile(packed):
    row, col = tile_ids()
    return jnp.where(row >= col, packed, 0.0) + jnp.where(row > col, packed, 0.0).T


def upper_tile(packed, tail):
    row, col = tile_ids()
    upper = jnp.where(row < col, packed, 0.0)
    return upper + upper.T + jnp.where(row == col, jnp.broadcast_to(tail[:1], (TILE, TILE)), 0.0)


def start_kernel(*refs):
    held, (l_ref, m_ref) = refs[:4], refs[4:]
    m_ref[0, :TILE, :] = lower_tile(total_of(held, 0, TILE))
    m_ref[0, TILE:, :] = total_of(held, TILE, ROWS)
    add_ridge(m_ref, (0,))
    factor(m_ref, l_ref, steps=(0,))


def start(parts):
    return pl.pallas_call(
        start_kernel,
        in_specs=[VMEM] * 4,
        out_specs=VMEM,
        out_shape=shape_of(SUPER, F32),
        scratch_shapes=[pltpu.VMEM((1, SUPER, TILE), F32)],
        compiler_params=PARAMS,
        cost_estimate=pl.CostEstimate(flops=4 * 10**9, bytes_accessed=1 << 20, transcendentals=0),
        name="start",
    )(*parts)


def rest_kernel(*refs):
    column, first, second, (l_out, l_ref, m_ref, out_sems) = refs[0], refs[1:5], refs[5:9], refs[9:]
    l_ref[:, :TILE] = column[...]
    stores = start_copies([l_ref.at[:, pl.ds(0, TILE)]], [l_out.at[:, pl.ds(0, TILE)]], out_sems)
    for parts, ((_, other), below_diagonal) in zip((first, second), ROUTES):
        packed, tail = total_of(parts, 0, TILE), total_of(parts, ROWS, MESSAGE)
        m_ref[other, TILE * other : TILE * (other + 1), :] = upper_tile(packed, tail)
        if other == 3:
            m_ref[2, 2 * TILE : 3 * TILE, :] = lower_tile(packed)
            for n, (i, j) in enumerate(below_diagonal):
                got = total_of(parts, TILE * (n + 1), TILE * (n + 2))
                m_ref[j, TILE * i : TILE * (i + 1), :] = got
    add_ridge(m_ref, (1, 2, 3))
    trail(m_ref, 0, split(column[TILE:, :]))

    def finished(kb):
        strip = pl.ds(TILE * kb, TILE)
        stores.extend(start_copies([l_ref.at[:, strip]], [l_out.at[:, strip]], out_sems, kb))

    factor(m_ref, l_ref, finished=finished, steps=(1, 2, 3))
    wait_all(stores)


def rest(column, parts):
    operands = [column, *parts]
    return pl.pallas_call(
        rest_kernel,
        in_specs=[VMEM] * 9,
        out_specs=ANY,
        out_shape=shape_of(SUPER, F32, SUPER),
        scratch_shapes=[pltpu.VMEM((SUPER, SUPER), F32), pltpu.VMEM((4, SUPER, TILE), F32), dma(4)],
        compiler_params=PARAMS,
        name="rest",
    )(*operands)


def shift(value, along_x, step):
    pairs = []
    for x in range(RING):
        for z in range(RING):
            to = ((x + step) % RING, z) if along_x else (x, (z + step) % RING)
            pairs.append((x * RING + z, to[0] * RING + to[1]))
    return lax.ppermute(value, "col", pairs)


def hand(value, dy, dc):
    pairs = [(y * 2 + c, (y + dy) % RING * 2 + (c ^ dc)) for y in range(RING) for c in range(2)]
    return lax.ppermute(value, "blk", pairs)


def gather(value, x_first):
    return [value] + [shift(value, x_first, s) for s in (1, 2, 3)]


def on_device(col_tiles, scales, positions, targets, parents):
    *blocks, give = place(col_tiles, scales, positions, targets)
    in1, keep = blocks[:8], blocks[8:]
    order = ((2, 0), (2, 1), (1, 0), (3, 0), (1, 1), (3, 1), (0, 1))
    for dy, dc in order:
        in1[2 * dy + dc] = hand(in1[2 * dy + dc], dy, dc)
    got = hand(give, 0, 1)
    pairs = [
        jnp.concatenate([keep[dy], got[BLOCK * dy : BLOCK * (dy + 1)]]) for dy in range(1, RING)
    ]
    landed = [in1[2 * dy + dc] for dy, dc in order[:3]]
    landed, pairs = lax.optimization_barrier((landed, pairs))
    for (dy, dc), value in zip(order[:3], landed):
        in1[2 * dy + dc] = value
    in2 = [hand(pairs[dy - 1], dy, 0) for dy in (1, 2, 3)]
    leaf_factor, inverse = leaf(in1)
    fronts = early(in1[:4], [keep[0], got[:BLOCK], in2[0]], inverse)
    leaf_panel, first, second = panel(parents, in1[4:], in2[1:], fronts, inverse)
    sums = []
    for route, value in enumerate((first, second)):
        own, *sends = sort(route, gather(value, route == 0))
        sums += [own] + [shift(send, route == 1, n + 1) for n, send in enumerate(sends)]
    parent_factor = rest(start(sums[:4]), sums)
    return (leaf_factor[None], leaf_panel[None], parent_factor[None])


def solution(mesh):
    in_specs = (
        P(("col", "blk"), None, None, None),
        P(("col", "blk"), None),
        P(("col", "blk"), None),
        P(("col", "blk"), None),
        P("col", "blk"),
    )
    out_specs = (
        P(("col", "blk"), None, None),
        P(("col", "blk"), None, None),
        P(("col", "blk"), None, None),
    )
    return jax.shard_map(
        on_device, mesh=mesh, in_specs=in_specs, out_specs=out_specs, check_vma=False
    )
```
